32 devices in a mesh: gx: 4 (over z), gy: 8 (over y, x, core).
Axes of the slice: x: 2, y: 2, z: 4, core: 2. Of those that a mesh axis runs over, the one named last changes fastest.
Arguments:
- features: bfloat16 [32, 128, 16, 128], P('gx', 'gy'), may hold values from -6 to 6
- w_first: bfloat16 [27, 128, 128], replicated, may hold values from -0.109375 to 0.109375
- w_second: bfloat16 [27, 128, 128], replicated, may hold values from -0.109375 to 0.109375
- occupancy: int32 [4, 16, 2], P('gx', 'gy'), may hold values from 0 to 1, as said below
- cotangent: bfloat16 [32, 128, 16, 128], P('gx', 'gy'), may hold values from -6 to 6
Outputs:
- output: bfloat16 [32, 128, 16, 128], P('gx', 'gy')
- grad_features: bfloat16 [32, 128, 16, 128], P('gx', 'gy')
- grad_first: float32 [27, 128, 128], P(None, 'gy')
- grad_second: float32 [27, 128, 128], P(None, 'gy')
The draws below stay inside these ranges and needn't reach their ends.
Inputs may be any that keep to these rules, and one draw needn't show every extreme that they name: `occupancy`: 1 marks an active block; the share of active blocks differs from one tile of 1 x 2 x 2 blocks to another.
All inputs are finite; a program needn't handle non-finite values.
Results may differ from the reference program's by a relative error of at most 0.0025.
The reference program's roundings to bfloat16 on the way (of `active`, `masked`, `hidden`, `up_grad` and `pre_grad`) count: a program that leaves them out, or rounds other values in their place, can miss the bound.
Values may be sent and summed in bfloat16 or wider, within the bound.
No kernel may reach another device: no remote copies, remote signals or barrier semaphores. Data moves between devices by JAX's collectives and lax.ppermute only.
A program may use at most 128 MiB of HBM per device.

```python
import math
import jax
import jax.numpy as jnp
from jax import lax

C = 128
TBX = 1
TBY = 2
NX = 32
NY = 128
NZ = 16
NBX = 4
NBY = 16
NBZ = 2


def draw_occupancy(key, part):
    base = jax.random.fold_in(key, 4471)
    key_tiles, key_blocks = jax.random.split(base)
    tiles_x = NBX // TBX
    tiles_y = NBY // TBY
    density = jax.random.randint(key_tiles, (tiles_x, tiles_y), 5, 101)
    spread = jnp.repeat(jnp.repeat(density, TBX, axis=0), TBY, axis=1)[:, :, None]
    rolled = jax.random.randint(key_blocks, (NBX, NBY, NBZ), 0, 100)
    return (rolled < spread).astype(jnp.int32)


def level_of(own_key, extent, cuts, smallest, high):
    loudness = 1.0
    for dim, shards_of in cuts:
        heights = jax.random.uniform(jax.random.fold_in(jax.random.fold_in(own_key, 6), dim), (shards_of,), jnp.float32, smallest / len(cuts), high / len(cuts))
        loudness = loudness * jnp.repeat(jnp.exp(heights), extent[dim] // shards_of).reshape((-1,) + (1,) * (len(extent) - 1 - dim))
    return loudness


def scatter_about(rng, dims, deviation, limit, cuts=(), held_as=jnp.bfloat16):
    array = jax.random.normal(rng, dims, jnp.float32) * deviation
    if len(cuts) > 0:
        array = level_of(rng, dims, cuts, -0.22, 0.18) * array
    return jnp.clip(array, min=-limit, max=limit).astype(held_as)


def setup_inputs(seed: int = 0) -> dict:
    key_of = jax.random.split(jax.random.key(seed), 6)
    return {
        "features": scatter_about(key_of[0], (NX, NY, NZ, C), 1.0, 6.0, ((0, 4), (1, 8))),
        "w_first": scatter_about(key_of[1], (27, C, C), (27 * C) ** -0.5, 0.109375),
        "w_second": scatter_about(key_of[2], (27, C, C), (27 * C) ** -0.5, 0.109375),
        "occupancy": draw_occupancy(jax.random.fold_in(key_of[5], 71), 0),
        "cotangent": scatter_about(key_of[4], (NX, NY, NZ, C), 1.0, 6.0, ((0, 4), (1, 8))),
    }


def voxel_mask(occupancy):
    block_x, block_y, block_z = occupancy.shape
    spread = jnp.broadcast_to(occupancy[:, None, :, None, :, None], (block_x, 8, block_y, 8, block_z, 8))
    return spread.reshape(block_x * 8, block_y * 8, block_z * 8).astype(jnp.bfloat16)

def arrange(weights):
    channels = weights.shape[2]
    forward = weights.reshape(3, 9 * channels, channels)
    backward = weights.reshape(3, 3, 3, channels, channels).swapaxes(3, 4).reshape(3, 9 * channels, channels)
    return (forward, backward)

def shifted_rows(padded, plane_x, flipped):
    inner_x = padded.shape[0] - 2
    inner_y = padded.shape[1] - 2
    inner_z = padded.shape[2] - 2
    channels = padded.shape[3]
    pieces = []
    for step_y in range(3):
        for step_z in range(3):
            if flipped:
                anchor = (2 - plane_x, 2 - step_y, 2 - step_z)
            else:
                anchor = (plane_x, step_y, step_z)
            pieces.append(padded[anchor[0]:anchor[0] + inner_x, anchor[1]:anchor[1] + inner_y, anchor[2]:anchor[2] + inner_z])
    return jnp.concatenate(pieces, axis=3).reshape(inner_x * inner_y * inner_z, 9 * channels)

def convolve(padded, kernel, flipped):
    inner_x = padded.shape[0] - 2
    inner_y = padded.shape[1] - 2
    inner_z = padded.shape[2] - 2
    summed = jnp.zeros((inner_x * inner_y * inner_z, kernel.shape[2]), jnp.float32)
    for plane_x in range(3):
        summed = summed + jnp.dot(shifted_rows(padded, plane_x, flipped), kernel[plane_x], preferred_element_type=jnp.float32)
    return summed.reshape(inner_x, inner_y, inner_z, kernel.shape[2])

def kernel_grad(padded, upstream):
    channels = upstream.shape[3]
    grad_rows = upstream.reshape(-1, channels)
    planes = []
    for plane_x in range(3):
        planes.append(lax.dot_general(shifted_rows(padded, plane_x, False), grad_rows, (((0,), (0,)), ((), ())), preferred_element_type=jnp.float32))
    return jnp.stack(planes).reshape(27, channels, channels)

def pad_all(field):
    return jnp.pad(field, ((1, 1), (1, 1), (1, 1), (0, 0)))

def slab_convolve(padded, kernel, flipped):
    slab_count = (padded.shape[0] - 2) // 8

    def per_slab(number):
        window = lax.dynamic_slice_in_dim(padded, number * 8, 10, 0)
        return convolve(window, kernel, flipped)
    stacked = lax.map(per_slab, jnp.arange(slab_count, dtype=jnp.int32))
    return stacked.reshape((-1,) + stacked.shape[2:])

def slab_kernel_grad(padded, upstream):
    slab_count = upstream.shape[0] // 8
    channels = upstream.shape[3]

    def accumulate(carried, number):
        window = lax.dynamic_slice_in_dim(padded, number * 8, 10, 0)
        grad_window = lax.dynamic_slice_in_dim(upstream, number * 8, 8, 0)
        return (carried + kernel_grad(window, grad_window), None)
    start_value = jnp.zeros((27, channels, channels), jnp.float32)
    result, unused = lax.scan(accumulate, start_value, jnp.arange(slab_count, dtype=jnp.int32))
    return result

def reference(features, w_first, w_second, occupancy, cotangent):
    active = voxel_mask(occupancy)[..., None]
    active_f = active.astype(jnp.float32)
    masked = features * active
    first_fwd, first_bwd = arrange(w_first)
    second_fwd, second_bwd = arrange(w_second)
    padded_x = pad_all(masked)
    pre_act = slab_convolve(padded_x, first_fwd, False)
    hidden = (active_f * jax.nn.silu(pre_act)).astype(jnp.bfloat16)
    padded_hidden = pad_all(hidden)
    second = slab_convolve(padded_hidden, second_fwd, False)
    output = (masked.astype(jnp.float32) + active_f * second).astype(jnp.bfloat16)
    up_grad = cotangent * active
    hidden_grad = slab_convolve(pad_all(up_grad), second_bwd, True)
    sigmoid_pre = jax.nn.sigmoid(pre_act)
    pre_grad = (active_f * hidden_grad * sigmoid_pre * (1.0 + pre_act * (1.0 - sigmoid_pre))).astype(jnp.bfloat16)
    feature_term = slab_convolve(pad_all(pre_grad), first_bwd, True)
    grad_features = (active_f * (cotangent.astype(jnp.float32) + feature_term)).astype(jnp.bfloat16)
    factor = 1.0 / math.sqrt(NX * NY * NZ)
    grad_second = slab_kernel_grad(padded_hidden, up_grad) * factor
    grad_first = slab_kernel_grad(padded_x, pre_grad) * factor
    return (output, grad_features, grad_first, grad_second)
```

```python
import math

import jax
import jax.numpy as jnp
from jax import lax
from jax.experimental import pallas as pl
from jax.experimental.pallas import tpu as pltpu
from jax.sharding import PartitionSpec as P

BF16 = jnp.bfloat16
F32 = jnp.float32
VMEM = pl.BlockSpec(memory_space=pltpu.VMEM)
SMEM = pl.BlockSpec(memory_space=pltpu.SMEM)
PARAMS = pltpu.CompilerParams(vmem_limit_bytes=48 * 1024 * 1024)
BLOCK = 8
X_ODD, Y_ODD, X_LOW, X_HIGH, Y_LOW, Y_HIGH, Y_INDEX = range(7)


def call(kernel, out_shapes, args, smem, scratch=(), flops=0, nbytes=0):
    return pl.pallas_call(
        kernel,
        out_shape=out_shapes,
        in_specs=[SMEM] * smem + [VMEM] * (len(args) - smem),
        out_specs=jax.tree.map(lambda _: VMEM, out_shapes),
        scratch_shapes=list(scratch),
        compiler_params=PARAMS,
        cost_estimate=pl.CostEstimate(flops=flops, bytes_accessed=nbytes, transcendentals=0),
    )(*args)


def swap_pairs(count, odd):
    if not odd:
        return [(i, i ^ 1) for i in range(count)]
    ends = [(0, 0), (count - 1, count - 1)]
    inner = [(i, i + 1) for i in range(1, count - 1, 2)]
    return ends + inner + [(b, a) for a, b in inner]


def plane_mask(occ, block_x, size_y, size_z):
    row = lax.broadcasted_iota(jnp.int32, (size_y * size_z, 128), 0)
    block_y = row // (BLOCK * size_z)
    block_z = (row % size_z) // BLOCK
    mask = jnp.zeros((size_y * size_z, 128), F32)
    for i in range(size_y // BLOCK):
        for j in range(size_z // BLOCK):
            here = (block_y == i) & (block_z == j)
            mask = jnp.where(here, occ[block_x, i, j].astype(F32), mask)
    return mask


def column_mask(occ, block_x, block_y, size_z):
    block_z = lax.broadcasted_iota(jnp.int32, (size_z, 128), 0) // BLOCK
    mask = jnp.zeros((size_z, 128), F32)
    for j in range(size_z // BLOCK):
        mask = jnp.where(block_z == j, occ[block_x, block_y, j].astype(F32), mask)
    return mask


def pick(odd, if_even, if_odd):
    return jnp.where(odd == 0, if_even, if_odd)


def pack_sides(fields, occ, flags):
    size_x, size_y, size_z, channels = fields[0].shape

    def kernel(flags, occ_ref, *refs):
        ins, (xa, xb, ya, yb) = refs[:2], refs[2:]
        first_x = pick(flags[X_ODD], size_x - 1, 0)
        first_y = pick(flags[Y_ODD], size_y - 1, 0)
        for f in range(2):
            for out, x in ((xa, first_x), (xb, size_x - 1 - first_x)):
                plane = ins[f][x]
                if occ is not None:
                    mask = plane_mask(occ_ref, x // BLOCK, size_y, size_z).astype(BF16)
                    plane = plane * mask.reshape(plane.shape)
                out[f] = plane
            for out, y in ((ya, first_y), (yb, size_y - 1 - first_y)):
                for x in range(size_x):
                    column = ins[f][x, y]
                    if occ is not None:
                        column = column * column_mask(occ_ref, x // BLOCK, y // BLOCK, size_z).astype(BF16)
                    out[f, x] = column

    if occ is None:
        occ_arg = flags
    else:
        occ_arg = occ
    side = jax.ShapeDtypeStruct((2, size_y, size_z, channels), BF16)
    column = jax.ShapeDtypeStruct((2, size_x, size_z, channels), BF16)
    return call(kernel, (side, side, column, column), (flags, occ_arg, *fields), 2, nbytes=3 << 20)


def finish_columns(flags, got_xa, got_xb, ya, yb):
    _, size_y, size_z, channels = got_xa.shape
    size_x = ya.shape[1]

    def kernel(flags, xa, xb, ya, yb, out_a, out_b):
        odd = flags[X_ODD]
        first_y = pick(flags[Y_ODD], size_y - 1, 0)
        low_ok = flags[X_LOW].astype(F32).astype(BF16)
        high_ok = flags[X_HIGH].astype(F32).astype(BF16)
        for out, own, y in ((out_a, ya, first_y), (out_b, yb, size_y - 1 - first_y)):
            for f in range(2):
                out[f, 0] = pick(odd, xb[f, y], xa[f, y]) * low_ok
                out[f, size_x + 1] = pick(odd, xa[f, y], xb[f, y]) * high_ok
                out[f, 1 : size_x + 1] = own[f]

    shape = jax.ShapeDtypeStruct((2, size_x + 2, size_z, channels), BF16)
    return call(kernel, (shape, shape), (flags, got_xa, got_xb, ya, yb), 1, nbytes=1 << 20)


def exchange(fields, occ, flags):
    even_x, odd_x = (swap_pairs(lax.axis_size("gx"), odd) for odd in (False, True))
    even_y, odd_y = (swap_pairs(lax.axis_size("gy"), odd) for odd in (False, True))
    xa, xb, ya, yb = pack_sides(fields, occ, flags)
    xa = lax.ppermute(xa, "gx", even_x)
    xb = lax.ppermute(xb, "gx", odd_x)
    ya, yb = finish_columns(flags, xa, xb, ya, yb)
    ya = lax.ppermute(ya, "gy", even_y)
    yb = lax.ppermute(yb, "gy", odd_y)
    return xa, xb, ya, yb


def store_shifts(zc, x, ys, rows):
    size_z = zc.shape[2]
    count, lanes = rows.shape
    wide = rows.astype(F32)
    z = lax.broadcasted_iota(jnp.int32, (count, lanes), 0) % size_z
    below = jnp.where(z == 0, 0.0, pltpu.roll(wide, 1, 0)).astype(BF16)
    above = jnp.where(z == size_z - 1, 0.0, pltpu.roll(wide, count - 1, 0)).astype(BF16)
    shape = (count // size_z, size_z, lanes)
    for k, part in enumerate((below, rows, above)):
        zc[x, ys[0] : ys[1], :, k * lanes : (k + 1) * lanes] = part.reshape(shape)


def fill(zc, f, plane, xa, xb, ya, yb, flags):
    size_x, size_y, size_z = zc.shape[0] - 2, zc.shape[1] - 2, zc.shape[2]
    channels = xa.shape[3]
    rows = size_y * size_z
    odd_x, odd_y = flags[X_ODD], flags[Y_ODD]
    ok = [flags[i].astype(F32).astype(BF16) for i in (X_LOW, X_HIGH, Y_LOW, Y_HIGH)]
    for x in range(size_x):
        store_shifts(zc, x + 1, (1, size_y + 1), plane(x))
    store_shifts(zc, 0, (1, size_y + 1), (pick(odd_x, xb[f], xa[f]) * ok[0]).reshape(rows, channels))
    store_shifts(zc, size_x + 1, (1, size_y + 1), (pick(odd_x, xa[f], xb[f]) * ok[1]).reshape(rows, channels))
    for x in range(size_x + 2):
        store_shifts(zc, x, (0, 1), pick(odd_y, yb[f, x], ya[f, x]) * ok[2])
        store_shifts(zc, x, (size_y + 1, size_y + 2), pick(odd_y, ya[f, x], yb[f, x]) * ok[3])


def lay_weights(taps, w):
    channels = w.shape[1]
    zero = jnp.zeros((3 * channels, channels), BF16)
    for i in range(4):
        for j in range(3):
            for side in range(2):
                tap = i - side
                part = w[9 * tap + 3 * j : 9 * tap + 3 * j + 3].reshape(3 * channels, channels) if 0 <= tap < 3 else zero
                taps[3 * i + j, :, side * channels : (side + 1) * channels] = part


def convolve(zc, taps, emit):
    size_x, size_y, size_z = zc.shape[0] - 2, zc.shape[1] - 2, zc.shape[2]
    depth = zc.shape[3]
    channels = depth // 3
    rows = size_y * size_z
    for x in range(0, size_x, 4):
        pieces = []
        for i in range(4):
            for j in range(3):
                halves = [zc[x + 2 * h + i, j : j + size_y].reshape(rows, depth) for h in range(2)]
                pieces.append(jnp.concatenate(halves, axis=0))
        both = jnp.dot(
            jnp.concatenate(pieces, axis=1),
            taps[...].reshape(12 * depth, 2 * channels),
            preferred_element_type=F32,
        )
        for h in range(2):
            for side in range(2):
                emit(x + 2 * h + side, both[h * rows : (h + 1) * rows, side * channels : (side + 1) * channels])


def turn_weights(w_first, w_second):
    def kernel(first, second, out_first, out_second):
        for w, out in ((first, out_first), (second, out_second)):
            for d in range(27):
                out[26 - d] = w[d].T

    shape = jax.ShapeDtypeStruct(w_first.shape, BF16)
    return call(kernel, (shape, shape), (w_first, w_second), 0, nbytes=4 << 20)


def field_scratch(shape):
    size_x, size_y, size_z, channels = shape
    return pltpu.VMEM((size_x + 2, size_y + 2, size_z, 3 * channels), BF16)


def taps_scratch(channels):
    return pltpu.VMEM((12, 3 * channels, 2 * channels), BF16)


def first_half(flags, occ, features, cotangent, halos, w_first, turned_second):
    size_x, size_y, size_z, channels = features.shape
    rows = size_y * size_z
    count_y = lax.axis_size("gy")
    share = channels // count_y

    def kernel(flags, occ, feat, cot, xa, xb, ya, yb, w1, w2t, hidden, pre_grad, keep, send, zm, zu, taps, slope):
        def masked(ref):
            def plane(x):
                mask = plane_mask(occ, x // BLOCK, size_y, size_z).astype(BF16)
                return ref[x].reshape(rows, channels) * mask

            return plane

        fill(zm, 0, masked(feat), xa, xb, ya, yb, flags)
        fill(zu, 1, masked(cot), xa, xb, ya, yb, flags)
        lay_weights(taps, w1)

        def emit_hidden(x, pre):
            mask = plane_mask(occ, x // BLOCK, size_y, size_z)
            s = jax.nn.sigmoid(pre)
            hidden[x] = (mask * (pre * s)).astype(BF16).reshape(size_y, size_z, channels)
            slope[x] = mask * (s * (1.0 + pre * (1.0 - s)))

        convolve(zm, taps, emit_hidden)
        lay_weights(taps, w2t)

        def emit_grad(x, grad):
            pre_grad[x] = (grad * slope[x]).astype(BF16).reshape(size_y, size_z, channels)

        convolve(zu, taps, emit_grad)

        half = flags[Y_INDEX] % 2
        place = flags[Y_INDEX] // 2

        def store(g, d, block):
            for j in range(count_y // 2):
                even = block[2 * j * share : (2 * j + 1) * share]
                odd = block[(2 * j + 1) * share : (2 * j + 2) * share]
                at = jnp.bitwise_xor(place, j)
                keep[at, g, d] = pick(half, even, odd)
                send[at, g, d] = pick(half, odd, even)

        shifts = [(i, j) for i in range(3) for j in range(3)]
        groups = [shifts[i : i + 2] for i in range(0, 9, 2)]

        def products(left, zc, start):
            for group in groups:
                pieces = []
                for i, j in group:
                    a, b = start(i, j)
                    pieces.append(zc[a : a + size_x, b : b + size_y].reshape(size_x * rows, 3 * channels))
                out = jnp.dot(left, jnp.concatenate(pieces, axis=1), preferred_element_type=F32)
                for n, (i, j) in enumerate(group):
                    for k in range(3):
                        yield 9 * i + 3 * j, k, out[:, (3 * n + k) * channels : (3 * n + k + 1) * channels]

        turned = hidden[...].reshape(size_x * rows, channels).T
        for d, k, block in products(turned, zu, lambda i, j: (2 - i, 2 - j)):
            store(0, d + 2 - k, block)
        turned = pre_grad[...].reshape(size_x * rows, channels).T
        for d, k, block in products(turned, zm, lambda i, j: (i, j)):
            store(1, d + k, block.T)

    field = jax.ShapeDtypeStruct(features.shape, BF16)
    terms = jax.ShapeDtypeStruct((count_y // 2, 2, 27, share, channels), F32)
    return call(
        kernel,
        (field, field, terms, terms),
        (flags, occ, features, cotangent, *halos, w_first, turned_second),
        2,
        scratch=[
            field_scratch(features.shape),
            field_scratch(features.shape),
            taps_scratch(channels),
            pltpu.VMEM((size_x, rows, channels), F32),
        ],
        flops=8 * 27 * size_x * rows * channels * channels,
        nbytes=8 << 20,
    )


def second_half(flags, occ, features, cotangent, hidden, pre_grad, halos, w_second, turned_first):
    size_x, size_y, size_z, channels = features.shape
    rows = size_y * size_z

    def kernel(flags, occ, feat, cot, hid, pre, xa, xb, ya, yb, w2, w1t, output, grad, zh, zp, taps):
        fill(zh, 0, lambda x: hid[x].reshape(rows, channels), xa, xb, ya, yb, flags)
        fill(zp, 1, lambda x: pre[x].reshape(rows, channels), xa, xb, ya, yb, flags)
        lay_weights(taps, w2)

        def emit_output(x, second):
            mask = plane_mask(occ, x // BLOCK, size_y, size_z)
            own = feat[x].reshape(rows, channels).astype(F32)
            output[x] = (mask * (own + second)).astype(BF16).reshape(size_y, size_z, channels)

        convolve(zh, taps, emit_output)
        lay_weights(taps, w1t)

        def emit_grad(x, term):
            mask = plane_mask(occ, x // BLOCK, size_y, size_z)
            own = cot[x].reshape(rows, channels).astype(F32)
            grad[x] = (mask * (own + term)).astype(BF16).reshape(size_y, size_z, channels)

        convolve(zp, taps, emit_grad)

    field = jax.ShapeDtypeStruct(features.shape, BF16)
    return call(
        kernel,
        (field, field),
        (flags, occ, features, cotangent, hidden, pre_grad, *halos, w_second, turned_first),
        2,
        scratch=[field_scratch(features.shape), field_scratch(features.shape), taps_scratch(channels)],
        flops=4 * 27 * size_x * rows * channels * channels,
        nbytes=6 << 20,
    )


def swap(value, axis, bit, travel):
    pairs = [(i, i ^ bit) for i in range(lax.axis_size(axis))]
    return lax.ppermute(value.astype(travel), axis, pairs).astype(F32)


def reduce_terms(keep, send):
    count_y = lax.axis_size("gy")
    bits = count_y.bit_length() - 1
    rows = keep.shape[2] * keep.shape[3]
    got = swap(send, "gy", 1, F32)
    total = (keep + got).reshape((2,) * (bits - 1) + (2, rows, keep.shape[4]))
    totals = []
    for g in range(2):
        part = total[(slice(None),) * (bits - 1) + (g,)]
        left = list(range(1, bits))
        order = left[:] if g == 0 else left[::-1]
        for bit in order:
            dim = len(left) - 1 - left.index(bit)
            leaves = lax.index_in_dim(part, 1, dim, keepdims=False)
            stays = lax.index_in_dim(part, 0, dim, keepdims=False)
            part = stays + swap(leaves, "gy", 1 << bit, BF16)
            left.remove(bit)
        totals.append(part)
    count_x = lax.axis_size("gx")
    odd = lax.axis_index("gx") % 2 == 1
    stays = jnp.where(odd, totals[1], totals[0])
    leaves = jnp.where(odd, totals[0], totals[1])
    stays = stays + swap(leaves, "gx", 1, F32)
    bit = 2
    while bit < count_x:
        stays = stays + swap(stays, "gx", bit, F32)
        bit *= 2
    other = swap(stays, "gx", 1, F32)
    return jnp.where(odd, other, stays), jnp.where(odd, stays, other)


def body(features, w_first, w_second, occupancy, cotangent):
    count_x, count_y = lax.axis_size("gx"), lax.axis_size("gy")
    index_x, index_y = lax.axis_index("gx"), lax.axis_index("gy")
    size_x, size_y, size_z, channels = features.shape
    flags = jnp.stack(
        [
            index_x % 2,
            index_y % 2,
            index_x > 0,
            index_x < count_x - 1,
            index_y > 0,
            index_y < count_y - 1,
            index_y,
            index_y * 0,
        ]
    ).astype(jnp.int32)
    halos = exchange((features, cotangent), occupancy, flags)
    turned_first, turned_second = turn_weights(w_first, w_second)
    hidden, pre_grad, keep, send = first_half(
        flags, occupancy, features, cotangent, halos, w_first, turned_second
    )
    total_second, total_first = reduce_terms(keep, send)
    halos = exchange((hidden, pre_grad), None, flags)
    output, grad_features = second_half(
        flags, occupancy, features, cotangent, hidden, pre_grad, halos, w_second, turned_first
    )
    factor = 1.0 / math.sqrt(count_x * count_y * size_x * size_y * size_z)
    shape = (27, channels // count_y, channels)
    return (
        output,
        grad_features,
        total_first.reshape(shape) * factor,
        total_second.reshape(shape) * factor,
    )


def solution(mesh):
    in_specs = (P("gx", "gy", None, None), P(), P(), P("gx", "gy", None), P("gx", "gy", None, None))
    out_specs = (
        P("gx", "gy", None, None),
        P("gx", "gy", None, None),
        P(None, "gy", None),
        P(None, "gy", None),
    )
    return jax.shard_map(body, mesh=mesh, in_specs=in_specs, out_specs=out_specs, check_vma=False)
```

```python
import math

import jax
import jax.numpy as jnp
from jax import lax
from jax.experimental import pallas as pl
from jax.experimental.pallas import tpu as pltpu
from jax.sharding import PartitionSpec as P

BF16 = jnp.bfloat16
F32 = jnp.float32
VMEM = pl.BlockSpec(memory_space=pltpu.VMEM)
HBM = pl.BlockSpec(memory_space=pltpu.HBM)
MIB = 1024 * 1024
BLOCK = 8


def call(kernel, out_shapes, args, spaces, scratch=(), flops=0, nbytes=0, vmem=16 * MIB, aliases=None):
    return pl.pallas_call(
        kernel,
        out_shape=out_shapes,
        in_specs=list(spaces) + [VMEM] * (len(args) - len(spaces)),
        out_specs=jax.tree.map(lambda _: VMEM, out_shapes),
        scratch_shapes=list(scratch),
        input_output_aliases=aliases or {},
        compiler_params=pltpu.CompilerParams(vmem_limit_bytes=vmem),
        cost_estimate=pl.CostEstimate(flops=flops, bytes_accessed=nbytes, transcendentals=0),
    )(*args)


def swap_pairs(count, odd):
    if not odd:
        return [(i, i ^ 1) for i in range(count)]
    ends = [(0, 0), (count - 1, count - 1)]
    inner = [(i, i + 1) for i in range(1, count - 1, 2)]
    return ends + inner + [(b, a) for a, b in inner]


def plane_mask(occ, block_x, size_y, size_z):
    row = lax.broadcasted_iota(jnp.int32, (size_y * size_z, 128), 0)
    block_y = row // (BLOCK * size_z)
    block_z = (row % size_z) // BLOCK
    mask = jnp.zeros((size_y * size_z, 128), F32)
    for i in range(size_y // BLOCK):
        for j in range(size_z // BLOCK):
            here = (block_y == i) & (block_z == j)
            mask = jnp.where(here, occ[block_x, i, j].astype(F32), mask)
    return mask


def pick(odd, if_even, if_odd):
    return jnp.where(odd == 0, if_even, if_odd)


def one_if(condition):
    return jnp.where(condition, 1.0, 0.0).astype(BF16)


def side_of(axis):
    index = lax.axis_index(axis)
    return index % 2, one_if(index > 0), one_if(index < lax.axis_size(axis) - 1)


def pack_sides(features, cotangent, occ):
    size_x, size_y, size_z, channels = features.shape
    rows = size_y * size_z

    def kernel(occ_hbm, first, second, mask, xa, xb, ya, yb, occ_ref, sem, occ_sem):
        odd_x, odd_y = lax.axis_index("gx") % 2, lax.axis_index("gy") % 2
        first_x = pick(odd_x, size_x - 1, 0)
        first_y = pick(odd_y, size_y - 1, 0)
        sides = ((xa, first_x), (xb, size_x - 1 - first_x))
        columns = ((ya, first_y), (yb, size_y - 1 - first_y))
        occ_copy = pltpu.make_async_copy(occ_hbm, occ_ref, occ_sem)
        occ_copy.start()
        copies = []
        for f, ref in enumerate((first, second)):
            for n, (out, x) in enumerate(sides):
                copies.append(pltpu.make_async_copy(ref.at[x], out.at[f], sem.at[f, n]))
            for n, (out, y) in enumerate(columns):
                copies.append(pltpu.make_async_copy(ref.at[:, y], out.at[f], sem.at[f, 2 + n]))
        for copy in copies:
            copy.start()
        occ_copy.wait()
        for n in range(size_x // BLOCK):
            mask[n] = plane_mask(occ_ref, n, size_y, size_z)
        for copy in copies:
            copy.wait()
        for out, x in sides:
            here = mask[x // BLOCK].astype(BF16).reshape(size_y, size_z, channels)
            for f in range(2):
                out[f] = out[f] * here
        for out, y in columns:
            at = pl.ds(pl.multiple_of(y * size_z, size_z), size_z)
            for x in range(size_x):
                here = mask[x // BLOCK, at, :].astype(BF16)
                for f in range(2):
                    out[f, x] = out[f, x] * here

    side = pltpu.VMEM((2, size_y, size_z, channels), BF16)
    column = pltpu.VMEM((2, size_x, size_z, channels), BF16)
    return call(
        kernel,
        (pltpu.VMEM((size_x // BLOCK, rows, channels), F32), side, side, column, column),
        [pltpu.with_memory_space_constraint(value, pltpu.HBM) for value in (occ, features, cotangent)],
        [HBM] * 3,
        scratch=[
            pltpu.SMEM(occ.shape, jnp.int32),
            pltpu.SemaphoreType.DMA((2, 4)),
            pltpu.SemaphoreType.DMA(()),
        ],
        nbytes=MIB,
        vmem=4 * MIB,
    )


def finish_columns(got_xa, got_xb, ya, yb):
    _, size_y, size_z, channels = got_xa.shape
    size_x = ya.shape[1]

    def kernel(xa, xb, ya, yb, out_a, out_b):
        odd, low_ok, high_ok = side_of("gx")
        first_y = pick(lax.axis_index("gy") % 2, size_y - 1, 0)
        for out, own, y in ((out_a, ya, first_y), (out_b, yb, size_y - 1 - first_y)):
            for f in range(2):
                out[f, 0] = pick(odd, xb[f, y], xa[f, y]) * low_ok
                out[f, size_x + 1] = pick(odd, xa[f, y], xb[f, y]) * high_ok
                out[f, 1 : size_x + 1] = own[f]

    shape = jax.ShapeDtypeStruct((2, size_x + 2, size_z, channels), BF16)
    return call(kernel, (shape, shape), (got_xa, got_xb, ya, yb), [], nbytes=MIB, vmem=4 * MIB)


def swap_sides(xa, xb):
    even, odd = (swap_pairs(lax.axis_size("gx"), which) for which in (False, True))
    return lax.ppermute(xa, "gx", even), lax.ppermute(xb, "gx", odd)


def swap_columns(ya, yb):
    even, odd = (swap_pairs(lax.axis_size("gy"), which) for which in (False, True))
    return lax.ppermute(ya, "gy", even), lax.ppermute(yb, "gy", odd)


def store_shifts(zc, x, ys, rows):
    size_z = zc.shape[2]
    count, lanes = rows.shape
    wide = rows.astype(F32)
    z = lax.broadcasted_iota(jnp.int32, (count, lanes), 0) % size_z
    below = jnp.where(z == 0, 0.0, pltpu.roll(wide, 1, 0)).astype(BF16)
    above = jnp.where(z == size_z - 1, 0.0, pltpu.roll(wide, count - 1, 0)).astype(BF16)
    shape = (count // size_z, size_z, lanes)
    for k, part in enumerate((below, rows, above)):
        zc[x, ys[0] : ys[1], :, k * lanes : (k + 1) * lanes] = part.reshape(shape)


def fill_own(zc, plane):
    size_x, size_y = zc.shape[0] - 2, zc.shape[1] - 2
    zc[0] = jnp.zeros(zc.shape[1:], BF16)
    zc[size_x + 1] = jnp.zeros(zc.shape[1:], BF16)
    for x in range(size_x):
        for y in (0, size_y + 1):
            zc[x + 1, y] = jnp.zeros(zc.shape[2:], BF16)
        store_shifts(zc, x + 1, (1, size_y + 1), plane(x))


def fill_sides(zc, f, xa, xb):
    size_x, size_y, size_z = zc.shape[0] - 2, zc.shape[1] - 2, zc.shape[2]
    rows = size_y * size_z
    odd, low_ok, high_ok = side_of("gx")
    channels = xa.shape[3]
    store_shifts(zc, 0, (1, size_y + 1), (pick(odd, xb[f], xa[f]) * low_ok).reshape(rows, channels))
    store_shifts(zc, size_x + 1, (1, size_y + 1), (pick(odd, xa[f], xb[f]) * high_ok).reshape(rows, channels))


def fill_columns(zc, f, ya, yb):
    size_x, size_y = zc.shape[0] - 2, zc.shape[1] - 2
    odd, low_ok, high_ok = side_of("gy")
    for x in range(size_x + 2):
        store_shifts(zc, x, (0, 1), pick(odd, yb[f, x], ya[f, x]) * low_ok)
        store_shifts(zc, x, (size_y + 1, size_y + 2), pick(odd, ya[f, x], yb[f, x]) * high_ok)


def straight(w):
    return lambda tap: w[tap]


def turned(w):
    return lambda tap: w[26 - tap].T


def lay_weights(taps, weight):
    channels = taps.shape[2] // 2
    zero = jnp.zeros((channels, channels), BF16)
    for j in range(3):
        for k in range(3):
            rows = slice(k * channels, (k + 1) * channels)
            for tap in range(3):
                value = weight(9 * tap + 3 * j + k)
                taps[3 * tap + j, rows, :channels] = value
                taps[3 * (tap + 1) + j, rows, channels:] = value
            taps[j, rows, channels:] = zero
            taps[9 + j, rows, :channels] = zero


def convolve(zc, taps, emit):
    size_x, size_y, size_z = zc.shape[0] - 2, zc.shape[1] - 2, zc.shape[2]
    depth = zc.shape[3]
    channels = depth // 3
    rows = size_y * size_z
    for x in range(0, size_x, 4):
        pieces = []
        for i in range(4):
            for j in range(3):
                halves = [zc[x + 2 * h + i, j : j + size_y].reshape(rows, depth) for h in range(2)]
                pieces.append(jnp.concatenate(halves, axis=0))
        both = jnp.dot(
            jnp.concatenate(pieces, axis=1),
            taps[...].reshape(12 * depth, 2 * channels),
            preferred_element_type=F32,
        )
        for h in range(2):
            for side in range(2):
                emit(x + 2 * h + side, both[h * rows : (h + 1) * rows, side * channels : (side + 1) * channels])


def add_halo_terms(total, zc, taps):
    size_x, size_y, size_z = zc.shape[0] - 2, zc.shape[1] - 2, zc.shape[2]
    depth = zc.shape[3]
    channels = depth // 3
    rows = size_y * size_z

    def weights(which):
        return jnp.concatenate([taps[n, :, :channels] for n in which], axis=0)

    for plane, x, first in ((0, 0, 0), (size_x + 1, size_x - 1, 6)):
        side = jnp.concatenate([zc[plane, j : j + size_y].reshape(rows, depth) for j in range(3)], axis=1)
        total[x] += jnp.dot(side, weights((first, first + 1, first + 2)), preferred_element_type=F32)
    none = jnp.zeros((size_z, depth), BF16)
    for column, y, j in ((0, 0, 0), (size_y + 1, size_y - 1, 2)):
        own = zc[1 : size_x + 1, column].reshape(size_x * size_z, depth)
        below = jnp.concatenate([none, own[:-size_z]], axis=0)
        above = jnp.concatenate([own[size_z:], none], axis=0)
        side = jnp.concatenate([below, own, above], axis=1)
        term = jnp.dot(side, weights((j, 3 + j, 6 + j)), preferred_element_type=F32)
        total[:, y * size_z : (y + 1) * size_z, :] += term.reshape(size_x, size_z, channels)


def field_shape(shape):
    size_x, size_y, size_z, channels = shape
    return (size_x + 2, size_y + 2, size_z, 3 * channels)


def taps_shape(channels):
    return (12, 3 * channels, 2 * channels)


def own_terms(mask, field, w, lay):
    size_x, size_y, size_z, channels = field.shape
    rows = size_y * size_z

    def kernel(mask, field, w, zc, taps, total):
        def plane(x):
            return field[x].reshape(rows, channels) * mask[x // BLOCK].astype(BF16)

        fill_own(zc, plane)
        lay_weights(taps, lay(w))

        def emit(x, value):
            total[x] = value

        convolve(zc, taps, emit)

    return call(
        kernel,
        (
            jax.ShapeDtypeStruct(field_shape(field.shape), BF16),
            jax.ShapeDtypeStruct(taps_shape(channels), BF16),
            jax.ShapeDtypeStruct((size_x, rows, channels), F32),
        ),
        (mask, field, w),
        [],
        flops=2 * 27 * size_x * rows * channels * channels,
        nbytes=4 * MIB,
        vmem=24 * MIB,
    )


def copy_sides(f, value, xa, xb, ya, yb):
    size_x, size_y = value.shape[:2]
    first_x = pick(lax.axis_index("gx") % 2, size_x - 1, 0)
    first_y = pick(lax.axis_index("gy") % 2, size_y - 1, 0)
    xa[f], xb[f] = value[first_x], value[size_x - 1 - first_x]
    for x in range(size_x):
        ya[f, x], yb[f, x] = value[x, first_y], value[x, size_y - 1 - first_y]


def side_shapes(shape):
    size_x, size_y, size_z, channels = shape
    side = jax.ShapeDtypeStruct((2, size_y, size_z, channels), BF16)
    column = jax.ShapeDtypeStruct((2, size_x, size_z, channels), BF16)
    return (side, side, column, column)


def grad_terms(left, zc, start, store):
    size_x, size_y, size_z = zc.shape[0] - 2, zc.shape[1] - 2, zc.shape[2]
    depth = zc.shape[3]
    channels = depth // 3
    shifts = [(i, j) for i in range(3) for j in range(3)]
    for group in [shifts[n : n + 2] for n in range(0, 9, 2)]:
        pieces = []
        for i, j in group:
            a, b = start(i, j)
            pieces.append(zc[a : a + size_x, b : b + size_y].reshape(size_x * size_y * size_z, depth))
        out = jnp.dot(left, jnp.concatenate(pieces, axis=1), preferred_element_type=F32)
        for n, (i, j) in enumerate(group):
            for k in range(3):
                store(9 * i + 3 * j, k, out[:, (3 * n + k) * channels : (3 * n + k + 1) * channels])


def scatter_block(keep, send, d, block):
    count = 2 * keep.shape[0]
    share = keep.shape[2]
    index = lax.axis_index("gy")
    half, place = index % 2, index // 2
    for j in range(count // 2):
        even = block[2 * j * share : (2 * j + 1) * share]
        odd = block[(2 * j + 1) * share : (2 * j + 2) * share]
        at = jnp.bitwise_xor(place, j)
        keep[at, d] = pick(half, even, odd)
        send[at, d] = pick(half, odd, even)


def terms_shape(channels):
    count_y = lax.axis_size("gy")
    return jax.ShapeDtypeStruct((count_y // 2, 27, channels // count_y, channels), F32)


def hidden_and_terms(mask, halos, zm, zu, taps, pre, shape):
    size_x, size_y, size_z, channels = shape
    rows = size_y * size_z

    def kernel(mask, xa, xb, ya, yb, taps, pre, zm_in, zu_in, zm, zu, hidden, slope, keep, send):
        for f, zc in enumerate((zm, zu)):
            fill_sides(zc, f, xa, xb)
            fill_columns(zc, f, ya, yb)
        slope[...] = pre[...]
        add_halo_terms(slope, zm, taps)
        for x in range(size_x):
            here = mask[x // BLOCK]
            value = slope[x]
            s = jax.nn.sigmoid(value)
            hidden[x] = (here * (value * s)).astype(BF16).reshape(size_y, size_z, channels)
            slope[x] = here * (s * (1.0 + value * (1.0 - s)))
        left = hidden[...].reshape(size_x * rows, channels).T

        def store(d, k, block):
            scatter_block(keep, send, d + 2 - k, block)

        grad_terms(left, zu, lambda i, j: (2 - i, 2 - j), store)

    field = jax.ShapeDtypeStruct(shape, BF16)
    wide = jax.ShapeDtypeStruct(pre.shape, F32)
    shifted = jax.ShapeDtypeStruct(zm.shape, BF16)
    terms = terms_shape(channels)
    return call(
        kernel,
        (shifted, shifted, field, wide, terms, terms),
        (mask, *halos, taps, pre, zm, zu),
        [],
        flops=2 * 27 * size_x * rows * channels * channels,
        nbytes=8 * MIB,
        vmem=24 * MIB,
        aliases={7: 0, 8: 1},
    )


def pre_grad_and_terms(hidden, slope, zm, zu, taps, grad):
    size_x, rows, channels = grad.shape
    size_y, size_z = zu.shape[1] - 2, zu.shape[2]
    shape = (size_x, size_y, size_z, channels)

    def kernel(hidden, slope, zm, zu, taps, grad, pre_grad, keep, send, xa, xb, ya, yb, total):
        total[...] = grad[...]
        add_halo_terms(total, zu, taps)
        for x in range(size_x):
            pre_grad[x] = (total[x] * slope[x]).astype(BF16).reshape(size_y, size_z, channels)
        for f, value in enumerate((hidden, pre_grad)):
            copy_sides(f, value, xa, xb, ya, yb)
        left = pre_grad[...].reshape(size_x * rows, channels).T

        def store(d, k, block):
            scatter_block(keep, send, d + k, block.T)

        grad_terms(left, zm, lambda i, j: (i, j), store)

    terms = terms_shape(channels)
    return call(
        kernel,
        (jax.ShapeDtypeStruct(shape, BF16), terms, terms, *side_shapes(shape)),
        (hidden, slope, zm, zu, taps, grad),
        [],
        scratch=[pltpu.VMEM(grad.shape, F32)],
        flops=2 * 27 * size_x * rows * channels * channels,
        nbytes=8 * MIB,
        vmem=24 * MIB,
    )


def add_convolution(mask, own, field, f, halos, w, lay):
    size_x, size_y, size_z, channels = own.shape
    rows = size_y * size_z

    def kernel(mask, own, field, xa, xb, ya, yb, w, out, zc, taps):
        for x in range(size_x):
            store_shifts(zc, x + 1, (1, size_y + 1), field[x].reshape(rows, channels))
        fill_sides(zc, f, xa, xb)
        fill_columns(zc, f, ya, yb)
        lay_weights(taps, lay(w))

        def emit(x, term):
            near = own[x].reshape(rows, channels).astype(F32)
            out[x] = (mask[x // BLOCK] * (near + term)).astype(BF16).reshape(size_y, size_z, channels)

        convolve(zc, taps, emit)

    return call(
        kernel,
        jax.ShapeDtypeStruct(own.shape, BF16),
        (mask, own, field, *halos, w),
        [],
        scratch=[pltpu.VMEM(field_shape(own.shape), BF16), pltpu.VMEM(taps_shape(channels), BF16)],
        flops=2 * 27 * size_x * rows * channels * channels,
        nbytes=3 * MIB,
        vmem=24 * MIB,
    )


def after(values, *others):
    return lax.optimization_barrier((values, others))[0]


def swap(value, axis, bit, travel):
    pairs = [(i, i ^ bit) for i in range(lax.axis_size(axis))]
    return lax.ppermute(value.astype(travel), axis, pairs)


def first_sums(keeps, cames):
    places, taps, share, channels = keeps[0].shape
    rows = taps * share

    def kernel(keep_a, keep_b, came_a, came_b, stays, *leaves):
        for g, (keep, came) in enumerate(((keep_a, came_a), (keep_b, came_b))):
            for p in range(places):
                value = (keep[p] + came[p]).reshape(rows, channels)
                if p == 0:
                    stays[g] = value
                else:
                    leaves[p - 1][g] = value.astype(BF16)

    stay = jax.ShapeDtypeStruct((2, rows, channels), F32)
    leave = jax.ShapeDtypeStruct((2, rows, channels), BF16)
    return call(kernel, (stay,) + (leave,) * (places - 1), (*keeps, *cames), [], nbytes=4 * MIB, vmem=8 * MIB)


def body(features, w_first, w_second, occ, cotangent):
    count_x, count_y = lax.axis_size("gx"), lax.axis_size("gy")
    shape = features.shape
    mask, xa, xb, ya, yb = pack_sides(features, cotangent, occ)
    xa, xb = swap_sides(xa, xb)
    zm, first_taps, pre = own_terms(mask, features, w_first, straight)
    xa, xb = after((xa, xb), pre)
    ya, yb = finish_columns(xa, xb, ya, yb)
    behind = after(mask, ya)
    ya, yb = swap_columns(ya, yb)
    zu, second_taps, grad = own_terms(behind, cotangent, w_second, turned)
    halos = after((xa, xb, ya, yb), grad)
    zm, zu, hidden, slope, keep_second, send = hidden_and_terms(mask, halos, zm, zu, first_taps, pre, shape)
    came_second = swap(send, "gy", 1, F32)
    pre_grad, keep_first, send, xa, xb, ya, yb = pre_grad_and_terms(hidden, slope, zm, zu, second_taps, grad)
    came_first = swap(send, "gy", 1, F32)
    xa, xb = swap_sides(xa, xb)

    stays, *leaves = first_sums((keep_second, keep_first), (came_second, came_first))
    came = [swap(value, "gy", 2 * (p + 1), BF16) for p, value in enumerate(leaves)]
    xa, xb = after((xa, xb), stays)
    ya, yb = finish_columns(xa, xb, ya, yb)
    came = after(came, ya)
    ya, yb = swap_columns(ya, yb)
    for value in came:
        stays = stays + value.astype(F32)
    odd = lax.axis_index("gx") % 2 == 1
    leaves = jnp.where(odd, stays[0], stays[1])
    stays = jnp.where(odd, stays[1], stays[0])
    came = swap(leaves, "gx", 1, F32)
    halos = after((xa, xb, ya, yb), leaves)
    output = add_convolution(mask, features, hidden, 0, halos, w_second, straight)
    stays = stays + after(came, output)
    bit = 2
    while bit < count_x:
        came = swap(stays, "gx", bit, F32)
        if bit == 2:
            halos = after((xa, xb, ya, yb), stays)
            grad_features = add_convolution(mask, cotangent, pre_grad, 1, halos, w_first, turned)
            came = after(came, grad_features)
        stays = stays + came
        bit *= 2
    came = swap(stays, "gx", 1, F32)
    factor = 1.0 / math.sqrt(count_x * count_y * shape[0] * shape[1] * shape[2])
    total_second = jnp.where(odd, came, stays) * factor
    total_first = jnp.where(odd, stays, came) * factor
    kernel_shape = (27, -1, shape[3])
    return output, grad_features, total_first.reshape(kernel_shape), total_second.reshape(kernel_shape)


def solution(mesh):
    in_specs = (P("gx", "gy", None, None), P(), P(), P("gx", "gy", None), P("gx", "gy", None, None))
    out_specs = (
        P("gx", "gy", None, None),
        P("gx", "gy", None, None),
        P(None, "gy", None),
        P(None, "gy", None),
    )
    return jax.shard_map(body, mesh=mesh, in_specs=in_specs, out_specs=out_specs, check_vma=False)
```

```python
import math

import jax
import jax.numpy as jnp
from jax import lax
from jax.experimental import pallas as pl
from jax.experimental.pallas import tpu as pltpu
from jax.sharding import PartitionSpec as P

BF16 = jnp.bfloat16
F32 = jnp.float32
VMEM = pl.BlockSpec(memory_space=pltpu.VMEM)
HBM = pl.BlockSpec(memory_space=pltpu.HBM)
MIB = 1024 * 1024
BLOCK = 8


def call(kernel, out_shapes, args, spaces, scratch=(), flops=0, nbytes=0, vmem=16 * MIB, aliases=None):
    return pl.pallas_call(
        kernel,
        out_shape=out_shapes,
        in_specs=list(spaces) + [VMEM] * (len(args) - len(spaces)),
        out_specs=jax.tree.map(lambda _: VMEM, out_shapes),
        scratch_shapes=list(scratch),
        input_output_aliases=aliases or {},
        compiler_params=pltpu.CompilerParams(vmem_limit_bytes=vmem),
        cost_estimate=pl.CostEstimate(flops=flops, bytes_accessed=nbytes, transcendentals=0),
    )(*args)


def swap_pairs(count, odd):
    if not odd:
        return [(i, i ^ 1) for i in range(count)]
    ends = [(0, 0), (count - 1, count - 1)]
    inner = [(i, i + 1) for i in range(1, count - 1, 2)]
    return ends + inner + [(b, a) for a, b in inner]


def plane_mask(occ, block_x, size_y, size_z):
    row = lax.broadcasted_iota(jnp.int32, (size_y * size_z, 128), 0)
    block_y = row // (BLOCK * size_z)
    block_z = (row % size_z) // BLOCK
    mask = jnp.zeros((size_y * size_z, 128), F32)
    for i in range(size_y // BLOCK):
        for j in range(size_z // BLOCK):
            here = (block_y == i) & (block_z == j)
            mask = jnp.where(here, occ[block_x, i, j].astype(F32), mask)
    return mask


def pick(odd, if_even, if_odd):
    return jnp.where(odd == 0, if_even, if_odd)


def one_if(condition):
    return jnp.where(condition, 1.0, 0.0).astype(BF16)


def side_of(axis):
    index = lax.axis_index(axis)
    return index % 2, one_if(index > 0), one_if(index < lax.axis_size(axis) - 1)


def pack_sides(features, cotangent, occ, w):
    size_x, size_y, size_z, channels = features.shape
    rows = size_y * size_z

    def kernel(occ_hbm, first, second, w_hbm, mask, xa, xb, ya, yb, own, weights, occ_ref, sem, occ_sem, own_sem, w_sem):
        odd_x, odd_y = lax.axis_index("gx") % 2, lax.axis_index("gy") % 2
        first_x = pick(odd_x, size_x - 1, 0)
        first_y = pick(odd_y, size_y - 1, 0)
        sides = ((xa, first_x), (xb, size_x - 1 - first_x))
        columns = ((ya, first_y), (yb, size_y - 1 - first_y))
        occ_copy = pltpu.make_async_copy(occ_hbm, occ_ref, occ_sem)
        own_copy = pltpu.make_async_copy(first, own, own_sem)
        w_copy = pltpu.make_async_copy(w_hbm, weights, w_sem)
        copies = []
        for n, (out, x) in enumerate(sides):
            copies.append(pltpu.make_async_copy(second.at[x], out.at[1], sem.at[n]))
        for n, (out, y) in enumerate(columns):
            copies.append(pltpu.make_async_copy(second.at[:, y], out.at[1], sem.at[2 + n]))
        for copy in [occ_copy, own_copy, *copies, w_copy]:
            copy.start()
        occ_copy.wait()
        for n in range(size_x // BLOCK):
            mask[n] = plane_mask(occ_ref, n, size_y, size_z)
        own_copy.wait()
        for out, x in sides:
            out[0] = own[x] * mask[x // BLOCK].astype(BF16).reshape(size_y, size_z, channels)
        for out, y in columns:
            at = pl.ds(pl.multiple_of(y * size_z, size_z), size_z)
            for x in range(size_x):
                out[0, x] = own[x, y] * mask[x // BLOCK, at, :].astype(BF16)
        for copy in copies:
            copy.wait()
        for out, x in sides:
            out[1] = out[1] * mask[x // BLOCK].astype(BF16).reshape(size_y, size_z, channels)
        for out, y in columns:
            at = pl.ds(pl.multiple_of(y * size_z, size_z), size_z)
            for x in range(size_x):
                out[1, x] = out[1, x] * mask[x // BLOCK, at, :].astype(BF16)
        w_copy.wait()

    side = pltpu.VMEM((2, size_y, size_z, channels), BF16)
    column = pltpu.VMEM((2, size_x, size_z, channels), BF16)
    return call(
        kernel,
        (
            pltpu.VMEM((size_x // BLOCK, rows, channels), F32),
            side,
            side,
            column,
            column,
            pltpu.VMEM(features.shape, BF16),
            pltpu.VMEM(w.shape, BF16),
        ),
        [pltpu.with_memory_space_constraint(value, pltpu.HBM) for value in (occ, features, cotangent, w)],
        [HBM] * 4,
        scratch=[
            pltpu.SMEM(occ.shape, jnp.int32),
            pltpu.SemaphoreType.DMA((4,)),
            pltpu.SemaphoreType.DMA(()),
            pltpu.SemaphoreType.DMA(()),
            pltpu.SemaphoreType.DMA(()),
        ],
        nbytes=MIB,
        vmem=4 * MIB,
    )


def finish_columns(got_xa, got_xb, ya, yb):
    _, size_y, size_z, channels = got_xa.shape
    size_x = ya.shape[1]

    def kernel(xa, xb, ya, yb, out_a, out_b):
        odd, low_ok, high_ok = side_of("gx")
        first_y = pick(lax.axis_index("gy") % 2, size_y - 1, 0)
        for out, own, y in ((out_a, ya, first_y), (out_b, yb, size_y - 1 - first_y)):
            for f in range(2):
                out[f, 0] = pick(odd, xb[f, y], xa[f, y]) * low_ok
                out[f, size_x + 1] = pick(odd, xa[f, y], xb[f, y]) * high_ok
                out[f, 1 : size_x + 1] = own[f]

    shape = jax.ShapeDtypeStruct((2, size_x + 2, size_z, channels), BF16)
    return call(kernel, (shape, shape), (got_xa, got_xb, ya, yb), [], nbytes=MIB, vmem=4 * MIB)


def swap_sides(xa, xb):
    even, odd = (swap_pairs(lax.axis_size("gx"), which) for which in (False, True))
    return lax.ppermute(xa, "gx", even), lax.ppermute(xb, "gx", odd)


def swap_columns(ya, yb):
    even, odd = (swap_pairs(lax.axis_size("gy"), which) for which in (False, True))
    return lax.ppermute(ya, "gy", even), lax.ppermute(yb, "gy", odd)


def store_shifts(zc, x, ys, rows):
    size_z = zc.shape[2]
    count, lanes = rows.shape
    wide = rows.astype(F32)
    z = lax.broadcasted_iota(jnp.int32, (count, lanes), 0) % size_z
    below = jnp.where(z == 0, 0.0, pltpu.roll(wide, 1, 0)).astype(BF16)
    above = jnp.where(z == size_z - 1, 0.0, pltpu.roll(wide, count - 1, 0)).astype(BF16)
    shape = (count // size_z, size_z, lanes)
    for k, part in enumerate((below, rows, above)):
        zc[x, ys[0] : ys[1], :, k * lanes : (k + 1) * lanes] = part.reshape(shape)


def fill_own(zc, plane):
    size_x, size_y = zc.shape[0] - 2, zc.shape[1] - 2
    zc[0] = jnp.zeros(zc.shape[1:], BF16)
    zc[size_x + 1] = jnp.zeros(zc.shape[1:], BF16)
    for x in range(size_x):
        for y in (0, size_y + 1):
            zc[x + 1, y] = jnp.zeros(zc.shape[2:], BF16)
        store_shifts(zc, x + 1, (1, size_y + 1), plane(x))


def fill_sides(zc, f, xa, xb):
    size_x, size_y, size_z = zc.shape[0] - 2, zc.shape[1] - 2, zc.shape[2]
    rows = size_y * size_z
    odd, low_ok, high_ok = side_of("gx")
    channels = xa.shape[3]
    store_shifts(zc, 0, (1, size_y + 1), (pick(odd, xb[f], xa[f]) * low_ok).reshape(rows, channels))
    store_shifts(zc, size_x + 1, (1, size_y + 1), (pick(odd, xa[f], xb[f]) * high_ok).reshape(rows, channels))


def fill_columns(zc, f, ya, yb):
    size_x, size_y = zc.shape[0] - 2, zc.shape[1] - 2
    odd, low_ok, high_ok = side_of("gy")
    for x in range(size_x + 2):
        store_shifts(zc, x, (0, 1), pick(odd, yb[f, x], ya[f, x]) * low_ok)
        store_shifts(zc, x, (size_y + 1, size_y + 2), pick(odd, ya[f, x], yb[f, x]) * high_ok)


def straight(w):
    return lambda tap: w[tap]


def turned(w):
    return lambda tap: w[26 - tap].T


def lay_weights(taps, weight):
    channels = taps.shape[2] // 2
    zero = jnp.zeros((channels, channels), BF16)
    for j in range(3):
        for k in range(3):
            rows = slice(k * channels, (k + 1) * channels)
            for tap in range(3):
                value = weight(9 * tap + 3 * j + k)
                taps[3 * tap + j, rows, :channels] = value
                taps[3 * (tap + 1) + j, rows, channels:] = value
            taps[j, rows, channels:] = zero
            taps[9 + j, rows, :channels] = zero


def convolve(zc, taps, emit):
    size_x, size_y, size_z = zc.shape[0] - 2, zc.shape[1] - 2, zc.shape[2]
    depth = zc.shape[3]
    channels = depth // 3
    rows = size_y * size_z
    for x in range(0, size_x, 4):
        pieces = []
        for i in range(4):
            for j in range(3):
                halves = [zc[x + 2 * h + i, j : j + size_y].reshape(rows, depth) for h in range(2)]
                pieces.append(jnp.concatenate(halves, axis=0))
        both = jnp.dot(
            jnp.concatenate(pieces, axis=1),
            taps[...].reshape(12 * depth, 2 * channels),
            preferred_element_type=F32,
        )
        for h in range(2):
            for side in range(2):
                emit(x + 2 * h + side, both[h * rows : (h + 1) * rows, side * channels : (side + 1) * channels])


def add_halo_terms(total, zc, taps):
    size_x, size_y, size_z = zc.shape[0] - 2, zc.shape[1] - 2, zc.shape[2]
    depth = zc.shape[3]
    channels = depth // 3
    rows = size_y * size_z

    def weights(which):
        return jnp.concatenate([taps[n, :, :channels] for n in which], axis=0)

    for plane, x, first in ((0, 0, 0), (size_x + 1, size_x - 1, 6)):
        side = jnp.concatenate([zc[plane, j : j + size_y].reshape(rows, depth) for j in range(3)], axis=1)
        total[x] += jnp.dot(side, weights((first, first + 1, first + 2)), preferred_element_type=F32)
    none = jnp.zeros((size_z, depth), BF16)
    for column, y, j in ((0, 0, 0), (size_y + 1, size_y - 1, 2)):
        own = zc[1 : size_x + 1, column].reshape(size_x * size_z, depth)
        below = jnp.concatenate([none, own[:-size_z]], axis=0)
        above = jnp.concatenate([own[size_z:], none], axis=0)
        side = jnp.concatenate([below, own, above], axis=1)
        term = jnp.dot(side, weights((j, 3 + j, 6 + j)), preferred_element_type=F32)
        total[:, y * size_z : (y + 1) * size_z, :] += term.reshape(size_x, size_z, channels)


def field_shape(shape):
    size_x, size_y, size_z, channels = shape
    return (size_x + 2, size_y + 2, size_z, 3 * channels)


def taps_shape(channels):
    return (12, 3 * channels, 2 * channels)


def own_terms(mask, field, w, lay):
    size_x, size_y, size_z, channels = field.shape
    rows = size_y * size_z

    def kernel(mask, field, w, zc, taps, total):
        def plane(x):
            return field[x].reshape(rows, channels) * mask[x // BLOCK].astype(BF16)

        fill_own(zc, plane)
        lay_weights(taps, lay(w))

        def emit(x, value):
            total[x] = value

        convolve(zc, taps, emit)

    return call(
        kernel,
        (
            pltpu.VMEM(field_shape(field.shape), BF16),
            pltpu.VMEM(taps_shape(channels), BF16),
            pltpu.VMEM((size_x, rows, channels), F32),
        ),
        (mask, field, w),
        [],
        flops=2 * 27 * size_x * rows * channels * channels,
        nbytes=4 * MIB,
        vmem=14 * MIB,
    )


def copy_sides(f, value, xa, xb, ya, yb):
    size_x, size_y = value.shape[:2]
    first_x = pick(lax.axis_index("gx") % 2, size_x - 1, 0)
    first_y = pick(lax.axis_index("gy") % 2, size_y - 1, 0)
    xa[f], xb[f] = value[first_x], value[size_x - 1 - first_x]
    for x in range(size_x):
        ya[f, x], yb[f, x] = value[x, first_y], value[x, size_y - 1 - first_y]


def side_shapes(shape):
    size_x, size_y, size_z, channels = shape
    side = jax.ShapeDtypeStruct((2, size_y, size_z, channels), BF16)
    column = jax.ShapeDtypeStruct((2, size_x, size_z, channels), BF16)
    return (side, side, column, column)


def grad_terms(left, zc, start, store):
    size_x, size_y, size_z = zc.shape[0] - 2, zc.shape[1] - 2, zc.shape[2]
    depth = zc.shape[3]
    channels = depth // 3
    shifts = [(i, j) for i in range(3) for j in range(3)]
    for group in [shifts[n : n + 2] for n in range(0, 9, 2)]:
        pieces = []
        for i, j in group:
            a, b = start(i, j)
            pieces.append(zc[a : a + size_x, b : b + size_y].reshape(size_x * size_y * size_z, depth))
        out = jnp.dot(left, jnp.concatenate(pieces, axis=1), preferred_element_type=F32)
        for n, (i, j) in enumerate(group):
            for k in range(3):
                store(9 * i + 3 * j, k, out[:, (3 * n + k) * channels : (3 * n + k + 1) * channels])


def scatter_block(keep, send, d, block):
    count = 2 * keep.shape[0]
    share = keep.shape[2]
    index = lax.axis_index("gy")
    half, place = index % 2, index // 2
    for j in range(count // 2):
        even = block[2 * j * share : (2 * j + 1) * share]
        odd = block[(2 * j + 1) * share : (2 * j + 2) * share]
        at = jnp.bitwise_xor(place, j)
        keep[at, d] = pick(half, even, odd)
        send[at, d] = pick(half, odd, even)


def terms_shape(channels):
    count_y = lax.axis_size("gy")
    return jax.ShapeDtypeStruct((count_y // 2, 27, channels // count_y, channels), F32)


def hidden_and_terms(mask, halos, zm, zu, taps, pre, shape):
    size_x, size_y, size_z, channels = shape
    rows = size_y * size_z

    def kernel(mask, xa, xb, ya, yb, taps, pre, zm_in, zu_in, zm, zu, hidden, slope, keep, send):
        for f, zc in enumerate((zm, zu)):
            fill_sides(zc, f, xa, xb)
            fill_columns(zc, f, ya, yb)
        slope[...] = pre[...]
        add_halo_terms(slope, zm, taps)
        for x in range(size_x):
            here = mask[x // BLOCK]
            value = slope[x]
            s = jax.nn.sigmoid(value)
            hidden[x] = (here * (value * s)).astype(BF16).reshape(size_y, size_z, channels)
            slope[x] = here * (s * (1.0 + value * (1.0 - s)))
        left = hidden[...].reshape(size_x * rows, channels).T

        def store(d, k, block):
            scatter_block(keep, send, d + 2 - k, block)

        grad_terms(left, zu, lambda i, j: (2 - i, 2 - j), store)

    field = jax.ShapeDtypeStruct(shape, BF16)
    wide = jax.ShapeDtypeStruct(pre.shape, F32)
    shifted = jax.ShapeDtypeStruct(zm.shape, BF16)
    terms = terms_shape(channels)
    return call(
        kernel,
        (shifted, shifted, field, wide, terms, terms),
        (mask, *halos, taps, pre, zm, zu),
        [],
        flops=2 * 27 * size_x * rows * channels * channels,
        nbytes=8 * MIB,
        vmem=14 * MIB,
        aliases={7: 0, 8: 1},
    )


def pre_grad_and_terms(hidden, slope, zm, zu, taps, grad):
    size_x, rows, channels = grad.shape
    size_y, size_z = zu.shape[1] - 2, zu.shape[2]
    shape = (size_x, size_y, size_z, channels)

    def kernel(hidden, slope, zm, zu, taps, grad, pre_grad, keep, send, xa, xb, ya, yb, total):
        total[...] = grad[...]
        add_halo_terms(total, zu, taps)
        for x in range(size_x):
            pre_grad[x] = (total[x] * slope[x]).astype(BF16).reshape(size_y, size_z, channels)
        for f, value in enumerate((hidden, pre_grad)):
            copy_sides(f, value, xa, xb, ya, yb)
        left = pre_grad[...].reshape(size_x * rows, channels).T

        def store(d, k, block):
            scatter_block(keep, send, d + k, block.T)

        grad_terms(left, zm, lambda i, j: (i, j), store)

    terms = terms_shape(channels)
    return call(
        kernel,
        (jax.ShapeDtypeStruct(shape, BF16), terms, terms, *side_shapes(shape)),
        (hidden, slope, zm, zu, taps, grad),
        [],
        scratch=[pltpu.VMEM(grad.shape, F32)],
        flops=2 * 27 * size_x * rows * channels * channels,
        nbytes=8 * MIB,
        vmem=14 * MIB,
    )


def add_convolution(mask, own, field, f, halos, w, lay):
    size_x, size_y, size_z, channels = own.shape
    rows = size_y * size_z

    def kernel(mask, own, field, xa, xb, ya, yb, w, out, zc, taps):
        for x in range(size_x):
            store_shifts(zc, x + 1, (1, size_y + 1), field[x].reshape(rows, channels))
        fill_sides(zc, f, xa, xb)
        fill_columns(zc, f, ya, yb)
        lay_weights(taps, lay(w))

        def emit(x, term):
            near = own[x].reshape(rows, channels).astype(F32)
            out[x] = (mask[x // BLOCK] * (near + term)).astype(BF16).reshape(size_y, size_z, channels)

        convolve(zc, taps, emit)

    return call(
        kernel,
        jax.ShapeDtypeStruct(own.shape, BF16),
        (mask, own, field, *halos, w),
        [],
        scratch=[pltpu.VMEM(field_shape(own.shape), BF16), pltpu.VMEM(taps_shape(channels), BF16)],
        flops=2 * 27 * size_x * rows * channels * channels,
        nbytes=3 * MIB,
        vmem=14 * MIB,
    )


def after(values, *others):
    return lax.optimization_barrier((values, others))[0]


def swap(value, axis, bit, travel):
    pairs = [(i, i ^ bit) for i in range(lax.axis_size(axis))]
    return lax.ppermute(value.astype(travel), axis, pairs)


def first_sum(g, keep, came, earlier):
    places, taps, share, channels = keep.shape
    rows = taps * share

    def kernel(keep, came, *refs):
        stays, *leaves = refs[-places:]
        for p in range(places):
            value = (keep[p] + came[p]).reshape(rows, channels)
            if p == 0:
                stays[g] = value
            else:
                leaves[p - 1][g] = value.astype(BF16)

    stay = pltpu.VMEM((2, rows, channels), F32)
    leave = pltpu.VMEM((2, rows, channels), BF16)
    return call(
        kernel,
        (stay,) + (leave,) * (places - 1),
        (keep, came, *earlier),
        [],
        nbytes=2 * MIB,
        vmem=4 * MIB,
        aliases={2 + n: n for n in range(len(earlier))},
    )


def second_sum(stays, came):
    _, rows, channels = stays.shape

    def kernel(stays, *refs):
        came, (stay, leave) = refs[:-2], refs[-2:]
        odd = lax.axis_index("gx") % 2
        for out, g in ((stay, odd), (leave, 1 - odd)):
            value = stays[g]
            for ref in came:
                value += ref[g].astype(F32)
            out[...] = value

    shape = pltpu.VMEM((rows, channels), F32)
    return call(kernel, (shape, shape), (stays, *came), [], nbytes=2 * MIB, vmem=4 * MIB)


def body(features, w_first, w_second, occ, cotangent):
    count_x, count_y = lax.axis_size("gx"), lax.axis_size("gy")
    shape = features.shape
    mask, xa, xb, ya, yb, own, weights = pack_sides(features, cotangent, occ, w_first)
    xa, xb = swap_sides(xa, xb)
    zm, first_taps, pre = own_terms(mask, own, weights, straight)
    xa, xb = after((xa, xb), pre)
    ya, yb = finish_columns(xa, xb, ya, yb)
    behind = after(mask, ya)
    ya, yb = swap_columns(ya, yb)
    zu, second_taps, grad = own_terms(behind, cotangent, w_second, turned)
    halos = after((xa, xb, ya, yb), grad)
    zm, zu, hidden, slope, keep_second, send = hidden_and_terms(mask, halos, zm, zu, first_taps, pre, shape)
    came = swap(send, "gy", 1, F32)
    pre_grad, keep_first, send, xa, xb, ya, yb = pre_grad_and_terms(hidden, slope, zm, zu, second_taps, grad)

    sums = first_sum(0, keep_second, after(came, pre_grad), ())
    came = swap(send, "gy", 1, F32)
    xa, xb = swap_sides(xa, xb)
    stays, *leaves = first_sum(1, keep_first, after(came, sums[0]), sums)
    came = [swap(value, "gy", 2 * (p + 1), BF16) for p, value in enumerate(leaves)]
    stays, leaves = second_sum(stays, after(came, xa, xb))
    xa, xb = after((xa, xb), leaves)
    came = swap(leaves, "gx", 1, F32)
    ya, yb = finish_columns(xa, xb, ya, yb)
    came = after(came, ya)
    ya, yb = swap_columns(ya, yb)
    stays = stays + came
    convolutions = [
        (mask, features, hidden, 0, w_second, straight),
        (mask, cotangent, pre_grad, 1, w_first, turned),
    ]
    results = []

    def convolve_beside(came, behind):
        if len(results) == len(convolutions):
            return came
        mask, own, field, f, w, lay = convolutions[len(results)]
        halos = after((xa, xb, ya, yb), behind)
        results.append(add_convolution(mask, own, field, f, halos, w, lay))
        return after(came, results[-1])

    bit = 2
    while bit < count_x:
        own = stays.astype(BF16)
        came = convolve_beside(swap(own, "gx", bit, BF16), own)
        stays = own.astype(F32) + came.astype(F32)
        bit *= 2
    came = convolve_beside(swap(stays, "gx", 1, F32), stays)
    output, grad_features = results
    odd = lax.axis_index("gx") % 2 == 1
    factor = 1.0 / math.sqrt(count_x * count_y * shape[0] * shape[1] * shape[2])
    total_second = jnp.where(odd, came, stays) * factor
    total_first = jnp.where(odd, stays, came) * factor
    kernel_shape = (27, -1, shape[3])
    return output, grad_features, total_first.reshape(kernel_shape), total_second.reshape(kernel_shape)


def solution(mesh):
    in_specs = (P("gx", "gy", None, None), P(), P(), P("gx", "gy", None), P("gx", "gy", None, None))
    out_specs = (
        P("gx", "gy", None, None),
        P("gx", "gy", None, None),
        P(None, "gy", None),
        P(None, "gy", None),
    )
    return jax.shard_map(body, mesh=mesh, in_specs=in_specs, out_specs=out_specs, check_vma=False)
```

```python
import math

import jax
import jax.numpy as jnp
from jax import lax
from jax.experimental import pallas as pl
from jax.experimental.pallas import tpu as pltpu
from jax.sharding import PartitionSpec as P

BF16 = jnp.bfloat16
F32 = jnp.float32
VMEM = pl.BlockSpec(memory_space=pltpu.VMEM)
HBM = pl.BlockSpec(memory_space=pltpu.HBM)
MIB = 1024 * 1024
BLOCK = 8


def call(kernel, out_shapes, args, spaces, scratch=(), flops=0, nbytes=0, vmem=16 * MIB, aliases=None):
    return pl.pallas_call(
        kernel,
        out_shape=out_shapes,
        in_specs=list(spaces) + [VMEM] * (len(args) - len(spaces)),
        out_specs=jax.tree.map(lambda _: VMEM, out_shapes),
        scratch_shapes=list(scratch),
        input_output_aliases=aliases or {},
        compiler_params=pltpu.CompilerParams(vmem_limit_bytes=vmem),
        cost_estimate=pl.CostEstimate(flops=flops, bytes_accessed=nbytes, transcendentals=0),
    )(*args)


def swap_pairs(axis, odd):
    count_x, count_y = lax.axis_size("gx"), lax.axis_size("gy")
    pairs = []
    for x in range(count_x):
        for y in range(count_y):
            at, count = (x, count_x) if axis == "gx" else (y, count_y)
            to = at - 1 if (at % 2 == 0) == odd else at + 1
            if not 0 <= to < count:
                other = (x, y ^ 1) if axis == "gx" else (x ^ 1, y)
            else:
                other = (to, y) if axis == "gx" else (x, to)
            pairs.append((x * count_y + y, other[0] * count_y + other[1]))
    return pairs


def plane_mask(occ, block_x, size_y, size_z):
    row = lax.broadcasted_iota(jnp.int32, (size_y * size_z, 128), 0)
    block_y = row // (BLOCK * size_z)
    block_z = (row % size_z) // BLOCK
    mask = jnp.zeros((size_y * size_z, 128), F32)
    for i in range(size_y // BLOCK):
        for j in range(size_z // BLOCK):
            here = (block_y == i) & (block_z == j)
            mask = jnp.where(here, occ[block_x, i, j].astype(F32), mask)
    return mask


def pick(odd, if_even, if_odd):
    return jnp.where(odd == 0, if_even, if_odd)


def one_if(condition):
    return jnp.where(condition, 1.0, 0.0).astype(BF16)


def side_of(axis):
    index = lax.axis_index(axis)
    return index % 2, one_if(index > 0), one_if(index < lax.axis_size(axis) - 1)


def pack_sides(features, cotangent, occ, w):
    size_x, size_y, size_z, channels = features.shape
    rows = size_y * size_z

    def kernel(occ_hbm, first, second, w_hbm, mask, xa, xb, ya, yb, own, weights, occ_ref, sem, occ_sem, own_sem, w_sem):
        odd_x, odd_y = lax.axis_index("gx") % 2, lax.axis_index("gy") % 2
        first_x = pick(odd_x, size_x - 1, 0)
        first_y = pick(odd_y, size_y - 1, 0)
        sides = ((xa, first_x), (xb, size_x - 1 - first_x))
        columns = ((ya, first_y), (yb, size_y - 1 - first_y))
        occ_copy = pltpu.make_async_copy(occ_hbm, occ_ref, occ_sem)
        own_copy = pltpu.make_async_copy(first, own, own_sem)
        w_copy = pltpu.make_async_copy(w_hbm, weights, w_sem)
        copies = []
        for n, (out, x) in enumerate(sides):
            copies.append(pltpu.make_async_copy(second.at[x], out.at[1], sem.at[n]))
        for n, (out, y) in enumerate(columns):
            copies.append(pltpu.make_async_copy(second.at[:, y], out.at[1], sem.at[2 + n]))
        for copy in [occ_copy, own_copy, *copies, w_copy]:
            copy.start()
        occ_copy.wait()
        for n in range(size_x // BLOCK):
            mask[n] = plane_mask(occ_ref, n, size_y, size_z)
        own_copy.wait()
        for out, x in sides:
            out[0] = own[x] * mask[x // BLOCK].astype(BF16).reshape(size_y, size_z, channels)
        for out, y in columns:
            at = pl.ds(pl.multiple_of(y * size_z, size_z), size_z)
            for x in range(size_x):
                out[0, x] = own[x, y] * mask[x // BLOCK, at, :].astype(BF16)
        for copy in copies:
            copy.wait()
        for out, x in sides:
            out[1] = out[1] * mask[x // BLOCK].astype(BF16).reshape(size_y, size_z, channels)
        for out, y in columns:
            at = pl.ds(pl.multiple_of(y * size_z, size_z), size_z)
            for x in range(size_x):
                out[1, x] = out[1, x] * mask[x // BLOCK, at, :].astype(BF16)
        w_copy.wait()

    side = pltpu.VMEM((2, size_y, size_z, channels), BF16)
    column = pltpu.VMEM((2, size_x, size_z, channels), BF16)
    return call(
        kernel,
        (
            pltpu.VMEM((size_x // BLOCK, rows, channels), F32),
            side,
            side,
            column,
            column,
            pltpu.VMEM(features.shape, BF16),
            pltpu.VMEM(w.shape, BF16),
        ),
        [pltpu.with_memory_space_constraint(value, pltpu.HBM) for value in (occ, features, cotangent, w)],
        [HBM] * 4,
        scratch=[
            pltpu.SMEM(occ.shape, jnp.int32),
            pltpu.SemaphoreType.DMA((4,)),
            pltpu.SemaphoreType.DMA(()),
            pltpu.SemaphoreType.DMA(()),
            pltpu.SemaphoreType.DMA(()),
        ],
        nbytes=MIB,
        vmem=4 * MIB,
    )


def finish_columns(got_xa, got_xb, ya, yb):
    _, size_y, size_z, channels = got_xa.shape
    size_x = ya.shape[1]

    def kernel(xa, xb, ya, yb, out_a, out_b):
        odd, low_ok, high_ok = side_of("gx")
        first_y = pick(lax.axis_index("gy") % 2, size_y - 1, 0)
        for out, own, y in ((out_a, ya, first_y), (out_b, yb, size_y - 1 - first_y)):
            for f in range(2):
                out[f, 0] = pick(odd, xb[f, y], xa[f, y]) * low_ok
                out[f, size_x + 1] = pick(odd, xa[f, y], xb[f, y]) * high_ok
                out[f, 1 : size_x + 1] = own[f]

    shape = jax.ShapeDtypeStruct((2, size_x + 2, size_z, channels), BF16)
    return call(kernel, (shape, shape), (got_xa, got_xb, ya, yb), [], nbytes=MIB, vmem=4 * MIB)


def swap_neighbours(axis, first, second):
    return tuple(
        lax.ppermute(value, ("gx", "gy"), swap_pairs(axis, odd)) for value, odd in ((first, False), (second, True))
    )


def store_shifts(zc, x, ys, rows):
    size_z = zc.shape[2]
    count, lanes = rows.shape
    wide = rows.astype(F32)
    z = lax.broadcasted_iota(jnp.int32, (count, lanes), 0) % size_z
    below = jnp.where(z == 0, 0.0, pltpu.roll(wide, 1, 0)).astype(BF16)
    above = jnp.where(z == size_z - 1, 0.0, pltpu.roll(wide, count - 1, 0)).astype(BF16)
    shape = (count // size_z, size_z, lanes)
    for k, part in enumerate((below, rows, above)):
        zc[x, ys[0] : ys[1], :, k * lanes : (k + 1) * lanes] = part.reshape(shape)


def fill_own(zc, plane):
    size_x, size_y = zc.shape[0] - 2, zc.shape[1] - 2
    zc[0] = jnp.zeros(zc.shape[1:], BF16)
    zc[size_x + 1] = jnp.zeros(zc.shape[1:], BF16)
    for x in range(size_x):
        for y in (0, size_y + 1):
            zc[x + 1, y] = jnp.zeros(zc.shape[2:], BF16)
        store_shifts(zc, x + 1, (1, size_y + 1), plane(x))


def fill_sides(zc, f, xa, xb):
    size_x, size_y, size_z = zc.shape[0] - 2, zc.shape[1] - 2, zc.shape[2]
    rows = size_y * size_z
    odd, low_ok, high_ok = side_of("gx")
    channels = xa.shape[3]
    store_shifts(zc, 0, (1, size_y + 1), (pick(odd, xb[f], xa[f]) * low_ok).reshape(rows, channels))
    store_shifts(zc, size_x + 1, (1, size_y + 1), (pick(odd, xa[f], xb[f]) * high_ok).reshape(rows, channels))


def fill_columns(zc, f, ya, yb):
    size_x, size_y = zc.shape[0] - 2, zc.shape[1] - 2
    odd, low_ok, high_ok = side_of("gy")
    for x in range(size_x + 2):
        store_shifts(zc, x, (0, 1), pick(odd, yb[f, x], ya[f, x]) * low_ok)
        store_shifts(zc, x, (size_y + 1, size_y + 2), pick(odd, ya[f, x], yb[f, x]) * high_ok)


def straight(w):
    return lambda tap: w[tap]


def turned(w):
    return lambda tap: w[26 - tap].T


def lay_weights(taps, weight):
    channels = taps.shape[2] // 2
    zero = jnp.zeros((channels, channels), BF16)
    for j in range(3):
        for k in range(3):
            rows = slice(k * channels, (k + 1) * channels)
            for tap in range(3):
                value = weight(9 * tap + 3 * j + k)
                taps[3 * tap + j, rows, :channels] = value
                taps[3 * (tap + 1) + j, rows, channels:] = value
            taps[j, rows, channels:] = zero
            taps[9 + j, rows, :channels] = zero


def convolve(zc, taps, emit):
    size_x, size_y, size_z = zc.shape[0] - 2, zc.shape[1] - 2, zc.shape[2]
    depth = zc.shape[3]
    channels = depth // 3
    rows = size_y * size_z
    for x in range(0, size_x, 4):
        pieces = []
        for i in range(4):
            for j in range(3):
                halves = [zc[x + 2 * h + i, j : j + size_y].reshape(rows, depth) for h in range(2)]
                pieces.append(jnp.concatenate(halves, axis=0))
        both = jnp.dot(
            jnp.concatenate(pieces, axis=1),
            taps[...].reshape(12 * depth, 2 * channels),
            preferred_element_type=F32,
        )
        for h in range(2):
            for side in range(2):
                emit(x + 2 * h + side, both[h * rows : (h + 1) * rows, side * channels : (side + 1) * channels])


def add_halo_terms(total, zc, taps):
    size_x, size_y, size_z = zc.shape[0] - 2, zc.shape[1] - 2, zc.shape[2]
    depth = zc.shape[3]
    channels = depth // 3
    rows = size_y * size_z

    def weights(which):
        return jnp.concatenate([taps[n, :, :channels] for n in which], axis=0)

    for plane, x, first in ((0, 0, 0), (size_x + 1, size_x - 1, 6)):
        side = jnp.concatenate([zc[plane, j : j + size_y].reshape(rows, depth) for j in range(3)], axis=1)
        total[x] += jnp.dot(side, weights((first, first + 1, first + 2)), preferred_element_type=F32)
    none = jnp.zeros((size_z, depth), BF16)
    for column, y, j in ((0, 0, 0), (size_y + 1, size_y - 1, 2)):
        own = zc[1 : size_x + 1, column].reshape(size_x * size_z, depth)
        below = jnp.concatenate([none, own[:-size_z]], axis=0)
        above = jnp.concatenate([own[size_z:], none], axis=0)
        side = jnp.concatenate([below, own, above], axis=1)
        term = jnp.dot(side, weights((j, 3 + j, 6 + j)), preferred_element_type=F32)
        total[:, y * size_z : (y + 1) * size_z, :] += term.reshape(size_x, size_z, channels)


def field_shape(shape):
    size_x, size_y, size_z, channels = shape
    return (size_x + 2, size_y + 2, size_z, 3 * channels)


def taps_shape(channels):
    return (12, 3 * channels, 2 * channels)


def own_terms(mask, field, w, lay):
    size_x, size_y, size_z, channels = field.shape
    rows = size_y * size_z

    def kernel(mask, field, w, zc, taps, total):
        def plane(x):
            return field[x].reshape(rows, channels) * mask[x // BLOCK].astype(BF16)

        fill_own(zc, plane)
        lay_weights(taps, lay(w))

        def emit(x, value):
            total[x] = value

        convolve(zc, taps, emit)

    return call(
        kernel,
        (
            pltpu.VMEM(field_shape(field.shape), BF16),
            pltpu.VMEM(taps_shape(channels), BF16),
            pltpu.VMEM((size_x, rows, channels), F32),
        ),
        (mask, field, w),
        [],
        flops=2 * 27 * size_x * rows * channels * channels,
        nbytes=4 * MIB,
        vmem=14 * MIB,
    )


def copy_sides(f, value, xa, xb, ya, yb):
    size_x, size_y = value.shape[:2]
    first_x = pick(lax.axis_index("gx") % 2, size_x - 1, 0)
    first_y = pick(lax.axis_index("gy") % 2, size_y - 1, 0)
    xa[f], xb[f] = value[first_x], value[size_x - 1 - first_x]
    for x in range(size_x):
        ya[f, x], yb[f, x] = value[x, first_y], value[x, size_y - 1 - first_y]


def side_shapes(shape):
    size_x, size_y, size_z, channels = shape
    side = jax.ShapeDtypeStruct((2, size_y, size_z, channels), BF16)
    column = jax.ShapeDtypeStruct((2, size_x, size_z, channels), BF16)
    return (side, side, column, column)


def grad_terms(left, zc, start, store):
    size_x, size_y, size_z = zc.shape[0] - 2, zc.shape[1] - 2, zc.shape[2]
    depth = zc.shape[3]
    channels = depth // 3
    shifts = [(i, j) for i in range(3) for j in range(3)]
    for group in [shifts[n : n + 2] for n in range(0, 9, 2)]:
        pieces = []
        for i, j in group:
            a, b = start(i, j)
            pieces.append(zc[a : a + size_x, b : b + size_y].reshape(size_x * size_y * size_z, depth))
        out = jnp.dot(left, jnp.concatenate(pieces, axis=1), preferred_element_type=F32)
        for n, (i, j) in enumerate(group):
            for k in range(3):
                store(9 * i + 3 * j, k, out[:, (3 * n + k) * channels : (3 * n + k + 1) * channels])


def scatter_block(keep, send, d, block):
    count = 2 * keep.shape[0]
    share = keep.shape[2]
    index = lax.axis_index("gy")
    half, place = index % 2, index // 2
    for j in range(count // 2):
        even = block[2 * j * share : (2 * j + 1) * share]
        odd = block[(2 * j + 1) * share : (2 * j + 2) * share]
        at = jnp.bitwise_xor(place, j)
        keep[at, d] = pick(half, even, odd)
        send[at, d] = pick(half, odd, even)


def terms_shape(channels):
    count_y = lax.axis_size("gy")
    return jax.ShapeDtypeStruct((count_y // 2, 27, channels // count_y, channels), F32)


def hidden_and_terms(mask, halos, zm, zu, taps, pre, shape):
    size_x, size_y, size_z, channels = shape
    rows = size_y * size_z

    def kernel(mask, xa, xb, ya, yb, taps, pre, zm_in, zu_in, zm, zu, hidden, slope, keep, send):
        for f, zc in enumerate((zm, zu)):
            fill_sides(zc, f, xa, xb)
            fill_columns(zc, f, ya, yb)
        slope[...] = pre[...]
        add_halo_terms(slope, zm, taps)
        for x in range(size_x):
            here = mask[x // BLOCK]
            value = slope[x]
            s = jax.nn.sigmoid(value)
            hidden[x] = (here * (value * s)).astype(BF16).reshape(size_y, size_z, channels)
            slope[x] = here * (s * (1.0 + value * (1.0 - s)))
        left = hidden[...].reshape(size_x * rows, channels).T

        def store(d, k, block):
            scatter_block(keep, send, d + 2 - k, block)

        grad_terms(left, zu, lambda i, j: (2 - i, 2 - j), store)

    field = jax.ShapeDtypeStruct(shape, BF16)
    wide = jax.ShapeDtypeStruct(pre.shape, F32)
    shifted = jax.ShapeDtypeStruct(zm.shape, BF16)
    terms = terms_shape(channels)
    return call(
        kernel,
        (shifted, shifted, field, wide, terms, terms),
        (mask, *halos, taps, pre, zm, zu),
        [],
        flops=2 * 27 * size_x * rows * channels * channels,
        nbytes=8 * MIB,
        vmem=14 * MIB,
        aliases={7: 0, 8: 1},
    )


def pre_grad_and_terms(hidden, slope, zm, zu, taps, grad):
    size_x, rows, channels = grad.shape
    size_y, size_z = zu.shape[1] - 2, zu.shape[2]
    shape = (size_x, size_y, size_z, channels)

    def kernel(hidden, slope, zm, zu, taps, grad, pre_grad, keep, send, xa, xb, ya, yb, total):
        total[...] = grad[...]
        add_halo_terms(total, zu, taps)
        for x in range(size_x):
            pre_grad[x] = (total[x] * slope[x]).astype(BF16).reshape(size_y, size_z, channels)
        for f, value in enumerate((hidden, pre_grad)):
            copy_sides(f, value, xa, xb, ya, yb)
        left = pre_grad[...].reshape(size_x * rows, channels).T

        def store(d, k, block):
            scatter_block(keep, send, d + k, block.T)

        grad_terms(left, zm, lambda i, j: (i, j), store)

    terms = terms_shape(channels)
    return call(
        kernel,
        (jax.ShapeDtypeStruct(shape, BF16), terms, terms, *side_shapes(shape)),
        (hidden, slope, zm, zu, taps, grad),
        [],
        scratch=[pltpu.VMEM(grad.shape, F32)],
        flops=2 * 27 * size_x * rows * channels * channels,
        nbytes=8 * MIB,
        vmem=14 * MIB,
    )


def add_convolution(mask, own, field, f, halos, w, lay):
    size_x, size_y, size_z, channels = own.shape
    rows = size_y * size_z

    def kernel(mask, own, field, xa, xb, ya, yb, w, out, zc, taps):
        for x in range(size_x):
            store_shifts(zc, x + 1, (1, size_y + 1), field[x].reshape(rows, channels))
        fill_sides(zc, f, xa, xb)
        fill_columns(zc, f, ya, yb)
        lay_weights(taps, lay(w))

        def emit(x, term):
            near = own[x].reshape(rows, channels).astype(F32)
            out[x] = (mask[x // BLOCK] * (near + term)).astype(BF16).reshape(size_y, size_z, channels)

        convolve(zc, taps, emit)

    return call(
        kernel,
        jax.ShapeDtypeStruct(own.shape, BF16),
        (mask, own, field, *halos, w),
        [],
        scratch=[pltpu.VMEM(field_shape(own.shape), BF16), pltpu.VMEM(taps_shape(channels), BF16)],
        flops=2 * 27 * size_x * rows * channels * channels,
        nbytes=3 * MIB,
        vmem=14 * MIB,
    )


def after(values, *others):
    return lax.optimization_barrier((values, others))[0]


def swap(value, axis, bit):
    return lax.ppermute(value, axis, [(i, i ^ bit) for i in range(lax.axis_size(axis))])


def first_sum(g, keep, came, earlier):
    places, taps, share, channels = keep.shape
    rows = taps * share

    def kernel(keep, came, *refs):
        stays, *leaves = refs[-places:]
        for p in range(places):
            value = (keep[p] + came[p]).reshape(rows, channels)
            if p == 0:
                stays[g] = value
            else:
                leaves[p - 1][g] = value.astype(BF16)

    stay = pltpu.VMEM((2, rows, channels), F32)
    leave = pltpu.VMEM((2, rows, channels), BF16)
    return call(
        kernel,
        (stay,) + (leave,) * (places - 1),
        (keep, came, *earlier),
        [],
        nbytes=2 * MIB,
        vmem=4 * MIB,
        aliases={2 + n: n for n in range(len(earlier))},
    )


CODE_ROWS = 16
CODE_TOP = 32000.0


def encode(value, out):
    most = jnp.max(jnp.max(jnp.abs(value), axis=0, keepdims=True), axis=1, keepdims=True)
    power = jnp.ceil(jnp.log2(jnp.clip(most, 2.0**-100, 2.0**100)))
    power = jnp.broadcast_to(power, (1, value.shape[1]))
    head = jnp.broadcast_to(power, (CODE_ROWS, value.shape[1]))
    out[:CODE_ROWS] = head.astype(jnp.int32).astype(jnp.int16)
    scaled = value * (CODE_TOP * jnp.exp2(-power))
    out[CODE_ROWS:] = jnp.round(scaled).astype(jnp.int32).astype(jnp.int16)


def decode(ref):
    power = ref[:CODE_ROWS].astype(jnp.int32).astype(F32)[:1]
    return ref[CODE_ROWS:].astype(jnp.int32).astype(F32) * (jnp.exp2(power) * (1.0 / CODE_TOP))


def coded_shape(rows, channels):
    return pltpu.VMEM((CODE_ROWS + rows, channels), jnp.int16)


def second_sums(stays, came):
    _, rows, channels = stays.shape

    def kernel(stays, *refs):
        came, (stay, leave) = refs[:-2], refs[-2:]
        odd = lax.axis_index("gx") % 2

        def total(g):
            value = stays[g]
            for ref in came:
                value += ref[g].astype(F32)
            return value

        stay[...] = total(odd)
        encode(total(1 - odd), leave)

    outs = (pltpu.VMEM((rows, channels), F32), coded_shape(rows, channels))
    return call(kernel, outs, (stays, *came), [], nbytes=2 * MIB, vmem=4 * MIB)


def next_sum(own, came):
    rows, channels = came.shape[0] - CODE_ROWS, came.shape[1]
    coded = own.dtype != F32

    def kernel(own, came, out):
        encode((decode(own) if coded else own[...]) + decode(came), out)

    return call(kernel, coded_shape(rows, channels), (own, came), [], nbytes=MIB, vmem=4 * MIB)


def final_grads(own, came, taps, factor):
    rows, channels = came.shape[0] - CODE_ROWS, came.shape[1]

    def kernel(own, came, second, first):
        odd = lax.axis_index("gx") % 2
        mine, other = decode(own) * factor, decode(came) * factor
        second[...] = pick(odd, mine, other).reshape(second.shape)
        first[...] = pick(odd, other, mine).reshape(first.shape)

    shape = jax.ShapeDtypeStruct((taps, rows // taps, channels), F32)
    return call(kernel, (shape, shape), (own, came), [], nbytes=MIB, vmem=4 * MIB)


def body(features, w_first, w_second, occ, cotangent):
    count_x, count_y = lax.axis_size("gx"), lax.axis_size("gy")
    shape = features.shape
    mask, xa, xb, ya, yb, own, weights = pack_sides(features, cotangent, occ, w_first)
    xa, xb = swap_neighbours("gx", xa, xb)
    zm, first_taps, pre = own_terms(mask, own, weights, straight)
    xa, xb = after((xa, xb), pre)
    ya, yb = finish_columns(xa, xb, ya, yb)
    behind = after(mask, ya)
    ya, yb = swap_neighbours("gy", ya, yb)
    zu, second_taps, grad = own_terms(behind, cotangent, w_second, turned)
    halos = after((xa, xb, ya, yb), grad)
    zm, zu, hidden, slope, keep_second, send = hidden_and_terms(mask, halos, zm, zu, first_taps, pre, shape)
    came = swap(send, "gy", 1)
    pre_grad, keep_first, send, xa, xb, ya, yb = pre_grad_and_terms(hidden, slope, zm, zu, second_taps, grad)

    sums = first_sum(0, keep_second, after(came, pre_grad), ())
    came = swap(send, "gy", 1)
    xa, xb = swap_neighbours("gx", xa, xb)
    stays, *leaves = first_sum(1, keep_first, after(came, sums[0]), sums)
    came = [swap(value, "gy", 2 * (p + 1)) for p, value in enumerate(leaves)]
    stays, leaves = second_sums(stays, after(came, xa, xb))
    xa, xb = after((xa, xb), leaves)
    came = swap(leaves, "gx", 1)
    ya, yb = finish_columns(xa, xb, ya, yb)
    came = after(came, ya)
    ya, yb = swap_neighbours("gy", ya, yb)
    stays = next_sum(stays, came)
    convolutions = [
        (mask, features, hidden, 0, w_second, straight),
        (mask, cotangent, pre_grad, 1, w_first, turned),
    ]
    results = []

    def convolve_beside(came, behind):
        if len(results) == len(convolutions):
            return came
        mask, own, field, f, w, lay = convolutions[len(results)]
        halos = after((xa, xb, ya, yb), behind)
        results.append(add_convolution(mask, own, field, f, halos, w, lay))
        return after(came, results[-1])

    bit = 2
    while bit < count_x:
        stays = next_sum(stays, convolve_beside(swap(stays, "gx", bit), stays))
        bit *= 2
    came = convolve_beside(swap(stays, "gx", 1), stays)
    factor = 1.0 / math.sqrt(count_x * count_y * shape[0] * shape[1] * shape[2])
    grad_second, grad_first = final_grads(stays, came, w_first.shape[0], factor)
    output, grad_features = results
    return output, grad_features, grad_first, grad_second


def solution(mesh):
    in_specs = (P("gx", "gy", None, None), P(), P(), P("gx", "gy", None), P("gx", "gy", None, None))
    out_specs = (
        P("gx", "gy", None, None),
        P("gx", "gy", None, None),
        P(None, "gy", None),
        P(None, "gy", None),
    )
    return jax.shard_map(body, mesh=mesh, in_specs=in_specs, out_specs=out_specs, check_vma=False)
```

```python
import math

import jax
import jax.numpy as jnp
from jax import lax
from jax.experimental import pallas as pl
from jax.experimental.pallas import tpu as pltpu
from jax.sharding import PartitionSpec as P

BF16 = jnp.bfloat16
F32 = jnp.float32
VMEM = pl.BlockSpec(memory_space=pltpu.VMEM)
HBM = pl.BlockSpec(memory_space=pltpu.HBM)
MIB = 1024 * 1024
BLOCK = 8


def call(kernel, out_shapes, args, spaces, scratch=(), flops=0, nbytes=0, vmem=16 * MIB, aliases=None):
    return pl.pallas_call(
        kernel,
        out_shape=out_shapes,
        in_specs=list(spaces) + [VMEM] * (len(args) - len(spaces)),
        out_specs=jax.tree.map(lambda _: VMEM, out_shapes),
        scratch_shapes=list(scratch),
        input_output_aliases=aliases or {},
        compiler_params=pltpu.CompilerParams(vmem_limit_bytes=vmem),
        cost_estimate=pl.CostEstimate(flops=flops, bytes_accessed=nbytes, transcendentals=0),
    )(*args)


def swap_pairs(axis, odd):
    count_x, count_y = lax.axis_size("gx"), lax.axis_size("gy")
    pairs = []
    for x in range(count_x):
        for y in range(count_y):
            at, count = (x, count_x) if axis == "gx" else (y, count_y)
            to = at - 1 if (at % 2 == 0) == odd else at + 1
            if not 0 <= to < count:
                other = (x, y ^ 1) if axis == "gx" else (x ^ 1, y)
            else:
                other = (to, y) if axis == "gx" else (x, to)
            pairs.append((x * count_y + y, other[0] * count_y + other[1]))
    return pairs


def plane_mask(occ, block_x, size_y, size_z):
    row = lax.broadcasted_iota(jnp.int32, (size_y * size_z, 128), 0)
    block_y = row // (BLOCK * size_z)
    block_z = (row % size_z) // BLOCK
    mask = jnp.zeros((size_y * size_z, 128), F32)
    for i in range(size_y // BLOCK):
        for j in range(size_z // BLOCK):
            here = (block_y == i) & (block_z == j)
            mask = jnp.where(here, occ[block_x, i, j].astype(F32), mask)
    return mask


def pick(odd, if_even, if_odd):
    return jnp.where(odd == 0, if_even, if_odd)


def one_if(condition):
    return jnp.where(condition, 1.0, 0.0).astype(BF16)


def side_of(axis):
    index = lax.axis_index(axis)
    return index % 2, one_if(index > 0), one_if(index < lax.axis_size(axis) - 1)


def pack_sides(features, cotangent, occ, w):
    size_x, size_y, size_z, channels = features.shape
    rows = size_y * size_z

    def kernel(occ_hbm, first, second, w_hbm, mask, xa, xb, ya, yb, own, weights, occ_ref, sem, occ_sem, own_sem, w_sem):
        odd_x, odd_y = lax.axis_index("gx") % 2, lax.axis_index("gy") % 2
        first_x = pick(odd_x, size_x - 1, 0)
        first_y = pick(odd_y, size_y - 1, 0)
        sides = ((xa, first_x), (xb, size_x - 1 - first_x))
        columns = ((ya, first_y), (yb, size_y - 1 - first_y))
        occ_copy = pltpu.make_async_copy(occ_hbm, occ_ref, occ_sem)
        own_copy = pltpu.make_async_copy(first, own, own_sem)
        w_copy = pltpu.make_async_copy(w_hbm, weights, w_sem)
        copies = []
        for n, (out, x) in enumerate(sides):
            copies.append(pltpu.make_async_copy(second.at[x], out.at[1], sem.at[n]))
        for n, (out, y) in enumerate(columns):
            copies.append(pltpu.make_async_copy(second.at[:, y], out.at[1], sem.at[2 + n]))
        for copy in [occ_copy, own_copy, *copies, w_copy]:
            copy.start()
        occ_copy.wait()
        for n in range(size_x // BLOCK):
            mask[n] = plane_mask(occ_ref, n, size_y, size_z)
        own_copy.wait()
        for out, x in sides:
            out[0] = own[x] * mask[x // BLOCK].astype(BF16).reshape(size_y, size_z, channels)
        for out, y in columns:
            at = pl.ds(pl.multiple_of(y * size_z, size_z), size_z)
            for x in range(size_x):
                out[0, x] = own[x, y] * mask[x // BLOCK, at, :].astype(BF16)
        for copy in copies:
            copy.wait()
        for out, x in sides:
            out[1] = out[1] * mask[x // BLOCK].astype(BF16).reshape(size_y, size_z, channels)
        for out, y in columns:
            at = pl.ds(pl.multiple_of(y * size_z, size_z), size_z)
            for x in range(size_x):
                out[1, x] = out[1, x] * mask[x // BLOCK, at, :].astype(BF16)
        w_copy.wait()

    side = pltpu.VMEM((2, size_y, size_z, channels), BF16)
    column = pltpu.VMEM((2, size_x, size_z, channels), BF16)
    return call(
        kernel,
        (
            pltpu.VMEM((size_x // BLOCK, rows, channels), F32),
            side,
            side,
            column,
            column,
            pltpu.VMEM(features.shape, BF16),
            pltpu.VMEM(w.shape, BF16),
        ),
        [pltpu.with_memory_space_constraint(value, pltpu.HBM) for value in (occ, features, cotangent, w)],
        [HBM] * 4,
        scratch=[
            pltpu.SMEM(occ.shape, jnp.int32),
            pltpu.SemaphoreType.DMA((4,)),
            pltpu.SemaphoreType.DMA(()),
            pltpu.SemaphoreType.DMA(()),
            pltpu.SemaphoreType.DMA(()),
        ],
        nbytes=MIB,
        vmem=4 * MIB,
    )


def finish_columns(got_xa, got_xb, ya, yb):
    _, size_y, size_z, channels = got_xa.shape
    size_x = ya.shape[1]

    def kernel(xa, xb, ya, yb, out_a, out_b):
        odd, low_ok, high_ok = side_of("gx")
        first_y = pick(lax.axis_index("gy") % 2, size_y - 1, 0)
        for out, own, y in ((out_a, ya, first_y), (out_b, yb, size_y - 1 - first_y)):
            for f in range(2):
                out[f, 0] = pick(odd, xb[f, y], xa[f, y]) * low_ok
                out[f, size_x + 1] = pick(odd, xa[f, y], xb[f, y]) * high_ok
                out[f, 1 : size_x + 1] = own[f]

    shape = jax.ShapeDtypeStruct((2, size_x + 2, size_z, channels), BF16)
    return call(kernel, (shape, shape), (got_xa, got_xb, ya, yb), [], nbytes=MIB, vmem=4 * MIB)


def swap_neighbours(axis, first, second):
    return tuple(
        lax.ppermute(value, ("gx", "gy"), swap_pairs(axis, odd)) for value, odd in ((first, False), (second, True))
    )


def store_shifts(zc, x, ys, rows):
    size_z = zc.shape[2]
    count, lanes = rows.shape
    wide = rows.astype(F32)
    z = lax.broadcasted_iota(jnp.int32, (count, lanes), 0) % size_z
    below = jnp.where(z == 0, 0.0, pltpu.roll(wide, 1, 0)).astype(BF16)
    above = jnp.where(z == size_z - 1, 0.0, pltpu.roll(wide, count - 1, 0)).astype(BF16)
    shape = (count // size_z, size_z, lanes)
    for k, part in enumerate((below, rows, above)):
        zc[x, ys[0] : ys[1], :, k * lanes : (k + 1) * lanes] = part.reshape(shape)


def fill_own(zc, plane):
    size_x, size_y = zc.shape[0] - 2, zc.shape[1] - 2
    zc[0] = jnp.zeros(zc.shape[1:], BF16)
    zc[size_x + 1] = jnp.zeros(zc.shape[1:], BF16)
    for x in range(size_x):
        for y in (0, size_y + 1):
            zc[x + 1, y] = jnp.zeros(zc.shape[2:], BF16)
        store_shifts(zc, x + 1, (1, size_y + 1), plane(x))


def fill_sides(zc, f, xa, xb):
    size_x, size_y, size_z = zc.shape[0] - 2, zc.shape[1] - 2, zc.shape[2]
    rows = size_y * size_z
    odd, low_ok, high_ok = side_of("gx")
    channels = xa.shape[3]
    store_shifts(zc, 0, (1, size_y + 1), (pick(odd, xb[f], xa[f]) * low_ok).reshape(rows, channels))
    store_shifts(zc, size_x + 1, (1, size_y + 1), (pick(odd, xa[f], xb[f]) * high_ok).reshape(rows, channels))


def fill_columns(zc, f, ya, yb):
    size_x, size_y = zc.shape[0] - 2, zc.shape[1] - 2
    odd, low_ok, high_ok = side_of("gy")
    for x in range(size_x + 2):
        store_shifts(zc, x, (0, 1), pick(odd, yb[f, x], ya[f, x]) * low_ok)
        store_shifts(zc, x, (size_y + 1, size_y + 2), pick(odd, ya[f, x], yb[f, x]) * high_ok)


def straight(w):
    return lambda tap: w[tap]


def turned(w):
    return lambda tap: w[26 - tap].T


def lay_weights(taps, weight):
    channels = taps.shape[2] // 2
    zero = jnp.zeros((channels, channels), BF16)
    for j in range(3):
        for k in range(3):
            rows = slice(k * channels, (k + 1) * channels)
            for tap in range(3):
                value = weight(9 * tap + 3 * j + k)
                taps[3 * tap + j, rows, :channels] = value
                taps[3 * (tap + 1) + j, rows, channels:] = value
            taps[j, rows, channels:] = zero
            taps[9 + j, rows, :channels] = zero


def convolve(zc, taps, emit):
    size_x, size_y, size_z = zc.shape[0] - 2, zc.shape[1] - 2, zc.shape[2]
    depth = zc.shape[3]
    channels = depth // 3
    rows = size_y * size_z
    for x in range(0, size_x, 4):
        pieces = []
        for i in range(4):
            for j in range(3):
                halves = [zc[x + 2 * h + i, j : j + size_y].reshape(rows, depth) for h in range(2)]
                pieces.append(jnp.concatenate(halves, axis=0))
        both = jnp.dot(
            jnp.concatenate(pieces, axis=1),
            taps[...].reshape(12 * depth, 2 * channels),
            preferred_element_type=F32,
        )
        for h in range(2):
            for side in range(2):
                emit(x + 2 * h + side, both[h * rows : (h + 1) * rows, side * channels : (side + 1) * channels])


def add_halo_terms(total, zc, taps):
    size_x, size_y, size_z = zc.shape[0] - 2, zc.shape[1] - 2, zc.shape[2]
    depth = zc.shape[3]
    channels = depth // 3
    rows = size_y * size_z

    def weights(which):
        return jnp.concatenate([taps[n, :, :channels] for n in which], axis=0)

    for plane, x, first in ((0, 0, 0), (size_x + 1, size_x - 1, 6)):
        side = jnp.concatenate([zc[plane, j : j + size_y].reshape(rows, depth) for j in range(3)], axis=1)
        total[x] += jnp.dot(side, weights((first, first + 1, first + 2)), preferred_element_type=F32)
    none = jnp.zeros((size_z, depth), BF16)
    for column, y, j in ((0, 0, 0), (size_y + 1, size_y - 1, 2)):
        own = zc[1 : size_x + 1, column].reshape(size_x * size_z, depth)
        below = jnp.concatenate([none, own[:-size_z]], axis=0)
        above = jnp.concatenate([own[size_z:], none], axis=0)
        side = jnp.concatenate([below, own, above], axis=1)
        term = jnp.dot(side, weights((j, 3 + j, 6 + j)), preferred_element_type=F32)
        total[:, y * size_z : (y + 1) * size_z, :] += term.reshape(size_x, size_z, channels)


def field_shape(shape):
    size_x, size_y, size_z, channels = shape
    return (size_x + 2, size_y + 2, size_z, 3 * channels)


def taps_shape(channels):
    return (12, 3 * channels, 2 * channels)


def own_terms(mask, field, w, lay):
    size_x, size_y, size_z, channels = field.shape
    rows = size_y * size_z

    def kernel(mask, field, w, zc, taps, total):
        def plane(x):
            return field[x].reshape(rows, channels) * mask[x // BLOCK].astype(BF16)

        fill_own(zc, plane)
        lay_weights(taps, lay(w))

        def emit(x, value):
            total[x] = value

        convolve(zc, taps, emit)

    return call(
        kernel,
        (
            pltpu.VMEM(field_shape(field.shape), BF16),
            pltpu.VMEM(taps_shape(channels), BF16),
            pltpu.VMEM((size_x, rows, channels), F32),
        ),
        (mask, field, w),
        [],
        flops=2 * 27 * size_x * rows * channels * channels,
        nbytes=4 * MIB,
        vmem=14 * MIB,
    )


def copy_sides(f, value, xa, xb, ya, yb):
    size_x, size_y = value.shape[:2]
    first_x = pick(lax.axis_index("gx") % 2, size_x - 1, 0)
    first_y = pick(lax.axis_index("gy") % 2, size_y - 1, 0)
    xa[f], xb[f] = value[first_x], value[size_x - 1 - first_x]
    for x in range(size_x):
        ya[f, x], yb[f, x] = value[x, first_y], value[x, size_y - 1 - first_y]


def side_shapes(shape):
    size_x, size_y, size_z, channels = shape
    side = jax.ShapeDtypeStruct((2, size_y, size_z, channels), BF16)
    column = jax.ShapeDtypeStruct((2, size_x, size_z, channels), BF16)
    return (side, side, column, column)


def grad_terms(left, zc, start, store):
    size_x, size_y, size_z = zc.shape[0] - 2, zc.shape[1] - 2, zc.shape[2]
    depth = zc.shape[3]
    channels = depth // 3
    shifts = [(i, j) for i in range(3) for j in range(3)]
    for group in [shifts[n : n + 2] for n in range(0, 9, 2)]:
        pieces = []
        for i, j in group:
            a, b = start(i, j)
            pieces.append(zc[a : a + size_x, b : b + size_y].reshape(size_x * size_y * size_z, depth))
        out = jnp.dot(left, jnp.concatenate(pieces, axis=1), preferred_element_type=F32)
        for n, (i, j) in enumerate(group):
            for k in range(3):
                store(9 * i + 3 * j, k, out[:, (3 * n + k) * channels : (3 * n + k + 1) * channels])


def scatter_block(keep, send, d, block):
    count = 2 * keep.shape[0]
    share = keep.shape[2]
    index = lax.axis_index("gy")
    half, place = index % 2, index // 2
    for j in range(count // 2):
        even = block[2 * j * share : (2 * j + 1) * share]
        odd = block[(2 * j + 1) * share : (2 * j + 2) * share]
        at = jnp.bitwise_xor(place, j)
        keep[at, d] = pick(half, even, odd)
        send[at, d] = pick(half, odd, even)


def terms_shape(channels):
    count_y = lax.axis_size("gy")
    return jax.ShapeDtypeStruct((count_y // 2, 27, channels // count_y, channels), F32)


def hidden_and_terms(mask, halos, zm, zu, taps, pre, shape):
    size_x, size_y, size_z, channels = shape
    rows = size_y * size_z

    def kernel(mask, xa, xb, ya, yb, taps, pre, zm_in, zu_in, zm, zu, hidden, slope, keep, send):
        for f, zc in enumerate((zm, zu)):
            fill_sides(zc, f, xa, xb)
            fill_columns(zc, f, ya, yb)
        slope[...] = pre[...]
        add_halo_terms(slope, zm, taps)
        for x in range(size_x):
            here = mask[x // BLOCK]
            value = slope[x]
            s = jax.nn.sigmoid(value)
            hidden[x] = (here * (value * s)).astype(BF16).reshape(size_y, size_z, channels)
            slope[x] = here * (s * (1.0 + value * (1.0 - s)))
        left = hidden[...].reshape(size_x * rows, channels).T

        def store(d, k, block):
            scatter_block(keep, send, d + 2 - k, block)

        grad_terms(left, zu, lambda i, j: (2 - i, 2 - j), store)

    field = jax.ShapeDtypeStruct(shape, BF16)
    wide = jax.ShapeDtypeStruct(pre.shape, F32)
    shifted = jax.ShapeDtypeStruct(zm.shape, BF16)
    terms = terms_shape(channels)
    return call(
        kernel,
        (shifted, shifted, field, wide, terms, terms),
        (mask, *halos, taps, pre, zm, zu),
        [],
        flops=2 * 27 * size_x * rows * channels * channels,
        nbytes=8 * MIB,
        vmem=14 * MIB,
        aliases={7: 0, 8: 1},
    )


def pre_grad_and_terms(hidden, slope, zm, zu, taps, grad):
    size_x, rows, channels = grad.shape
    size_y, size_z = zu.shape[1] - 2, zu.shape[2]
    shape = (size_x, size_y, size_z, channels)

    def kernel(hidden, slope, zm, zu, taps, grad, pre_grad, keep, send, xa, xb, ya, yb, total):
        total[...] = grad[...]
        add_halo_terms(total, zu, taps)
        for x in range(size_x):
            pre_grad[x] = (total[x] * slope[x]).astype(BF16).reshape(size_y, size_z, channels)
        for f, value in enumerate((hidden, pre_grad)):
            copy_sides(f, value, xa, xb, ya, yb)
        left = pre_grad[...].reshape(size_x * rows, channels).T

        def store(d, k, block):
            scatter_block(keep, send, d + k, block.T)

        grad_terms(left, zm, lambda i, j: (i, j), store)

    terms = terms_shape(channels)
    return call(
        kernel,
        (jax.ShapeDtypeStruct(shape, BF16), terms, terms, *side_shapes(shape)),
        (hidden, slope, zm, zu, taps, grad),
        [],
        scratch=[pltpu.VMEM(grad.shape, F32)],
        flops=2 * 27 * size_x * rows * channels * channels,
        nbytes=8 * MIB,
        vmem=14 * MIB,
    )


def add_convolution(mask, own, field, f, halos, w, lay):
    size_x, size_y, size_z, channels = own.shape
    rows = size_y * size_z

    def kernel(mask, own, field, xa, xb, ya, yb, w, out, zc, taps):
        for x in range(size_x):
            store_shifts(zc, x + 1, (1, size_y + 1), field[x].reshape(rows, channels))
        fill_sides(zc, f, xa, xb)
        fill_columns(zc, f, ya, yb)
        lay_weights(taps, lay(w))

        def emit(x, term):
            near = own[x].reshape(rows, channels).astype(F32)
            out[x] = (mask[x // BLOCK] * (near + term)).astype(BF16).reshape(size_y, size_z, channels)

        convolve(zc, taps, emit)

    return call(
        kernel,
        jax.ShapeDtypeStruct(own.shape, BF16),
        (mask, own, field, *halos, w),
        [],
        scratch=[pltpu.VMEM(field_shape(own.shape), BF16), pltpu.VMEM(taps_shape(channels), BF16)],
        flops=2 * 27 * size_x * rows * channels * channels,
        nbytes=3 * MIB,
        vmem=14 * MIB,
    )


def after(values, *others):
    return lax.optimization_barrier((values, others))[0]


def swap(value, axis, bit):
    return lax.ppermute(value, axis, [(i, i ^ bit) for i in range(lax.axis_size(axis))])


def is_far(place):
    return place & (place - 1) != 0


def first_sum(g, keep, came, earlier):
    places, taps, share, channels = keep.shape
    rows = taps * share
    far = [p for p in range(places) if is_far(p)]
    near = [p for p in range(1, places) if not is_far(p)]

    def kernel(keep, came, *refs):
        outs = refs[-places:]
        for p in range(places):
            value = (keep[p] + came[p]).reshape(rows, channels)
            if p == 0:
                outs[0][g] = value
            elif p in near:
                outs[1 + near.index(p)][g] = value.astype(BF16)
            else:
                outs[1 + len(near) + far.index(p)][...] = value.astype(BF16)

    stay = pltpu.VMEM((2, rows, channels), F32)
    both = pltpu.VMEM((2, rows, channels), BF16)
    one = pltpu.VMEM((rows, channels), BF16)
    outs = call(
        kernel,
        (stay,) + (both,) * len(near) + (one,) * len(far),
        (keep, came, *earlier),
        [],
        nbytes=2 * MIB,
        vmem=4 * MIB,
        aliases={2 + n: n for n in range(len(earlier))},
    )
    count = 1 + len(near)
    return outs[:count], outs[count:]


CODE_ROWS = 16
CODE_TOP = 32000.0


def encode(value, out):
    most = jnp.max(jnp.max(jnp.abs(value), axis=0, keepdims=True), axis=1, keepdims=True)
    power = jnp.ceil(jnp.log2(jnp.clip(most, 2.0**-100, 2.0**100)))
    power = jnp.broadcast_to(power, (1, value.shape[1]))
    head = jnp.broadcast_to(power, (CODE_ROWS, value.shape[1]))
    out[:CODE_ROWS] = head.astype(jnp.int32).astype(jnp.int16)
    scaled = value * (CODE_TOP * jnp.exp2(-power))
    out[CODE_ROWS:] = jnp.round(scaled).astype(jnp.int32).astype(jnp.int16)


def decode(ref):
    power = ref[:CODE_ROWS].astype(jnp.int32).astype(F32)[:1]
    return ref[CODE_ROWS:].astype(jnp.int32).astype(F32) * (jnp.exp2(power) * (1.0 / CODE_TOP))


def coded_shape(rows, channels):
    return pltpu.VMEM((CODE_ROWS + rows, channels), jnp.int16)


def second_sums(stays, near, far):
    _, rows, channels = stays.shape
    count = len(near)

    def kernel(stays, *refs):
        near, (stay, leave) = refs[:count], refs[-2:]
        far = (refs[count : count + len(far_second)], refs[count + len(far_second) : -2])
        odd = lax.axis_index("gx") % 2
        totals = []
        for g in range(2):
            value = stays[g]
            for ref in near:
                value += ref[g].astype(F32)
            for ref in far[g]:
                value += ref[...].astype(F32)
            totals.append(value)
        stay[...] = pick(odd, totals[0], totals[1])
        encode(pick(odd, totals[1], totals[0]), leave)

    far_second, far_first = far
    outs = (pltpu.VMEM((rows, channels), F32), coded_shape(rows, channels))
    return call(kernel, outs, (stays, *near, *far_second, *far_first), [], nbytes=2 * MIB, vmem=4 * MIB)


def next_sum(own, came):
    rows, channels = came.shape[0] - CODE_ROWS, came.shape[1]
    coded = own.dtype != F32

    def kernel(own, came, out):
        encode((decode(own) if coded else own[...]) + decode(came), out)

    return call(kernel, coded_shape(rows, channels), (own, came), [], nbytes=MIB, vmem=4 * MIB)


def final_grads(own, came, taps, factor):
    rows, channels = came.shape[0] - CODE_ROWS, came.shape[1]

    def kernel(own, came, second, first):
        odd = lax.axis_index("gx") % 2
        mine, other = decode(own) * factor, decode(came) * factor
        second[...] = pick(odd, mine, other).reshape(second.shape)
        first[...] = pick(odd, other, mine).reshape(first.shape)

    shape = jax.ShapeDtypeStruct((taps, rows // taps, channels), F32)
    return call(kernel, (shape, shape), (own, came), [], nbytes=MIB, vmem=4 * MIB)


def body(features, w_first, w_second, occ, cotangent):
    count_x, count_y = lax.axis_size("gx"), lax.axis_size("gy")
    shape = features.shape
    mask, xa, xb, ya, yb, own, weights = pack_sides(features, cotangent, occ, w_first)
    xa, xb = swap_neighbours("gx", xa, xb)
    zm, first_taps, pre = own_terms(mask, own, weights, straight)
    xa, xb = after((xa, xb), pre)
    ya, yb = finish_columns(xa, xb, ya, yb)
    behind = after(mask, ya)
    ya, yb = swap_neighbours("gy", ya, yb)
    zu, second_taps, grad = own_terms(behind, cotangent, w_second, turned)
    halos = after((xa, xb, ya, yb), grad)
    zm, zu, hidden, slope, keep_second, send = hidden_and_terms(mask, halos, zm, zu, first_taps, pre, shape)
    came = swap(send, "gy", 1)
    pre_grad, keep_first, send, xa, xb, ya, yb = pre_grad_and_terms(hidden, slope, zm, zu, second_taps, grad)

    places = range(1, keep_first.shape[0])
    sums, leaves = first_sum(0, keep_second, after(came, pre_grad), ())
    far_second = [swap(value, "gy", 2 * p) for value, p in zip(leaves, filter(is_far, places))]
    came = swap(send, "gy", 1)
    (stays, *near), leaves = first_sum(1, keep_first, after(came, sums[0]), sums)
    near = [swap(value, "gy", 2 * p) for value, p in zip(near, (p for p in places if not is_far(p)))]
    far_first = [swap(value, "gy", 2 * p) for value, p in zip(leaves, filter(is_far, places))]
    xa, xb = swap_neighbours("gx", *after((xa, xb), far_second, stays))
    stays, leaves = second_sums(stays, *after((near, (far_second, far_first)), xa, xb))
    xa, xb = after((xa, xb), leaves)
    came = swap(leaves, "gx", 1)
    ya, yb = finish_columns(xa, xb, ya, yb)
    came = after(came, ya)
    ya, yb = swap_neighbours("gy", ya, yb)
    stays = next_sum(stays, came)
    convolutions = [
        (mask, features, hidden, 0, w_second, straight),
        (mask, cotangent, pre_grad, 1, w_first, turned),
    ]
    results = []

    def convolve_beside(came, behind):
        if len(results) == len(convolutions):
            return came
        mask, own, field, f, w, lay = convolutions[len(results)]
        halos = after((xa, xb, ya, yb), behind)
        results.append(add_convolution(mask, own, field, f, halos, w, lay))
        return after(came, results[-1])

    bit = 2
    while bit < count_x:
        stays = next_sum(stays, convolve_beside(swap(stays, "gx", bit), stays))
        bit *= 2
    came = convolve_beside(swap(stays, "gx", 1), stays)
    factor = 1.0 / math.sqrt(count_x * count_y * shape[0] * shape[1] * shape[2])
    grad_second, grad_first = final_grads(stays, came, w_first.shape[0], factor)
    output, grad_features = results
    return output, grad_features, grad_first, grad_second


def solution(mesh):
    in_specs = (P("gx", "gy", None, None), P(), P(), P("gx", "gy", None), P("gx", "gy", None, None))
    out_specs = (
        P("gx", "gy", None, None),
        P("gx", "gy", None, None),
        P(None, "gy", None),
        P(None, "gy", None),
    )
    return jax.shard_map(body, mesh=mesh, in_specs=in_specs, out_specs=out_specs, check_vma=False)
```

```python
import math

import jax
import jax.numpy as jnp
from jax import lax
from jax.experimental import pallas as pl
from jax.experimental.pallas import tpu as pltpu
from jax.sharding import PartitionSpec as P

BF16 = jnp.bfloat16
F32 = jnp.float32
VMEM = pl.BlockSpec(memory_space=pltpu.VMEM)
HBM = pl.BlockSpec(memory_space=pltpu.HBM)
MIB = 1024 * 1024
BLOCK = 8


def call(kernel, out_shapes, args, spaces, scratch=(), flops=0, nbytes=0, vmem=16 * MIB, aliases=None):
    return pl.pallas_call(
        kernel,
        out_shape=out_shapes,
        in_specs=list(spaces) + [VMEM] * (len(args) - len(spaces)),
        out_specs=jax.tree.map(lambda _: VMEM, out_shapes),
        scratch_shapes=list(scratch),
        input_output_aliases=aliases or {},
        compiler_params=pltpu.CompilerParams(vmem_limit_bytes=vmem),
        cost_estimate=pl.CostEstimate(flops=flops, bytes_accessed=nbytes, transcendentals=0),
    )(*args)


def swap_pairs(axis, odd):
    count_x, count_y = lax.axis_size("gx"), lax.axis_size("gy")
    pairs = []
    for x in range(count_x):
        for y in range(count_y):
            at, count = (x, count_x) if axis == "gx" else (y, count_y)
            to = at - 1 if (at % 2 == 0) == odd else at + 1
            if not 0 <= to < count:
                other = (x, y ^ 1) if axis == "gx" else (x ^ 1, y)
            else:
                other = (to, y) if axis == "gx" else (x, to)
            pairs.append((x * count_y + y, other[0] * count_y + other[1]))
    return pairs


def plane_mask(occ, block_x, size_y, size_z):
    row = lax.broadcasted_iota(jnp.int32, (size_y * size_z, 128), 0)
    block_y = row // (BLOCK * size_z)
    block_z = (row % size_z) // BLOCK
    mask = jnp.zeros((size_y * size_z, 128), F32)
    for i in range(size_y // BLOCK):
        for j in range(size_z // BLOCK):
            here = (block_y == i) & (block_z == j)
            mask = jnp.where(here, occ[block_x, i, j].astype(F32), mask)
    return mask


def pick(odd, if_even, if_odd):
    return jnp.where(odd == 0, if_even, if_odd)


def one_if(condition):
    return jnp.where(condition, 1.0, 0.0).astype(BF16)


def side_of(axis):
    index = lax.axis_index(axis)
    return index % 2, one_if(index > 0), one_if(index < lax.axis_size(axis) - 1)


def pack_sides(features, cotangent, occ):
    size_x, size_y, size_z, channels = features.shape
    rows = size_y * size_z

    def kernel(occ_hbm, first, second, mask, xa, xb, ya, yb, own, occ_ref, sem, occ_sem, own_sem):
        odd_x, odd_y = lax.axis_index("gx") % 2, lax.axis_index("gy") % 2
        first_x = pick(odd_x, size_x - 1, 0)
        first_y = pick(odd_y, size_y - 1, 0)
        sides = ((xa, first_x), (xb, size_x - 1 - first_x))
        columns = ((ya, first_y), (yb, size_y - 1 - first_y))
        occ_copy = pltpu.make_async_copy(occ_hbm, occ_ref, occ_sem)
        own_copy = pltpu.make_async_copy(first, own, own_sem)
        copies = []
        for n, (out, x) in enumerate(sides):
            copies.append(pltpu.make_async_copy(second.at[x], out.at[1], sem.at[n]))
        for n, (out, y) in enumerate(columns):
            copies.append(pltpu.make_async_copy(second.at[:, y], out.at[1], sem.at[2 + n]))
        for copy in [occ_copy, own_copy, *copies]:
            copy.start()
        occ_copy.wait()
        for n in range(size_x // BLOCK):
            mask[n] = plane_mask(occ_ref, n, size_y, size_z)
        own_copy.wait()
        for out, x in sides:
            out[0] = own[x] * mask[x // BLOCK].astype(BF16).reshape(size_y, size_z, channels)
        for out, y in columns:
            at = pl.ds(pl.multiple_of(y * size_z, size_z), size_z)
            for x in range(size_x):
                out[0, x] = own[x, y] * mask[x // BLOCK, at, :].astype(BF16)
        for copy in copies:
            copy.wait()
        for out, x in sides:
            out[1] = out[1] * mask[x // BLOCK].astype(BF16).reshape(size_y, size_z, channels)
        for out, y in columns:
            at = pl.ds(pl.multiple_of(y * size_z, size_z), size_z)
            for x in range(size_x):
                out[1, x] = out[1, x] * mask[x // BLOCK, at, :].astype(BF16)

    side = pltpu.VMEM((2, size_y, size_z, channels), BF16)
    column = pltpu.VMEM((2, size_x, size_z, channels), BF16)
    return call(
        kernel,
        (
            pltpu.VMEM((size_x // BLOCK, rows, channels), F32),
            side,
            side,
            column,
            column,
            pltpu.VMEM(features.shape, BF16),
        ),
        [pltpu.with_memory_space_constraint(value, pltpu.HBM) for value in (occ, features, cotangent)],
        [HBM] * 3,
        scratch=[
            pltpu.SMEM(occ.shape, jnp.int32),
            pltpu.SemaphoreType.DMA((4,)),
            pltpu.SemaphoreType.DMA(()),
            pltpu.SemaphoreType.DMA(()),
        ],
        flops=8 << 30,
        nbytes=MIB,
        vmem=4 * MIB,
    )


def finish_columns(got_xa, got_xb, ya, yb):
    _, size_y, size_z, channels = got_xa.shape
    size_x = ya.shape[1]

    def kernel(xa, xb, ya, yb, out_a, out_b):
        odd, low_ok, high_ok = side_of("gx")
        first_y = pick(lax.axis_index("gy") % 2, size_y - 1, 0)
        for out, own, y in ((out_a, ya, first_y), (out_b, yb, size_y - 1 - first_y)):
            for f in range(2):
                out[f, 0] = pick(odd, xb[f, y], xa[f, y]) * low_ok
                out[f, size_x + 1] = pick(odd, xa[f, y], xb[f, y]) * high_ok
                out[f, 1 : size_x + 1] = own[f]

    shape = jax.ShapeDtypeStruct((2, size_x + 2, size_z, channels), BF16)
    return call(kernel, (shape, shape), (got_xa, got_xb, ya, yb), [], nbytes=MIB, vmem=4 * MIB)


def swap_neighbours(axis, first, second):
    second = lax.ppermute(second, ("gx", "gy"), swap_pairs(axis, True))
    first = lax.ppermute(first, ("gx", "gy"), swap_pairs(axis, False))
    return first, second


def store_shifts(zc, x, ys, rows):
    size_z = zc.shape[2]
    count, lanes = rows.shape
    wide = rows.astype(F32)
    z = lax.broadcasted_iota(jnp.int32, (count, lanes), 0) % size_z
    below = jnp.where(z == 0, 0.0, pltpu.roll(wide, 1, 0)).astype(BF16)
    above = jnp.where(z == size_z - 1, 0.0, pltpu.roll(wide, count - 1, 0)).astype(BF16)
    shape = (count // size_z, size_z, lanes)
    for k, part in enumerate((below, rows, above)):
        zc[x, ys[0] : ys[1], :, k * lanes : (k + 1) * lanes] = part.reshape(shape)


def fill_own(zc, plane):
    size_x, size_y = zc.shape[0] - 2, zc.shape[1] - 2
    zc[0] = jnp.zeros(zc.shape[1:], BF16)
    zc[size_x + 1] = jnp.zeros(zc.shape[1:], BF16)
    for x in range(size_x):
        for y in (0, size_y + 1):
            zc[x + 1, y] = jnp.zeros(zc.shape[2:], BF16)
        store_shifts(zc, x + 1, (1, size_y + 1), plane(x))


def fill_sides(zc, f, xa, xb):
    size_x, size_y, size_z = zc.shape[0] - 2, zc.shape[1] - 2, zc.shape[2]
    rows = size_y * size_z
    odd, low_ok, high_ok = side_of("gx")
    channels = xa.shape[3]
    store_shifts(zc, 0, (1, size_y + 1), (pick(odd, xb[f], xa[f]) * low_ok).reshape(rows, channels))
    store_shifts(zc, size_x + 1, (1, size_y + 1), (pick(odd, xa[f], xb[f]) * high_ok).reshape(rows, channels))


def fill_columns(zc, f, ya, yb):
    size_x, size_y = zc.shape[0] - 2, zc.shape[1] - 2
    odd, low_ok, high_ok = side_of("gy")
    for x in range(size_x + 2):
        store_shifts(zc, x, (0, 1), pick(odd, yb[f, x], ya[f, x]) * low_ok)
        store_shifts(zc, x, (size_y + 1, size_y + 2), pick(odd, ya[f, x], yb[f, x]) * high_ok)


def straight(w):
    return lambda tap: w[tap]


def turned(w):
    return lambda tap: w[26 - tap].T


def lay_weights(taps, weight):
    channels = taps.shape[2] // 2
    zero = jnp.zeros((channels, channels), BF16)
    for j in range(3):
        for k in range(3):
            rows = slice(k * channels, (k + 1) * channels)
            for tap in range(3):
                value = weight(9 * tap + 3 * j + k)
                taps[3 * tap + j, rows, :channels] = value
                taps[3 * (tap + 1) + j, rows, channels:] = value
            taps[j, rows, channels:] = zero
            taps[9 + j, rows, :channels] = zero


def convolve(zc, taps, emit):
    size_x, size_y, size_z = zc.shape[0] - 2, zc.shape[1] - 2, zc.shape[2]
    depth = zc.shape[3]
    channels = depth // 3
    rows = size_y * size_z
    for x in range(0, size_x, 4):
        pieces = []
        for i in range(4):
            for j in range(3):
                halves = [zc[x + 2 * h + i, j : j + size_y].reshape(rows, depth) for h in range(2)]
                pieces.append(jnp.concatenate(halves, axis=0))
        both = jnp.dot(
            jnp.concatenate(pieces, axis=1),
            taps[...].reshape(12 * depth, 2 * channels),
            preferred_element_type=F32,
        )
        for h in range(2):
            for side in range(2):
                emit(x + 2 * h + side, both[h * rows : (h + 1) * rows, side * channels : (side + 1) * channels])


def side_weights(taps, which):
    channels = taps.shape[2] // 2
    return jnp.concatenate([taps[n, :, :channels] for n in which], axis=0)


def add_side_terms(total, zc, taps):
    size_x, size_y, size_z = zc.shape[0] - 2, zc.shape[1] - 2, zc.shape[2]
    depth = zc.shape[3]
    rows = size_y * size_z
    for plane, x, first in ((0, 0, 0), (size_x + 1, size_x - 1, 6)):
        side = jnp.concatenate([zc[plane, j : j + size_y].reshape(rows, depth) for j in range(3)], axis=1)
        weights = side_weights(taps, (first, first + 1, first + 2))
        total[x] += jnp.dot(side, weights, preferred_element_type=F32)


def add_column_terms(total, zc, taps):
    size_x, size_y, size_z = zc.shape[0] - 2, zc.shape[1] - 2, zc.shape[2]
    depth = zc.shape[3]
    for column, y, j in ((0, 0, 0), (size_y + 1, size_y - 1, 2)):
        pieces = [zc[i : i + size_x, column].reshape(size_x * size_z, depth) for i in range(3)]
        weights = side_weights(taps, (j, 3 + j, 6 + j))
        term = jnp.dot(jnp.concatenate(pieces, axis=1), weights, preferred_element_type=F32)
        total[:, y * size_z : (y + 1) * size_z, :] += term.reshape(size_x, size_z, -1)


def field_shape(shape):
    size_x, size_y, size_z, channels = shape
    return (size_x + 2, size_y + 2, size_z, 3 * channels)


def taps_shape(channels):
    return (12, 3 * channels, 2 * channels)


def own_shapes(shape):
    size_x, size_y, size_z, channels = shape
    return (
        pltpu.VMEM(field_shape(shape), BF16),
        pltpu.VMEM(taps_shape(channels), BF16),
        pltpu.VMEM((size_x, size_y * size_z, channels), F32),
    )


def masked_plane(field, mask):
    def plane(x):
        value = field[x]
        return value.reshape(-1, value.shape[2]) * mask[x // BLOCK].astype(BF16)

    return plane


def store_in(total):
    def emit(x, value):
        total[x] = value

    return emit


def own_terms(mask, field, w, lay):
    size_x, size_y, size_z, channels = field.shape

    def kernel(mask, field, w, zc, taps, total):
        fill_own(zc, masked_plane(field, mask))
        lay_weights(taps, lay(w))
        convolve(zc, taps, store_in(total))

    return call(
        kernel,
        own_shapes(field.shape),
        (mask, field, w),
        [],
        flops=2 * 27 * field.size * channels,
        nbytes=4 * MIB,
        vmem=14 * MIB,
    )


def own_terms_and_sides(mask, field, w, zm, first_taps, pre, xa, xb):
    channels = field.shape[3]

    def kernel(mask, field, w, first_taps, xa, xb, zm_in, pre_in, zu, taps, total, zm, pre):
        fill_own(zu, masked_plane(field, mask))
        lay_weights(taps, turned(w))
        convolve(zu, taps, store_in(total))
        for f, (zc, weights, out) in enumerate(((zm, first_taps, pre), (zu, taps, total))):
            fill_sides(zc, f, xa, xb)
            add_side_terms(out, zc, weights)

    return call(
        kernel,
        (*own_shapes(field.shape), pltpu.VMEM(zm.shape, BF16), pltpu.VMEM(pre.shape, F32)),
        (mask, field, w, first_taps, xa, xb, zm, pre),
        [],
        flops=2 * 27 * field.size * channels,
        nbytes=4 * MIB,
        vmem=14 * MIB,
        aliases={6: 3, 7: 4},
    )


def copy_sides(f, value, xa, xb, ya, yb):
    size_x, size_y = value.shape[:2]
    first_x = pick(lax.axis_index("gx") % 2, size_x - 1, 0)
    first_y = pick(lax.axis_index("gy") % 2, size_y - 1, 0)
    xa[f], xb[f] = value[first_x], value[size_x - 1 - first_x]
    for x in range(size_x):
        ya[f, x], yb[f, x] = value[x, first_y], value[x, size_y - 1 - first_y]


def side_shapes(shape):
    size_x, size_y, size_z, channels = shape
    side = jax.ShapeDtypeStruct((2, size_y, size_z, channels), BF16)
    column = jax.ShapeDtypeStruct((2, size_x, size_z, channels), BF16)
    return (side, side, column, column)


def grad_terms(left, zc, start, store):
    size_x, size_y, size_z = zc.shape[0] - 2, zc.shape[1] - 2, zc.shape[2]
    depth = zc.shape[3]
    channels = depth // 3
    shifts = [(i, j) for i in range(3) for j in range(3)]
    for group in [shifts[n : n + 2] for n in range(0, 9, 2)]:
        pieces = []
        for i, j in group:
            a, b = start(i, j)
            pieces.append(zc[a : a + size_x, b : b + size_y].reshape(size_x * size_y * size_z, depth))
        out = jnp.dot(left, jnp.concatenate(pieces, axis=1), preferred_element_type=F32)
        for n, (i, j) in enumerate(group):
            for k in range(3):
                store(9 * i + 3 * j, k, out[:, (3 * n + k) * channels : (3 * n + k + 1) * channels])


def scatter_block(keep, send, d, block):
    count = 2 * keep.shape[0]
    share = keep.shape[2]
    index = lax.axis_index("gy")
    half, place = index % 2, index // 2
    for j in range(count // 2):
        even = block[2 * j * share : (2 * j + 1) * share]
        odd = block[(2 * j + 1) * share : (2 * j + 2) * share]
        at = jnp.bitwise_xor(place, j)
        keep[at, d] = pick(half, even, odd)
        send[at, d] = pick(half, odd, even).astype(send.dtype)


def terms_shape(channels, travel):
    count_y = lax.axis_size("gy")
    shape = (count_y // 2, 27, channels // count_y, channels)
    return jax.ShapeDtypeStruct(shape, F32), jax.ShapeDtypeStruct(shape, travel)


def hidden_and_terms(mask, ya, yb, zm, zu, taps, pre, shape):
    size_x, size_y, size_z, channels = shape
    rows = size_y * size_z

    def kernel(mask, ya, yb, taps, pre, zm_in, zu_in, zm, zu, hidden, slope, keep, send):
        for f, zc in enumerate((zm, zu)):
            fill_columns(zc, f, ya, yb)
        slope[...] = pre[...]
        add_column_terms(slope, zm, taps)
        for x in range(size_x):
            here = mask[x // BLOCK]
            value = slope[x]
            s = jax.nn.sigmoid(value)
            hidden[x] = (here * (value * s)).astype(BF16).reshape(size_y, size_z, channels)
            slope[x] = here * (s * (1.0 + value * (1.0 - s)))
        left = hidden[...].reshape(size_x * rows, channels).T

        def store(d, k, block):
            scatter_block(keep, send, d + 2 - k, block)

        grad_terms(left, zu, lambda i, j: (2 - i, 2 - j), store)

    field = jax.ShapeDtypeStruct(shape, BF16)
    wide = jax.ShapeDtypeStruct(pre.shape, F32)
    shifted = jax.ShapeDtypeStruct(zm.shape, BF16)
    return call(
        kernel,
        (shifted, shifted, field, wide, *terms_shape(channels, F32)),
        (mask, ya, yb, taps, pre, zm, zu),
        [],
        flops=2 * 27 * size_x * rows * channels * channels,
        nbytes=8 * MIB,
        vmem=14 * MIB,
        aliases={5: 0, 6: 1},
    )


def pre_grad_and_terms(hidden, slope, zm, zu, taps, grad):
    size_x, rows, channels = grad.shape
    size_y, size_z = zu.shape[1] - 2, zu.shape[2]
    shape = (size_x, size_y, size_z, channels)

    def kernel(hidden, slope, zm, zu, taps, grad, pre_grad, keep, send, xa, xb, ya, yb, total):
        total[...] = grad[...]
        add_column_terms(total, zu, taps)
        for x in range(size_x):
            pre_grad[x] = (total[x] * slope[x]).astype(BF16).reshape(size_y, size_z, channels)
        for f, value in enumerate((hidden, pre_grad)):
            copy_sides(f, value, xa, xb, ya, yb)
        left = pre_grad[...].reshape(size_x * rows, channels).T

        def store(d, k, block):
            scatter_block(keep, send, d + k, block.T)

        grad_terms(left, zm, lambda i, j: (i, j), store)

    return call(
        kernel,
        (jax.ShapeDtypeStruct(shape, BF16), *terms_shape(channels, BF16), *side_shapes(shape)),
        (hidden, slope, zm, zu, taps, grad),
        [],
        scratch=[pltpu.VMEM(grad.shape, F32)],
        flops=2 * 27 * size_x * rows * channels * channels,
        nbytes=8 * MIB,
        vmem=14 * MIB,
    )


def add_convolution(mask, own, field, f, halos, w, lay):
    size_x, size_y, size_z, channels = own.shape
    rows = size_y * size_z

    def kernel(mask, own, field, xa, xb, ya, yb, w, out, zc, taps):
        for x in range(size_x):
            store_shifts(zc, x + 1, (1, size_y + 1), field[x].reshape(rows, channels))
        fill_sides(zc, f, xa, xb)
        fill_columns(zc, f, ya, yb)
        lay_weights(taps, lay(w))

        def emit(x, term):
            near = own[x].reshape(rows, channels).astype(F32)
            out[x] = (mask[x // BLOCK] * (near + term)).astype(BF16).reshape(size_y, size_z, channels)

        convolve(zc, taps, emit)

    return call(
        kernel,
        jax.ShapeDtypeStruct(own.shape, BF16),
        (mask, own, field, *halos, w),
        [],
        scratch=[pltpu.VMEM(field_shape(own.shape), BF16), pltpu.VMEM(taps_shape(channels), BF16)],
        flops=2 * 27 * size_x * rows * channels * channels,
        nbytes=3 * MIB,
        vmem=14 * MIB,
    )


def add_halos(mask, own, zc, taps, total, f, halos):
    size_x, size_y, size_z, channels = own.shape
    rows = size_y * size_z

    def kernel(mask, own, taps, total_in, xa, xb, ya, yb, zc_in, zc, out, total):
        total[...] = total_in[...]
        fill_sides(zc, f, xa, xb)
        add_side_terms(total, zc, taps)
        fill_columns(zc, f, ya, yb)
        add_column_terms(total, zc, taps)
        for x in range(size_x):
            near = own[x].reshape(rows, channels).astype(F32)
            value = mask[x // BLOCK] * (near + total[x])
            out[x] = value.astype(BF16).reshape(size_y, size_z, channels)

    return call(
        kernel,
        (pltpu.VMEM(zc.shape, BF16), jax.ShapeDtypeStruct(own.shape, BF16)),
        (mask, own, taps, total, *halos, zc),
        [],
        scratch=[pltpu.VMEM(total.shape, F32)],
        nbytes=3 * MIB,
        vmem=14 * MIB,
        aliases={8: 0},
    )[1]


def after(values, *others):
    return lax.optimization_barrier((values, others))[0]


def swap(value, axis, bit):
    return lax.ppermute(value, axis, [(i, i ^ bit) for i in range(lax.axis_size(axis))])


def is_far(place):
    return place & (place - 1) != 0


def first_sum(g, keep, came, earlier):
    places, taps, share, channels = keep.shape
    rows = taps * share
    far = [p for p in range(places) if is_far(p)]
    near = [p for p in range(1, places) if not is_far(p)]

    def kernel(keep, came, *refs):
        outs = refs[-places:]
        for p in range(places):
            value = (keep[p] + came[p].astype(F32)).reshape(rows, channels)
            if p == 0:
                outs[0][g] = value
            elif p in near:
                outs[1 + near.index(p)][g] = value.astype(BF16)
            else:
                outs[1 + len(near) + far.index(p)][...] = value.astype(BF16)

    stay = pltpu.VMEM((2, rows, channels), F32)
    both = pltpu.VMEM((2, rows, channels), BF16)
    one = pltpu.VMEM((rows, channels), BF16)
    outs = call(
        kernel,
        (stay,) + (both,) * len(near) + (one,) * len(far),
        (keep, came, *earlier),
        [],
        nbytes=2 * MIB,
        vmem=4 * MIB,
        aliases={2 + n: n for n in range(len(earlier))},
    )
    count = 1 + len(near)
    return outs[:count], outs[count:]


CODE_ROWS = 16
CODE_TOP = 32000.0


def encode(value, out):
    most = jnp.max(jnp.max(jnp.abs(value), axis=0, keepdims=True), axis=1, keepdims=True)
    power = jnp.ceil(jnp.log2(jnp.clip(most, 2.0**-100, 2.0**100)))
    power = jnp.broadcast_to(power, (1, value.shape[1]))
    head = jnp.broadcast_to(power, (CODE_ROWS, value.shape[1]))
    out[:CODE_ROWS] = head.astype(jnp.int32).astype(jnp.int16)
    scaled = value * (CODE_TOP * jnp.exp2(-power))
    out[CODE_ROWS:] = jnp.round(scaled).astype(jnp.int32).astype(jnp.int16)


def decode(ref):
    power = ref[:CODE_ROWS].astype(jnp.int32).astype(F32)[:1]
    return ref[CODE_ROWS:].astype(jnp.int32).astype(F32) * (jnp.exp2(power) * (1.0 / CODE_TOP))


def coded_shape(rows, channels):
    return pltpu.VMEM((CODE_ROWS + rows, channels), jnp.int16)


def second_sums(stays, near, far):
    _, rows, channels = stays.shape
    count = len(near)

    def kernel(stays, *refs):
        near, (stay, leave) = refs[:count], refs[-2:]
        far = (refs[count : count + len(far_second)], refs[count + len(far_second) : -2])
        odd = lax.axis_index("gx") % 2
        totals = []
        for g in range(2):
            value = stays[g]
            for ref in near:
                value += ref[g].astype(F32)
            for ref in far[g]:
                value += ref[...].astype(F32)
            totals.append(value)
        stay[...] = pick(odd, totals[0], totals[1])
        encode(pick(odd, totals[1], totals[0]), leave)

    far_second, far_first = far
    outs = (pltpu.VMEM((rows, channels), F32), coded_shape(rows, channels))
    return call(kernel, outs, (stays, *near, *far_second, *far_first), [], nbytes=2 * MIB, vmem=4 * MIB)


def next_sum(own, came):
    rows, channels = came.shape[0] - CODE_ROWS, came.shape[1]
    coded = own.dtype != F32

    def kernel(own, came, out):
        encode((decode(own) if coded else own[...]) + decode(came), out)

    return call(kernel, coded_shape(rows, channels), (own, came), [], nbytes=MIB, vmem=4 * MIB)


def final_grads(own, came, taps, factor):
    rows, channels = came.shape[0] - CODE_ROWS, came.shape[1]
    shape = (taps, rows // taps, channels)

    def kernel(own, came, second, first, mine, other, sem):
        odd = lax.axis_index("gx") % 2
        mine[...] = (decode(own) * factor).reshape(shape)

        def copies(value, is_odd, n):
            return (
                (odd == is_odd, pltpu.make_async_copy(value, second, sem.at[n])),
                (odd != is_odd, pltpu.make_async_copy(value, first, sem.at[n])),
            )

        started = copies(mine, 0, 0)
        for where, copy in started:
            pl.when(where)(copy.start)
        other[...] = (decode(came) * factor).reshape(shape)
        later = copies(other, 1, 1)
        for where, copy in later:
            pl.when(where)(copy.start)
        for where, copy in started + later:
            pl.when(where)(copy.wait)

    out = jax.ShapeDtypeStruct(shape, F32)
    return pl.pallas_call(
        kernel,
        out_shape=(out, out),
        in_specs=[VMEM, VMEM],
        out_specs=(HBM, HBM),
        scratch_shapes=[pltpu.VMEM(shape, F32), pltpu.VMEM(shape, F32), pltpu.SemaphoreType.DMA((2,))],
        compiler_params=pltpu.CompilerParams(vmem_limit_bytes=4 * MIB),
        cost_estimate=pl.CostEstimate(flops=0, bytes_accessed=MIB, transcendentals=0),
    )(own, came)


def body(features, w_first, w_second, occ, cotangent):
    count_x, count_y = lax.axis_size("gx"), lax.axis_size("gy")
    shape = features.shape
    mask, xa, xb, ya, yb, own = pack_sides(features, cotangent, occ)
    xa, xb = swap_neighbours("gx", xa, xb)
    zm, first_taps, pre = own_terms(mask, own, w_first, straight)
    xa, xb = after((xa, xb), pre)
    ya, yb = finish_columns(xa, xb, ya, yb)
    behind = after(mask, ya)
    ya, yb = swap_neighbours("gy", ya, yb)
    zu, second_taps, grad, zm, pre = own_terms_and_sides(behind, cotangent, w_second, zm, first_taps, pre, xa, xb)
    ya, yb = after((ya, yb), grad)
    zm, zu, hidden, slope, keep_second, send = hidden_and_terms(mask, ya, yb, zm, zu, first_taps, pre, shape)
    came = swap(send, "gy", 1)
    pre_grad, keep_first, send, xa, xb, ya, yb = pre_grad_and_terms(hidden, slope, zm, zu, second_taps, grad)

    places = range(1, keep_first.shape[0])
    sums, leaves = first_sum(0, keep_second, after(came, pre_grad), ())
    far_second = [swap(value, "gy", 2 * p) for value, p in zip(leaves, filter(is_far, places))]
    came = swap(send, "gy", 1)
    (stays, *near), leaves = first_sum(1, keep_first, after(came, sums[0]), sums)
    near = [swap(value, "gy", 2 * p) for value, p in zip(near, (p for p in places if not is_far(p)))]
    far_first = [swap(value, "gy", 2 * p) for value, p in zip(leaves, filter(is_far, places))]
    behind = after(mask, far_second, stays)
    zp, *own_pre = own_terms(behind, pre_grad, w_first, turned)
    xa, xb = swap_neighbours("gx", *after((xa, xb), own_pre[1]))
    stays, leaves = second_sums(stays, *after((near, (far_second, far_first)), own_pre[1]))
    xa, xb = after((xa, xb), leaves)
    came = swap(leaves, "gx", 1)
    ya, yb = finish_columns(xa, xb, ya, yb)
    came = after(came, ya)
    ya, yb = swap_neighbours("gy", ya, yb)
    stays = next_sum(stays, came)
    bit = 2
    while bit < count_x:
        came = swap(stays, "gx", bit)
        if bit == 2:
            halos = after((xa, xb, ya, yb), stays)
            output = add_convolution(mask, features, hidden, 0, halos, w_second, straight)
            came = after(came, output)
        stays = next_sum(stays, came)
        bit *= 2
    came = swap(stays, "gx", 1)
    grad_features = add_halos(mask, cotangent, zp, *own_pre, 1, after(halos, stays))
    came = after(came, grad_features)
    factor = 1.0 / math.sqrt(count_x * count_y * shape[0] * shape[1] * shape[2])
    grad_second, grad_first = final_grads(stays, came, w_first.shape[0], factor)
    return output, grad_features, grad_first, grad_second


def solution(mesh):
    in_specs = (P("gx", "gy", None, None), P(), P(), P("gx", "gy", None), P("gx", "gy", None, None))
    out_specs = (
        P("gx", "gy", None, None),
        P("gx", "gy", None, None),
        P(None, "gy", None),
        P(None, "gy", None),
    )
    return jax.shard_map(body, mesh=mesh, in_specs=in_specs, out_specs=out_specs, check_vma=False)
```

```python
import math

import jax
import jax.numpy as jnp
from jax import lax
from jax.experimental import pallas as pl
from jax.experimental.pallas import tpu as pltpu
from jax.sharding import PartitionSpec as P

BF16 = jnp.bfloat16
F32 = jnp.float32
VMEM = pl.BlockSpec(memory_space=pltpu.VMEM)
HBM = pl.BlockSpec(memory_space=pltpu.HBM)
MIB = 1024 * 1024
BLOCK = 8


def call(kernel, out_shapes, args, spaces, scratch=(), flops=0, nbytes=0, vmem=16 * MIB, aliases=None):
    return pl.pallas_call(
        kernel,
        out_shape=out_shapes,
        in_specs=list(spaces) + [VMEM] * (len(args) - len(spaces)),
        out_specs=jax.tree.map(lambda _: VMEM, out_shapes),
        scratch_shapes=list(scratch),
        input_output_aliases=aliases or {},
        compiler_params=pltpu.CompilerParams(vmem_limit_bytes=vmem),
        cost_estimate=pl.CostEstimate(flops=flops, bytes_accessed=nbytes, transcendentals=0),
    )(*args)


def swap_pairs(axis, odd):
    count_x, count_y = lax.axis_size("gx"), lax.axis_size("gy")
    pairs = []
    for x in range(count_x):
        for y in range(count_y):
            at, count = (x, count_x) if axis == "gx" else (y, count_y)
            to = at - 1 if (at % 2 == 0) == odd else at + 1
            if not 0 <= to < count:
                other = (x, y ^ 1) if axis == "gx" else (x ^ 1, y)
            else:
                other = (to, y) if axis == "gx" else (x, to)
            pairs.append((x * count_y + y, other[0] * count_y + other[1]))
    return pairs


def plane_mask(occ, block_x, size_y, size_z):
    row = lax.broadcasted_iota(jnp.int32, (size_y * size_z, 128), 0)
    block_y = row // (BLOCK * size_z)
    block_z = (row % size_z) // BLOCK
    mask = jnp.zeros((size_y * size_z, 128), F32)
    for i in range(size_y // BLOCK):
        for j in range(size_z // BLOCK):
            here = (block_y == i) & (block_z == j)
            mask = jnp.where(here, occ[block_x, i, j].astype(F32), mask)
    return mask


def pick(odd, if_even, if_odd):
    return jnp.where(odd == 0, if_even, if_odd)


def one_if(condition):
    return jnp.where(condition, 1.0, 0.0).astype(BF16)


def side_of(axis):
    index = lax.axis_index(axis)
    return index % 2, one_if(index > 0), one_if(index < lax.axis_size(axis) - 1)


def pack_sides(features, cotangent, occ):
    size_x, size_y, size_z, channels = features.shape
    rows = size_y * size_z

    def kernel(occ_hbm, first, second, mask, xa, xb, ya, yb, own, occ_ref, sem, occ_sem, own_sem):
        odd_x, odd_y = lax.axis_index("gx") % 2, lax.axis_index("gy") % 2
        first_x = pick(odd_x, size_x - 1, 0)
        first_y = pick(odd_y, size_y - 1, 0)
        sides = ((xa, first_x), (xb, size_x - 1 - first_x))
        columns = ((ya, first_y), (yb, size_y - 1 - first_y))
        occ_copy = pltpu.make_async_copy(occ_hbm, occ_ref, occ_sem)
        own_copy = pltpu.make_async_copy(first, own, own_sem)
        copies = []
        for n, (out, x) in enumerate(sides):
            copies.append(pltpu.make_async_copy(second.at[x], out.at[1], sem.at[n]))
        for n, (out, y) in enumerate(columns):
            copies.append(pltpu.make_async_copy(second.at[:, y], out.at[1], sem.at[2 + n]))
        for copy in [occ_copy, own_copy, *copies]:
            copy.start()
        occ_copy.wait()
        for n in range(size_x // BLOCK):
            mask[n] = plane_mask(occ_ref, n, size_y, size_z)
        own_copy.wait()
        for out, x in sides:
            out[0] = own[x] * mask[x // BLOCK].astype(BF16).reshape(size_y, size_z, channels)
        for out, y in columns:
            at = pl.ds(pl.multiple_of(y * size_z, size_z), size_z)
            for x in range(size_x):
                out[0, x] = own[x, y] * mask[x // BLOCK, at, :].astype(BF16)
        for copy in copies:
            copy.wait()
        for out, x in sides:
            out[1] = out[1] * mask[x // BLOCK].astype(BF16).reshape(size_y, size_z, channels)
        for out, y in columns:
            at = pl.ds(pl.multiple_of(y * size_z, size_z), size_z)
            for x in range(size_x):
                out[1, x] = out[1, x] * mask[x // BLOCK, at, :].astype(BF16)

    side = pltpu.VMEM((2, size_y, size_z, channels), BF16)
    column = pltpu.VMEM((2, size_x, size_z, channels), BF16)
    return call(
        kernel,
        (
            pltpu.VMEM((size_x // BLOCK, rows, channels), F32),
            side,
            side,
            column,
            column,
            pltpu.VMEM(features.shape, BF16),
        ),
        [pltpu.with_memory_space_constraint(value, pltpu.HBM) for value in (occ, features, cotangent)],
        [HBM] * 3,
        scratch=[
            pltpu.SMEM(occ.shape, jnp.int32),
            pltpu.SemaphoreType.DMA((4,)),
            pltpu.SemaphoreType.DMA(()),
            pltpu.SemaphoreType.DMA(()),
        ],
        flops=8 << 30,
        nbytes=MIB,
        vmem=4 * MIB,
    )


def finish_columns(got_xa, got_xb, ya, yb):
    _, size_y, size_z, channels = got_xa.shape
    size_x = ya.shape[1]

    def kernel(xa, xb, ya, yb, out_a, out_b):
        odd, low_ok, high_ok = side_of("gx")
        first_y = pick(lax.axis_index("gy") % 2, size_y - 1, 0)
        for out, own, y in ((out_a, ya, first_y), (out_b, yb, size_y - 1 - first_y)):
            for f in range(2):
                out[f, 0] = pick(odd, xb[f, y], xa[f, y]) * low_ok
                out[f, size_x + 1] = pick(odd, xa[f, y], xb[f, y]) * high_ok
                out[f, 1 : size_x + 1] = own[f]

    shape = jax.ShapeDtypeStruct((2, size_x + 2, size_z, channels), BF16)
    return call(kernel, (shape, shape), (got_xa, got_xb, ya, yb), [], nbytes=MIB, vmem=4 * MIB)


def swap_neighbours(axis, first, second):
    second = lax.ppermute(second, ("gx", "gy"), swap_pairs(axis, True))
    first = lax.ppermute(first, ("gx", "gy"), swap_pairs(axis, False))
    return first, second


def store_shifts(zc, x, ys, rows):
    size_z = zc.shape[2]
    count, lanes = rows.shape
    wide = rows.astype(F32)
    z = lax.broadcasted_iota(jnp.int32, (count, lanes), 0) % size_z
    below = jnp.where(z == 0, 0.0, pltpu.roll(wide, 1, 0)).astype(BF16)
    above = jnp.where(z == size_z - 1, 0.0, pltpu.roll(wide, count - 1, 0)).astype(BF16)
    shape = (count // size_z, size_z, lanes)
    for k, part in enumerate((below, rows, above)):
        zc[x, ys[0] : ys[1], :, k * lanes : (k + 1) * lanes] = part.reshape(shape)


def fill_own(zc, plane):
    size_x, size_y = zc.shape[0] - 2, zc.shape[1] - 2
    zc[0] = jnp.zeros(zc.shape[1:], BF16)
    zc[size_x + 1] = jnp.zeros(zc.shape[1:], BF16)
    for x in range(size_x):
        for y in (0, size_y + 1):
            zc[x + 1, y] = jnp.zeros(zc.shape[2:], BF16)
        store_shifts(zc, x + 1, (1, size_y + 1), plane(x))


def fill_sides(zc, f, xa, xb):
    size_x, size_y, size_z = zc.shape[0] - 2, zc.shape[1] - 2, zc.shape[2]
    rows = size_y * size_z
    odd, low_ok, high_ok = side_of("gx")
    channels = xa.shape[3]
    store_shifts(zc, 0, (1, size_y + 1), (pick(odd, xb[f], xa[f]) * low_ok).reshape(rows, channels))
    store_shifts(zc, size_x + 1, (1, size_y + 1), (pick(odd, xa[f], xb[f]) * high_ok).reshape(rows, channels))


def fill_columns(zc, f, ya, yb):
    size_x, size_y = zc.shape[0] - 2, zc.shape[1] - 2
    odd, low_ok, high_ok = side_of("gy")
    for x in range(size_x + 2):
        store_shifts(zc, x, (0, 1), pick(odd, yb[f, x], ya[f, x]) * low_ok)
        store_shifts(zc, x, (size_y + 1, size_y + 2), pick(odd, ya[f, x], yb[f, x]) * high_ok)


def straight(w):
    return lambda tap: w[tap]


def turned(w):
    return lambda tap: w[26 - tap].T


def lay_weights(taps, weight):
    channels = taps.shape[2] // 2
    zero = jnp.zeros((channels, channels), BF16)
    for j in range(3):
        for k in range(3):
            rows = slice(k * channels, (k + 1) * channels)
            for tap in range(3):
                value = weight(9 * tap + 3 * j + k)
                taps[3 * tap + j, rows, :channels] = value
                taps[3 * (tap + 1) + j, rows, channels:] = value
            taps[j, rows, channels:] = zero
            taps[9 + j, rows, :channels] = zero


def convolve(zc, taps, emit):
    size_x, size_y, size_z = zc.shape[0] - 2, zc.shape[1] - 2, zc.shape[2]
    depth = zc.shape[3]
    channels = depth // 3
    rows = size_y * size_z
    for x in range(0, size_x, 4):
        pieces = []
        for i in range(4):
            for j in range(3):
                halves = [zc[x + 2 * h + i, j : j + size_y].reshape(rows, depth) for h in range(2)]
                pieces.append(jnp.concatenate(halves, axis=0))
        both = jnp.dot(
            jnp.concatenate(pieces, axis=1),
            taps[...].reshape(12 * depth, 2 * channels),
            preferred_element_type=F32,
        )
        for h in range(2):
            for side in range(2):
                emit(x + 2 * h + side, both[h * rows : (h + 1) * rows, side * channels : (side + 1) * channels])


def side_weights(taps, which):
    channels = taps.shape[2] // 2
    return jnp.concatenate([taps[n, :, :channels] for n in which], axis=0)


def add_side_terms(total, zc, taps):
    size_x, size_y, size_z = zc.shape[0] - 2, zc.shape[1] - 2, zc.shape[2]
    depth = zc.shape[3]
    rows = size_y * size_z
    for plane, x, first in ((0, 0, 0), (size_x + 1, size_x - 1, 6)):
        side = jnp.concatenate([zc[plane, j : j + size_y].reshape(rows, depth) for j in range(3)], axis=1)
        weights = side_weights(taps, (first, first + 1, first + 2))
        total[x] += jnp.dot(side, weights, preferred_element_type=F32)


def add_column_terms(total, zc, taps):
    size_x, size_y, size_z = zc.shape[0] - 2, zc.shape[1] - 2, zc.shape[2]
    depth = zc.shape[3]
    for column, y, j in ((0, 0, 0), (size_y + 1, size_y - 1, 2)):
        pieces = [zc[i : i + size_x, column].reshape(size_x * size_z, depth) for i in range(3)]
        weights = side_weights(taps, (j, 3 + j, 6 + j))
        term = jnp.dot(jnp.concatenate(pieces, axis=1), weights, preferred_element_type=F32)
        total[:, y * size_z : (y + 1) * size_z, :] += term.reshape(size_x, size_z, -1)


def field_shape(shape):
    size_x, size_y, size_z, channels = shape
    return (size_x + 2, size_y + 2, size_z, 3 * channels)


def taps_shape(channels):
    return (12, 3 * channels, 2 * channels)


def own_shapes(shape):
    size_x, size_y, size_z, channels = shape
    return (
        pltpu.VMEM(field_shape(shape), BF16),
        pltpu.VMEM(taps_shape(channels), BF16),
        pltpu.VMEM((size_x, size_y * size_z, channels), F32),
    )


def masked_plane(field, mask):
    def plane(x):
        value = field[x]
        return value.reshape(-1, value.shape[2]) * mask[x // BLOCK].astype(BF16)

    return plane


def store_in(total):
    def emit(x, value):
        total[x] = value

    return emit


def own_terms(mask, field, w, lay):
    size_x, size_y, size_z, channels = field.shape

    def kernel(mask, field, w, zc, taps, total):
        fill_own(zc, masked_plane(field, mask))
        lay_weights(taps, lay(w))
        convolve(zc, taps, store_in(total))

    return call(
        kernel,
        own_shapes(field.shape),
        (mask, field, w),
        [],
        flops=2 * 27 * field.size * channels,
        nbytes=4 * MIB,
        vmem=14 * MIB,
    )


def own_terms_and_sides(mask, field, w, zm, first_taps, pre, xa, xb):
    channels = field.shape[3]

    def kernel(mask, field, w, first_taps, xa, xb, zm_in, pre_in, zu, taps, total, zm, pre):
        fill_own(zu, masked_plane(field, mask))
        lay_weights(taps, turned(w))
        convolve(zu, taps, store_in(total))
        for f, (zc, weights, out) in enumerate(((zm, first_taps, pre), (zu, taps, total))):
            fill_sides(zc, f, xa, xb)
            add_side_terms(out, zc, weights)

    return call(
        kernel,
        (*own_shapes(field.shape), pltpu.VMEM(zm.shape, BF16), pltpu.VMEM(pre.shape, F32)),
        (mask, field, w, first_taps, xa, xb, zm, pre),
        [],
        flops=2 * 27 * field.size * channels,
        nbytes=4 * MIB,
        vmem=14 * MIB,
        aliases={6: 3, 7: 4},
    )


def copy_sides(f, value, xa, xb, ya, yb):
    size_x, size_y = value.shape[:2]
    first_x = pick(lax.axis_index("gx") % 2, size_x - 1, 0)
    first_y = pick(lax.axis_index("gy") % 2, size_y - 1, 0)
    xa[f], xb[f] = value[first_x], value[size_x - 1 - first_x]
    for x in range(size_x):
        ya[f, x], yb[f, x] = value[x, first_y], value[x, size_y - 1 - first_y]


def side_shapes(shape):
    size_x, size_y, size_z, channels = shape
    side = jax.ShapeDtypeStruct((2, size_y, size_z, channels), BF16)
    column = jax.ShapeDtypeStruct((2, size_x, size_z, channels), BF16)
    return (side, side, column, column)


def grad_terms(left, zc, start, store):
    size_x, size_y, size_z = zc.shape[0] - 2, zc.shape[1] - 2, zc.shape[2]
    depth = zc.shape[3]
    channels = depth // 3
    shifts = [(i, j) for i in range(3) for j in range(3)]
    for group in [shifts[n : n + 2] for n in range(0, 9, 2)]:
        pieces = []
        for i, j in group:
            a, b = start(i, j)
            pieces.append(zc[a : a + size_x, b : b + size_y].reshape(size_x * size_y * size_z, depth))
        out = jnp.dot(left, jnp.concatenate(pieces, axis=1), preferred_element_type=F32)
        for n, (i, j) in enumerate(group):
            for k in range(3):
                store(9 * i + 3 * j, k, out[:, (3 * n + k) * channels : (3 * n + k + 1) * channels])


def scatter_block(keep, send, d, block):
    count = 2 * keep.shape[0]
    share = keep.shape[2]
    index = lax.axis_index("gy")
    half, place = index % 2, index // 2
    for j in range(count // 2):
        even = block[2 * j * share : (2 * j + 1) * share]
        odd = block[(2 * j + 1) * share : (2 * j + 2) * share]
        at = jnp.bitwise_xor(place, j)
        keep[at, d] = pick(half, even, odd)
        send[at, d] = pick(half, odd, even).astype(send.dtype)


def terms_shape(channels, travel):
    count_y = lax.axis_size("gy")
    shape = (count_y // 2, 27, channels // count_y, channels)
    return jax.ShapeDtypeStruct(shape, F32), jax.ShapeDtypeStruct(shape, travel)


def hidden_and_terms(mask, ya, yb, zm, zu, taps, pre, shape):
    size_x, size_y, size_z, channels = shape
    rows = size_y * size_z

    def kernel(mask, ya, yb, taps, pre, zm_in, zu_in, zm, zu, hidden, slope, keep, send):
        for f, zc in enumerate((zm, zu)):
            fill_columns(zc, f, ya, yb)
        slope[...] = pre[...]
        add_column_terms(slope, zm, taps)
        for x in range(size_x):
            here = mask[x // BLOCK]
            value = slope[x]
            s = jax.nn.sigmoid(value)
            hidden[x] = (here * (value * s)).astype(BF16).reshape(size_y, size_z, channels)
            slope[x] = here * (s * (1.0 + value * (1.0 - s)))
        left = hidden[...].reshape(size_x * rows, channels).T

        def store(d, k, block):
            scatter_block(keep, send, d + 2 - k, block)

        grad_terms(left, zu, lambda i, j: (2 - i, 2 - j), store)

    field = jax.ShapeDtypeStruct(shape, BF16)
    wide = jax.ShapeDtypeStruct(pre.shape, F32)
    shifted = jax.ShapeDtypeStruct(zm.shape, BF16)
    return call(
        kernel,
        (shifted, shifted, field, wide, *terms_shape(channels, F32)),
        (mask, ya, yb, taps, pre, zm, zu),
        [],
        flops=2 * 27 * size_x * rows * channels * channels,
        nbytes=8 * MIB,
        vmem=14 * MIB,
        aliases={5: 0, 6: 1},
    )


def pre_grad_and_terms(hidden, slope, zm, zu, taps, grad):
    size_x, rows, channels = grad.shape
    size_y, size_z = zu.shape[1] - 2, zu.shape[2]
    shape = (size_x, size_y, size_z, channels)

    def kernel(hidden, slope, zm, zu, taps, grad, pre_grad, keep, send, xa, xb, ya, yb, total):
        total[...] = grad[...]
        add_column_terms(total, zu, taps)
        for x in range(size_x):
            pre_grad[x] = (total[x] * slope[x]).astype(BF16).reshape(size_y, size_z, channels)
        for f, value in enumerate((hidden, pre_grad)):
            copy_sides(f, value, xa, xb, ya, yb)
        left = pre_grad[...].reshape(size_x * rows, channels).T

        def store(d, k, block):
            scatter_block(keep, send, d + k, block.T)

        grad_terms(left, zm, lambda i, j: (i, j), store)

    return call(
        kernel,
        (jax.ShapeDtypeStruct(shape, BF16), *terms_shape(channels, F32), *side_shapes(shape)),
        (hidden, slope, zm, zu, taps, grad),
        [],
        scratch=[pltpu.VMEM(grad.shape, F32)],
        flops=2 * 27 * size_x * rows * channels * channels,
        nbytes=8 * MIB,
        vmem=14 * MIB,
    )


def add_convolution(mask, own, field, f, halos, w, lay):
    size_x, size_y, size_z, channels = own.shape
    rows = size_y * size_z

    def kernel(mask, own, field, xa, xb, ya, yb, w, out, zc, taps):
        for x in range(size_x):
            store_shifts(zc, x + 1, (1, size_y + 1), field[x].reshape(rows, channels))
        fill_sides(zc, f, xa, xb)
        fill_columns(zc, f, ya, yb)
        lay_weights(taps, lay(w))

        def emit(x, term):
            near = own[x].reshape(rows, channels).astype(F32)
            out[x] = (mask[x // BLOCK] * (near + term)).astype(BF16).reshape(size_y, size_z, channels)

        convolve(zc, taps, emit)

    return call(
        kernel,
        jax.ShapeDtypeStruct(own.shape, BF16),
        (mask, own, field, *halos, w),
        [],
        scratch=[pltpu.VMEM(field_shape(own.shape), BF16), pltpu.VMEM(taps_shape(channels), BF16)],
        flops=2 * 27 * size_x * rows * channels * channels,
        nbytes=3 * MIB,
        vmem=14 * MIB,
    )


def add_halos(mask, own, zc, taps, total, f, halos):
    size_x, size_y, size_z, channels = own.shape
    rows = size_y * size_z

    def kernel(mask, own, taps, total_in, xa, xb, ya, yb, zc_in, zc, out, total):
        total[...] = total_in[...]
        fill_sides(zc, f, xa, xb)
        add_side_terms(total, zc, taps)
        fill_columns(zc, f, ya, yb)
        add_column_terms(total, zc, taps)
        for x in range(size_x):
            near = own[x].reshape(rows, channels).astype(F32)
            value = mask[x // BLOCK] * (near + total[x])
            out[x] = value.astype(BF16).reshape(size_y, size_z, channels)

    return call(
        kernel,
        (pltpu.VMEM(zc.shape, BF16), jax.ShapeDtypeStruct(own.shape, BF16)),
        (mask, own, taps, total, *halos, zc),
        [],
        scratch=[pltpu.VMEM(total.shape, F32)],
        nbytes=3 * MIB,
        vmem=14 * MIB,
        aliases={8: 0},
    )[1]


def after(values, *others):
    return lax.optimization_barrier((values, others))[0]


def swap(value, axis, bit):
    return lax.ppermute(value, axis, [(i, i ^ bit) for i in range(lax.axis_size(axis))])


def is_far(place):
    return place & (place - 1) != 0


def first_sum(g, keep, came, earlier):
    places, taps, share, channels = keep.shape
    rows = taps * share
    far = [p for p in range(places) if is_far(p)]
    near = [p for p in range(1, places) if not is_far(p)]

    def kernel(keep, came, *refs):
        outs = refs[-places:]
        for p in range(places):
            value = (keep[p] + came[p].astype(F32)).reshape(rows, channels)
            if p == 0:
                outs[0][g] = value
            elif p in near:
                outs[1 + near.index(p)][g] = value.astype(BF16)
            else:
                outs[1 + len(near) + far.index(p)][...] = value.astype(BF16)

    stay = pltpu.VMEM((2, rows, channels), F32)
    both = pltpu.VMEM((2, rows, channels), BF16)
    one = pltpu.VMEM((rows, channels), BF16)
    outs = call(
        kernel,
        (stay,) + (both,) * len(near) + (one,) * len(far),
        (keep, came, *earlier),
        [],
        nbytes=2 * MIB,
        vmem=4 * MIB,
        aliases={2 + n: n for n in range(len(earlier))},
    )
    count = 1 + len(near)
    return outs[:count], outs[count:]


CODE_ROWS = 16
CODE_TOP = 32000.0


def encode(value, out):
    most = jnp.max(jnp.max(jnp.abs(value), axis=0, keepdims=True), axis=1, keepdims=True)
    power = jnp.ceil(jnp.log2(jnp.clip(most, 2.0**-100, 2.0**100)))
    power = jnp.broadcast_to(power, (1, value.shape[1]))
    head = jnp.broadcast_to(power, (CODE_ROWS, value.shape[1]))
    out[:CODE_ROWS] = head.astype(jnp.int32).astype(jnp.int16)
    scaled = value * (CODE_TOP * jnp.exp2(-power))
    out[CODE_ROWS:] = jnp.round(scaled).astype(jnp.int32).astype(jnp.int16)


def decode(ref):
    power = ref[:CODE_ROWS].astype(jnp.int32).astype(F32)[:1]
    return ref[CODE_ROWS:].astype(jnp.int32).astype(F32) * (jnp.exp2(power) * (1.0 / CODE_TOP))


def coded_shape(rows, channels):
    return pltpu.VMEM((CODE_ROWS + rows, channels), jnp.int16)


def second_sums(stays, near, far):
    _, rows, channels = stays.shape
    count = len(near)

    def kernel(stays, *refs):
        near, (stay, leave) = refs[:count], refs[-2:]
        far = (refs[count : count + len(far_second)], refs[count + len(far_second) : -2])
        odd = lax.axis_index("gx") % 2
        totals = []
        for g in range(2):
            value = stays[g]
            for ref in near:
                value += ref[g].astype(F32)
            for ref in far[g]:
                value += ref[...].astype(F32)
            totals.append(value)
        stay[...] = pick(odd, totals[0], totals[1])
        encode(pick(odd, totals[1], totals[0]), leave)

    far_second, far_first = far
    outs = (pltpu.VMEM((rows, channels), F32), coded_shape(rows, channels))
    return call(kernel, outs, (stays, *near, *far_second, *far_first), [], nbytes=2 * MIB, vmem=4 * MIB)


def next_sum(own, came):
    rows, channels = came.shape[0] - CODE_ROWS, came.shape[1]
    coded = own.dtype != F32

    def kernel(own, came, out):
        encode((decode(own) if coded else own[...]) + decode(came), out)

    return call(kernel, coded_shape(rows, channels), (own, came), [], nbytes=MIB, vmem=4 * MIB)


def final_grads(own, came, taps, factor):
    rows, channels = came.shape[0] - CODE_ROWS, came.shape[1]
    shape = (taps, rows // taps, channels)

    def kernel(own, came, second, first, mine, other, sem):
        odd = lax.axis_index("gx") % 2
        mine[...] = (decode(own) * factor).reshape(shape)

        def copies(value, is_odd, n):
            return (
                (odd == is_odd, pltpu.make_async_copy(value, second, sem.at[n])),
                (odd != is_odd, pltpu.make_async_copy(value, first, sem.at[n])),
            )

        started = copies(mine, 0, 0)
        for where, copy in started:
            pl.when(where)(copy.start)
        other[...] = (decode(came) * factor).reshape(shape)
        later = copies(other, 1, 1)
        for where, copy in later:
            pl.when(where)(copy.start)
        for where, copy in started + later:
            pl.when(where)(copy.wait)

    out = jax.ShapeDtypeStruct(shape, F32)
    return pl.pallas_call(
        kernel,
        out_shape=(out, out),
        in_specs=[VMEM, VMEM],
        out_specs=(HBM, HBM),
        scratch_shapes=[pltpu.VMEM(shape, F32), pltpu.VMEM(shape, F32), pltpu.SemaphoreType.DMA((2,))],
        compiler_params=pltpu.CompilerParams(vmem_limit_bytes=4 * MIB),
        cost_estimate=pl.CostEstimate(flops=0, bytes_accessed=MIB, transcendentals=0),
    )(own, came)


def body(features, w_first, w_second, occ, cotangent):
    count_x, count_y = lax.axis_size("gx"), lax.axis_size("gy")
    shape = features.shape
    mask, xa, xb, ya, yb, own = pack_sides(features, cotangent, occ)
    xa, xb = swap_neighbours("gx", xa, xb)
    zm, first_taps, pre = own_terms(mask, own, w_first, straight)
    xa, xb = after((xa, xb), pre)
    ya, yb = finish_columns(xa, xb, ya, yb)
    behind = after(mask, ya)
    ya, yb = swap_neighbours("gy", ya, yb)
    zu, second_taps, grad, zm, pre = own_terms_and_sides(behind, cotangent, w_second, zm, first_taps, pre, xa, xb)
    ya, yb = after((ya, yb), grad)
    zm, zu, hidden, slope, keep_second, send = hidden_and_terms(mask, ya, yb, zm, zu, first_taps, pre, shape)
    came = swap(send, "gy", 1)
    pre_grad, keep_first, send, xa, xb, ya, yb = pre_grad_and_terms(hidden, slope, zm, zu, second_taps, grad)

    places = range(1, keep_first.shape[0])
    sums, leaves = first_sum(0, keep_second, after(came, pre_grad), ())
    far_second = [swap(value, "gy", 2 * p) for value, p in zip(leaves, filter(is_far, places))]
    came = swap(send, "gy", 1)
    (stays, *near), leaves = first_sum(1, keep_first, after(came, sums[0]), sums)
    near = [swap(value, "gy", 2 * p) for value, p in zip(near, (p for p in places if not is_far(p)))]
    far_first = [swap(value, "gy", 2 * p) for value, p in zip(leaves, filter(is_far, places))]
    behind = after(mask, far_second, stays)
    zp, *own_pre = own_terms(behind, pre_grad, w_first, turned)
    xa, xb = swap_neighbours("gx", *after((xa, xb), own_pre[1]))
    stays, leaves = second_sums(stays, *after((near, (far_second, far_first)), own_pre[1]))
    xa, xb = after((xa, xb), leaves)
    came = swap(leaves, "gx", 1)
    ya, yb = finish_columns(xa, xb, ya, yb)
    came = after(came, ya)
    ya, yb = swap_neighbours("gy", ya, yb)
    stays = next_sum(stays, came)
    bit = 2
    while bit < count_x:
        came = swap(stays, "gx", bit)
        if bit == 2:
            halos = after((xa, xb, ya, yb), stays)
            output = add_convolution(mask, features, hidden, 0, halos, w_second, straight)
            came = after(came, output)
        stays = next_sum(stays, came)
        bit *= 2
    came = swap(stays, "gx", 1)
    grad_features = add_halos(mask, cotangent, zp, *own_pre, 1, after(halos, stays))
    came = after(came, grad_features)
    factor = 1.0 / math.sqrt(count_x * count_y * shape[0] * shape[1] * shape[2])
    grad_second, grad_first = final_grads(stays, came, w_first.shape[0], factor)
    return output, grad_features, grad_first, grad_second


def solution(mesh):
    in_specs = (P("gx", "gy", None, None), P(), P(), P("gx", "gy", None), P("gx", "gy", None, None))
    out_specs = (
        P("gx", "gy", None, None),
        P("gx", "gy", None, None),
        P(None, "gy", None),
        P(None, "gy", None),
    )
    return jax.shard_map(body, mesh=mesh, in_specs=in_specs, out_specs=out_specs, check_vma=False)
```

```python
import math

import jax
import jax.numpy as jnp
from jax import lax
from jax.experimental import pallas as pl
from jax.experimental.pallas import tpu as pltpu
from jax.sharding import PartitionSpec as P

BF16 = jnp.bfloat16
F32 = jnp.float32
VMEM = pl.BlockSpec(memory_space=pltpu.VMEM)
HBM = pl.BlockSpec(memory_space=pltpu.HBM)
MIB = 1024 * 1024
BLOCK = 8


def call(kernel, out_shapes, args, spaces, scratch=(), flops=0, nbytes=0, vmem=16 * MIB, aliases=None):
    return pl.pallas_call(
        kernel,
        out_shape=out_shapes,
        in_specs=list(spaces) + [VMEM] * (len(args) - len(spaces)),
        out_specs=jax.tree.map(lambda _: VMEM, out_shapes),
        scratch_shapes=list(scratch),
        input_output_aliases=aliases or {},
        compiler_params=pltpu.CompilerParams(vmem_limit_bytes=vmem),
        cost_estimate=pl.CostEstimate(flops=flops, bytes_accessed=nbytes, transcendentals=0),
    )(*args)


def swap_pairs(axis, odd):
    count_x, count_y = lax.axis_size("gx"), lax.axis_size("gy")
    pairs = []
    for x in range(count_x):
        for y in range(count_y):
            at, count = (x, count_x) if axis == "gx" else (y, count_y)
            to = at - 1 if (at % 2 == 0) == odd else at + 1
            if not 0 <= to < count:
                other = (x, y ^ 1) if axis == "gx" else (x ^ 1, y)
            else:
                other = (to, y) if axis == "gx" else (x, to)
            pairs.append((x * count_y + y, other[0] * count_y + other[1]))
    return pairs


def plane_mask(occ, block_x, size_y, size_z):
    row = lax.broadcasted_iota(jnp.int32, (size_y * size_z, 128), 0)
    block_y = row // (BLOCK * size_z)
    block_z = (row % size_z) // BLOCK
    mask = jnp.zeros((size_y * size_z, 128), F32)
    for i in range(size_y // BLOCK):
        for j in range(size_z // BLOCK):
            here = (block_y == i) & (block_z == j)
            mask = jnp.where(here, occ[block_x, i, j].astype(F32), mask)
    return mask


def pick(odd, if_even, if_odd):
    return jnp.where(odd == 0, if_even, if_odd)


def one_if(condition):
    return jnp.where(condition, 1.0, 0.0).astype(BF16)


def side_of(axis):
    index = lax.axis_index(axis)
    return index % 2, one_if(index > 0), one_if(index < lax.axis_size(axis) - 1)


def pack_sides(features, cotangent, occ):
    size_x, size_y, size_z, channels = features.shape
    rows = size_y * size_z

    def kernel(occ_hbm, first, second, mask, xa, xb, ya, yb, own, occ_ref, sem, occ_sem, own_sem):
        odd_x, odd_y = lax.axis_index("gx") % 2, lax.axis_index("gy") % 2
        first_x = pick(odd_x, size_x - 1, 0)
        first_y = pick(odd_y, size_y - 1, 0)
        sides = ((xa, first_x), (xb, size_x - 1 - first_x))
        columns = ((ya, first_y), (yb, size_y - 1 - first_y))
        occ_copy = pltpu.make_async_copy(occ_hbm, occ_ref, occ_sem)
        own_copy = pltpu.make_async_copy(first, own, own_sem)
        copies = []
        for n, (out, x) in enumerate(sides):
            copies.append(pltpu.make_async_copy(second.at[x], out.at[1], sem.at[n]))
        for n, (out, y) in enumerate(columns):
            copies.append(pltpu.make_async_copy(second.at[:, y], out.at[1], sem.at[2 + n]))
        for copy in [occ_copy, own_copy, *copies]:
            copy.start()
        occ_copy.wait()
        for n in range(size_x // BLOCK):
            mask[n] = plane_mask(occ_ref, n, size_y, size_z)
        own_copy.wait()
        for out, x in sides:
            out[0] = own[x] * mask[x // BLOCK].astype(BF16).reshape(size_y, size_z, channels)
        for out, y in columns:
            at = pl.ds(pl.multiple_of(y * size_z, size_z), size_z)
            for x in range(size_x):
                out[0, x] = own[x, y] * mask[x // BLOCK, at, :].astype(BF16)
        for copy in copies:
            copy.wait()
        for out, x in sides:
            out[1] = out[1] * mask[x // BLOCK].astype(BF16).reshape(size_y, size_z, channels)
        for out, y in columns:
            at = pl.ds(pl.multiple_of(y * size_z, size_z), size_z)
            for x in range(size_x):
                out[1, x] = out[1, x] * mask[x // BLOCK, at, :].astype(BF16)

    side = pltpu.VMEM((2, size_y, size_z, channels), BF16)
    column = pltpu.VMEM((2, size_x, size_z, channels), BF16)
    return call(
        kernel,
        (
            pltpu.VMEM((size_x // BLOCK, rows, channels), F32),
            side,
            side,
            column,
            column,
            pltpu.VMEM(features.shape, BF16),
        ),
        [pltpu.with_memory_space_constraint(value, pltpu.HBM) for value in (occ, features, cotangent)],
        [HBM] * 3,
        scratch=[
            pltpu.SMEM(occ.shape, jnp.int32),
            pltpu.SemaphoreType.DMA((4,)),
            pltpu.SemaphoreType.DMA(()),
            pltpu.SemaphoreType.DMA(()),
        ],
        flops=8 << 30,
        nbytes=MIB,
        vmem=4 * MIB,
    )


def finish_columns(got_xa, got_xb, ya, yb):
    _, size_y, size_z, channels = got_xa.shape
    size_x = ya.shape[1]

    def kernel(xa, xb, ya, yb, out_a, out_b):
        odd, low_ok, high_ok = side_of("gx")
        first_y = pick(lax.axis_index("gy") % 2, size_y - 1, 0)
        for out, own, y in ((out_a, ya, first_y), (out_b, yb, size_y - 1 - first_y)):
            for f in range(2):
                out[f, 0] = pick(odd, xb[f, y], xa[f, y]) * low_ok
                out[f, size_x + 1] = pick(odd, xa[f, y], xb[f, y]) * high_ok
                out[f, 1 : size_x + 1] = own[f]

    shape = jax.ShapeDtypeStruct((2, size_x + 2, size_z, channels), BF16)
    return call(kernel, (shape, shape), (got_xa, got_xb, ya, yb), [], nbytes=MIB, vmem=4 * MIB)


def swap_neighbours(axis, first, second):
    second = lax.ppermute(second, ("gx", "gy"), swap_pairs(axis, True))
    first = lax.ppermute(first, ("gx", "gy"), swap_pairs(axis, False))
    return first, second


def store_shifts(zc, x, ys, rows):
    size_z = zc.shape[2]
    count, lanes = rows.shape
    wide = rows.astype(F32)
    z = lax.broadcasted_iota(jnp.int32, (count, lanes), 0) % size_z
    below = jnp.where(z == 0, 0.0, pltpu.roll(wide, 1, 0)).astype(BF16)
    above = jnp.where(z == size_z - 1, 0.0, pltpu.roll(wide, count - 1, 0)).astype(BF16)
    shape = (count // size_z, size_z, lanes)
    for k, part in enumerate((below, rows, above)):
        zc[x, ys[0] : ys[1], :, k * lanes : (k + 1) * lanes] = part.reshape(shape)


def fill_own(zc, plane):
    size_x, size_y = zc.shape[0] - 2, zc.shape[1] - 2
    zc[0] = jnp.zeros(zc.shape[1:], BF16)
    zc[size_x + 1] = jnp.zeros(zc.shape[1:], BF16)
    for x in range(size_x):
        for y in (0, size_y + 1):
            zc[x + 1, y] = jnp.zeros(zc.shape[2:], BF16)
        store_shifts(zc, x + 1, (1, size_y + 1), plane(x))


def fill_sides(zc, f, xa, xb):
    size_x, size_y, size_z = zc.shape[0] - 2, zc.shape[1] - 2, zc.shape[2]
    rows = size_y * size_z
    odd, low_ok, high_ok = side_of("gx")
    channels = xa.shape[3]
    store_shifts(zc, 0, (1, size_y + 1), (pick(odd, xb[f], xa[f]) * low_ok).reshape(rows, channels))
    store_shifts(zc, size_x + 1, (1, size_y + 1), (pick(odd, xa[f], xb[f]) * high_ok).reshape(rows, channels))


def fill_columns(zc, f, ya, yb):
    size_x, size_y = zc.shape[0] - 2, zc.shape[1] - 2
    odd, low_ok, high_ok = side_of("gy")
    for x in range(size_x + 2):
        store_shifts(zc, x, (0, 1), pick(odd, yb[f, x], ya[f, x]) * low_ok)
        store_shifts(zc, x, (size_y + 1, size_y + 2), pick(odd, ya[f, x], yb[f, x]) * high_ok)


def straight(w):
    return lambda tap: w[tap]


def turned(w):
    return lambda tap: w[26 - tap].T


def lay_weights(taps, weight):
    channels = taps.shape[2] // 2
    zero = jnp.zeros((channels, channels), BF16)
    for j in range(3):
        for k in range(3):
            rows = slice(k * channels, (k + 1) * channels)
            for tap in range(3):
                value = weight(9 * tap + 3 * j + k)
                taps[3 * tap + j, rows, :channels] = value
                taps[3 * (tap + 1) + j, rows, channels:] = value
            taps[j, rows, channels:] = zero
            taps[9 + j, rows, :channels] = zero


def convolve(zc, taps, emit):
    size_x, size_y, size_z = zc.shape[0] - 2, zc.shape[1] - 2, zc.shape[2]
    depth = zc.shape[3]
    channels = depth // 3
    rows = size_y * size_z
    for x in range(0, size_x, 4):
        pieces = []
        for i in range(4):
            for j in range(3):
                halves = [zc[x + 2 * h + i, j : j + size_y].reshape(rows, depth) for h in range(2)]
                pieces.append(jnp.concatenate(halves, axis=0))
        both = jnp.dot(
            jnp.concatenate(pieces, axis=1),
            taps[...].reshape(12 * depth, 2 * channels),
            preferred_element_type=F32,
        )
        for h in range(2):
            for side in range(2):
                emit(x + 2 * h + side, both[h * rows : (h + 1) * rows, side * channels : (side + 1) * channels])


def side_weights(taps, which):
    channels = taps.shape[2] // 2
    return jnp.concatenate([taps[n, :, :channels] for n in which], axis=0)


def add_side_terms(total, zc, taps):
    size_x, size_y, size_z = zc.shape[0] - 2, zc.shape[1] - 2, zc.shape[2]
    depth = zc.shape[3]
    rows = size_y * size_z
    for plane, x, first in ((0, 0, 0), (size_x + 1, size_x - 1, 6)):
        side = jnp.concatenate([zc[plane, j : j + size_y].reshape(rows, depth) for j in range(3)], axis=1)
        weights = side_weights(taps, (first, first + 1, first + 2))
        total[x] += jnp.dot(side, weights, preferred_element_type=F32)


def add_column_terms(total, zc, taps):
    size_x, size_y, size_z = zc.shape[0] - 2, zc.shape[1] - 2, zc.shape[2]
    depth = zc.shape[3]
    for column, y, j in ((0, 0, 0), (size_y + 1, size_y - 1, 2)):
        pieces = [zc[i : i + size_x, column].reshape(size_x * size_z, depth) for i in range(3)]
        weights = side_weights(taps, (j, 3 + j, 6 + j))
        term = jnp.dot(jnp.concatenate(pieces, axis=1), weights, preferred_element_type=F32)
        total[:, y * size_z : (y + 1) * size_z, :] += term.reshape(size_x, size_z, -1)


def field_shape(shape):
    size_x, size_y, size_z, channels = shape
    return (size_x + 2, size_y + 2, size_z, 3 * channels)


def taps_shape(channels):
    return (12, 3 * channels, 2 * channels)


def own_shapes(shape):
    size_x, size_y, size_z, channels = shape
    return (
        pltpu.VMEM(field_shape(shape), BF16),
        pltpu.VMEM(taps_shape(channels), BF16),
        pltpu.VMEM((size_x, size_y * size_z, channels), F32),
    )


def masked_plane(field, mask):
    def plane(x):
        value = field[x]
        return value.reshape(-1, value.shape[2]) * mask[x // BLOCK].astype(BF16)

    return plane


def store_in(total):
    def emit(x, value):
        total[x] = value

    return emit


def own_terms(mask, field, w, lay):
    size_x, size_y, size_z, channels = field.shape

    def kernel(mask, field, w, zc, taps, total):
        fill_own(zc, masked_plane(field, mask))
        lay_weights(taps, lay(w))
        convolve(zc, taps, store_in(total))

    return call(
        kernel,
        own_shapes(field.shape),
        (mask, field, w),
        [],
        flops=2 * 27 * field.size * channels,
        nbytes=4 * MIB,
        vmem=14 * MIB,
    )


def own_terms_and_sides(mask, field, w, zm, first_taps, pre, xa, xb):
    channels = field.shape[3]

    def kernel(mask, field, w, first_taps, xa, xb, zm_in, pre_in, zu, taps, total, zm, pre):
        fill_own(zu, masked_plane(field, mask))
        lay_weights(taps, turned(w))
        convolve(zu, taps, store_in(total))
        for f, (zc, weights, out) in enumerate(((zm, first_taps, pre), (zu, taps, total))):
            fill_sides(zc, f, xa, xb)
            add_side_terms(out, zc, weights)

    return call(
        kernel,
        (*own_shapes(field.shape), pltpu.VMEM(zm.shape, BF16), pltpu.VMEM(pre.shape, F32)),
        (mask, field, w, first_taps, xa, xb, zm, pre),
        [],
        flops=2 * 27 * field.size * channels,
        nbytes=4 * MIB,
        vmem=14 * MIB,
        aliases={6: 3, 7: 4},
    )


def copy_sides(f, value, xa, xb, ya, yb):
    size_x, size_y = value.shape[:2]
    first_x = pick(lax.axis_index("gx") % 2, size_x - 1, 0)
    first_y = pick(lax.axis_index("gy") % 2, size_y - 1, 0)
    xa[f], xb[f] = value[first_x], value[size_x - 1 - first_x]
    for x in range(size_x):
        ya[f, x], yb[f, x] = value[x, first_y], value[x, size_y - 1 - first_y]


def side_shapes(shape):
    size_x, size_y, size_z, channels = shape
    side = jax.ShapeDtypeStruct((2, size_y, size_z, channels), BF16)
    column = jax.ShapeDtypeStruct((2, size_x, size_z, channels), BF16)
    return (side, side, column, column)


def grad_terms(left, zc, start, store):
    size_x, size_y, size_z = zc.shape[0] - 2, zc.shape[1] - 2, zc.shape[2]
    depth = zc.shape[3]
    channels = depth // 3
    shifts = [(i, j) for i in range(3) for j in range(3)]
    for group in [shifts[n : n + 2] for n in range(0, 9, 2)]:
        pieces = []
        for i, j in group:
            a, b = start(i, j)
            pieces.append(zc[a : a + size_x, b : b + size_y].reshape(size_x * size_y * size_z, depth))
        out = jnp.dot(left, jnp.concatenate(pieces, axis=1), preferred_element_type=F32)
        for n, (i, j) in enumerate(group):
            for k in range(3):
                store(9 * i + 3 * j, k, out[:, (3 * n + k) * channels : (3 * n + k + 1) * channels])


def scatter_block(keep, send, d, block):
    count = 2 * keep.shape[0]
    share = keep.shape[2]
    index = lax.axis_index("gy")
    half, place = index % 2, index // 2
    for j in range(count // 2):
        even = block[2 * j * share : (2 * j + 1) * share]
        odd = block[(2 * j + 1) * share : (2 * j + 2) * share]
        at = jnp.bitwise_xor(place, j)
        keep[at, d] = pick(half, even, odd)
        send[at, d] = pick(half, odd, even).astype(send.dtype)


def terms_shape(channels, travel):
    count_y = lax.axis_size("gy")
    shape = (count_y // 2, 27, channels // count_y, channels)
    return jax.ShapeDtypeStruct(shape, F32), jax.ShapeDtypeStruct(shape, travel)


def hidden_and_terms(mask, ya, yb, zm, zu, taps, pre, shape):
    size_x, size_y, size_z, channels = shape
    rows = size_y * size_z

    def kernel(mask, ya, yb, taps, pre, zm_in, zu_in, zm, zu, hidden, slope, keep, send):
        for f, zc in enumerate((zm, zu)):
            fill_columns(zc, f, ya, yb)
        slope[...] = pre[...]
        add_column_terms(slope, zm, taps)
        for x in range(size_x):
            here = mask[x // BLOCK]
            value = slope[x]
            s = jax.nn.sigmoid(value)
            hidden[x] = (here * (value * s)).astype(BF16).reshape(size_y, size_z, channels)
            slope[x] = here * (s * (1.0 + value * (1.0 - s)))
        left = hidden[...].reshape(size_x * rows, channels).T

        def store(d, k, block):
            scatter_block(keep, send, d + 2 - k, block)

        grad_terms(left, zu, lambda i, j: (2 - i, 2 - j), store)

    field = jax.ShapeDtypeStruct(shape, BF16)
    wide = jax.ShapeDtypeStruct(pre.shape, F32)
    shifted = jax.ShapeDtypeStruct(zm.shape, BF16)
    return call(
        kernel,
        (shifted, shifted, field, wide, *terms_shape(channels, F32)),
        (mask, ya, yb, taps, pre, zm, zu),
        [],
        flops=2 * 27 * size_x * rows * channels * channels,
        nbytes=8 * MIB,
        vmem=14 * MIB,
        aliases={5: 0, 6: 1},
    )


def pre_grad_and_terms(hidden, slope, zm, zu, taps, grad):
    size_x, rows, channels = grad.shape
    size_y, size_z = zu.shape[1] - 2, zu.shape[2]
    shape = (size_x, size_y, size_z, channels)

    def kernel(hidden, slope, zm, zu, taps, grad, pre_grad, keep, send, xa, xb, ya, yb, total):
        total[...] = grad[...]
        add_column_terms(total, zu, taps)
        for x in range(size_x):
            pre_grad[x] = (total[x] * slope[x]).astype(BF16).reshape(size_y, size_z, channels)
        for f, value in enumerate((hidden, pre_grad)):
            copy_sides(f, value, xa, xb, ya, yb)
        left = pre_grad[...].reshape(size_x * rows, channels).T

        def store(d, k, block):
            scatter_block(keep, send, d + k, block.T)

        grad_terms(left, zm, lambda i, j: (i, j), store)

    return call(
        kernel,
        (jax.ShapeDtypeStruct(shape, BF16), *terms_shape(channels, F32), *side_shapes(shape)),
        (hidden, slope, zm, zu, taps, grad),
        [],
        scratch=[pltpu.VMEM(grad.shape, F32)],
        flops=2 * 27 * size_x * rows * channels * channels,
        nbytes=8 * MIB,
        vmem=14 * MIB,
    )


def add_convolution(mask, own, field, f, halos, w, lay):
    size_x, size_y, size_z, channels = own.shape
    rows = size_y * size_z

    def kernel(mask, own, field, xa, xb, ya, yb, w, out, zc, taps):
        for x in range(size_x):
            store_shifts(zc, x + 1, (1, size_y + 1), field[x].reshape(rows, channels))
        fill_sides(zc, f, xa, xb)
        fill_columns(zc, f, ya, yb)
        lay_weights(taps, lay(w))

        def emit(x, term):
            near = own[x].reshape(rows, channels).astype(F32)
            out[x] = (mask[x // BLOCK] * (near + term)).astype(BF16).reshape(size_y, size_z, channels)

        convolve(zc, taps, emit)

    return call(
        kernel,
        jax.ShapeDtypeStruct(own.shape, BF16),
        (mask, own, field, *halos, w),
        [],
        scratch=[pltpu.VMEM(field_shape(own.shape), BF16), pltpu.VMEM(taps_shape(channels), BF16)],
        flops=2 * 27 * size_x * rows * channels * channels,
        nbytes=3 * MIB,
        vmem=14 * MIB,
    )


def add_halos(mask, own, zc, taps, total, f, halos):
    size_x, size_y, size_z, channels = own.shape
    rows = size_y * size_z

    def kernel(mask, own, taps, total_in, xa, xb, ya, yb, zc_in, zc, out, total):
        total[...] = total_in[...]
        fill_sides(zc, f, xa, xb)
        add_side_terms(total, zc, taps)
        fill_columns(zc, f, ya, yb)
        add_column_terms(total, zc, taps)
        for x in range(size_x):
            near = own[x].reshape(rows, channels).astype(F32)
            value = mask[x // BLOCK] * (near + total[x])
            out[x] = value.astype(BF16).reshape(size_y, size_z, channels)

    return call(
        kernel,
        (pltpu.VMEM(zc.shape, BF16), jax.ShapeDtypeStruct(own.shape, BF16)),
        (mask, own, taps, total, *halos, zc),
        [],
        scratch=[pltpu.VMEM(total.shape, F32)],
        nbytes=3 * MIB,
        vmem=14 * MIB,
        aliases={8: 0},
    )[1]


def after(values, *others):
    return lax.optimization_barrier((values, others))[0]


def swap(value, axis, bit):
    return lax.ppermute(value, axis, [(i, i ^ bit) for i in range(lax.axis_size(axis))])


def is_far(place):
    return place & (place - 1) != 0


def first_sum(g, keep, came, earlier):
    places, taps, share, channels = keep.shape
    rows = taps * share
    far = [p for p in range(places) if is_far(p)]
    near = [p for p in range(1, places) if not is_far(p)]

    def kernel(keep, came, *refs):
        outs = refs[-places:]
        for p in range(places):
            value = (keep[p] + came[p].astype(F32)).reshape(rows, channels)
            if p == 0:
                outs[0][g] = value
            elif p in near:
                outs[1 + near.index(p)][g] = value.astype(BF16)
            else:
                outs[1 + len(near) + far.index(p)][...] = value.astype(BF16)

    stay = pltpu.VMEM((2, rows, channels), F32)
    both = pltpu.VMEM((2, rows, channels), BF16)
    one = pltpu.VMEM((rows, channels), BF16)
    outs = call(
        kernel,
        (stay,) + (both,) * len(near) + (one,) * len(far),
        (keep, came, *earlier),
        [],
        nbytes=2 * MIB,
        vmem=4 * MIB,
        aliases={2 + n: n for n in range(len(earlier))},
    )
    count = 1 + len(near)
    return outs[:count], outs[count:]


CODE_ROWS = 16
CODE_TOP = 32000.0


def encode(value, out):
    most = jnp.max(jnp.max(jnp.abs(value), axis=0, keepdims=True), axis=1, keepdims=True)
    power = jnp.ceil(jnp.log2(jnp.clip(most, 2.0**-100, 2.0**100)))
    power = jnp.broadcast_to(power, (1, value.shape[1]))
    head = jnp.broadcast_to(power, (CODE_ROWS, value.shape[1]))
    out[:CODE_ROWS] = head.astype(jnp.int32).astype(jnp.int16)
    scaled = value * (CODE_TOP * jnp.exp2(-power))
    out[CODE_ROWS:] = jnp.round(scaled).astype(jnp.int32).astype(jnp.int16)


def decode(ref):
    power = ref[:CODE_ROWS].astype(jnp.int32).astype(F32)[:1]
    return ref[CODE_ROWS:].astype(jnp.int32).astype(F32) * (jnp.exp2(power) * (1.0 / CODE_TOP))


def coded_shape(rows, channels):
    return pltpu.VMEM((CODE_ROWS + rows, channels), jnp.int16)


def second_sums(stays, near, far):
    _, rows, channels = stays.shape
    count = len(near)

    def kernel(stays, *refs):
        near, (stay, leave) = refs[:count], refs[-2:]
        far = (refs[count : count + len(far_second)], refs[count + len(far_second) : -2])
        odd = lax.axis_index("gx") % 2
        totals = []
        for g in range(2):
            value = stays[g]
            for ref in near:
                value += ref[g].astype(F32)
            for ref in far[g]:
                value += ref[...].astype(F32)
            totals.append(value)
        stay[...] = pick(odd, totals[0], totals[1])
        encode(pick(odd, totals[1], totals[0]), leave)

    far_second, far_first = far
    outs = (pltpu.VMEM((rows, channels), F32), coded_shape(rows, channels))
    return call(kernel, outs, (stays, *near, *far_second, *far_first), [], nbytes=2 * MIB, vmem=4 * MIB)


def next_sum(own, came):
    rows, channels = came.shape[0] - CODE_ROWS, came.shape[1]
    coded = own.dtype != F32

    def kernel(own, came, out):
        encode((decode(own) if coded else own[...]) + decode(came), out)

    return call(kernel, coded_shape(rows, channels), (own, came), [], nbytes=MIB, vmem=4 * MIB)


def final_grads(own, came, taps, factor):
    rows, channels = came.shape[0] - CODE_ROWS, came.shape[1]
    shape = (taps, rows // taps, channels)

    def kernel(own, came, second, first, mine, other, sem):
        odd = lax.axis_index("gx") % 2
        mine[...] = (decode(own) * factor).reshape(shape)

        def copies(value, is_odd, n):
            return (
                (odd == is_odd, pltpu.make_async_copy(value, second, sem.at[n])),
                (odd != is_odd, pltpu.make_async_copy(value, first, sem.at[n])),
            )

        started = copies(mine, 0, 0)
        for where, copy in started:
            pl.when(where)(copy.start)
        other[...] = (decode(came) * factor).reshape(shape)
        later = copies(other, 1, 1)
        for where, copy in later:
            pl.when(where)(copy.start)
        for where, copy in started + later:
            pl.when(where)(copy.wait)

    out = jax.ShapeDtypeStruct(shape, F32)
    return pl.pallas_call(
        kernel,
        out_shape=(out, out),
        in_specs=[VMEM, VMEM],
        out_specs=(HBM, HBM),
        scratch_shapes=[pltpu.VMEM(shape, F32), pltpu.VMEM(shape, F32), pltpu.SemaphoreType.DMA((2,))],
        compiler_params=pltpu.CompilerParams(vmem_limit_bytes=4 * MIB),
        cost_estimate=pl.CostEstimate(flops=0, bytes_accessed=MIB, transcendentals=0),
    )(own, came)


def body(features, w_first, w_second, occ, cotangent):
    count_x, count_y = lax.axis_size("gx"), lax.axis_size("gy")
    shape = features.shape
    mask, xa, xb, ya, yb, own = pack_sides(features, cotangent, occ)
    xa, xb = swap_neighbours("gx", xa, xb)
    zm, first_taps, pre = own_terms(mask, own, w_first, straight)
    xa, xb = after((xa, xb), pre)
    ya, yb = finish_columns(xa, xb, ya, yb)
    behind = after(mask, ya)
    ya, yb = swap_neighbours("gy", ya, yb)
    zu, second_taps, grad, zm, pre = own_terms_and_sides(behind, cotangent, w_second, zm, first_taps, pre, xa, xb)
    ya, yb = after((ya, yb), grad)
    zm, zu, hidden, slope, keep_second, send = hidden_and_terms(mask, ya, yb, zm, zu, first_taps, pre, shape)
    came = swap(send, "gy", 1)
    pre_grad, keep_first, send, xa, xb, ya, yb = pre_grad_and_terms(hidden, slope, zm, zu, second_taps, grad)

    places = range(1, keep_first.shape[0])
    sums, leaves = first_sum(0, keep_second, after(came, pre_grad), ())
    far_second = [swap(value, "gy", 2 * p) for value, p in zip(leaves, filter(is_far, places))]
    came = swap(send, "gy", 1)
    (stays, *near), leaves = first_sum(1, keep_first, after(came, sums[0]), sums)
    near = [swap(value, "gy", 2 * p) for value, p in zip(near, (p for p in places if not is_far(p)))]
    far_first = [swap(value, "gy", 2 * p) for value, p in zip(leaves, filter(is_far, places))]
    xa, xb = swap_neighbours("gx", *after((xa, xb), far_second, stays))
    behind = after(mask, far_second, stays)
    zp, *own_pre = own_terms(behind, pre_grad, w_first, turned)
    xa, xb = after((xa, xb), own_pre[1])
    stays, leaves = second_sums(stays, *after((near, (far_second, far_first)), own_pre[1]))
    xa, xb = after((xa, xb), leaves)
    came = swap(leaves, "gx", 1)
    ya, yb = finish_columns(xa, xb, ya, yb)
    came = after(came, ya)
    ya, yb = swap_neighbours("gy", ya, yb)
    stays = next_sum(stays, came)
    bit = 2
    while bit < count_x:
        came = swap(stays, "gx", bit)
        if bit == 2:
            halos = after((xa, xb, ya, yb), stays)
            output = add_convolution(mask, features, hidden, 0, halos, w_second, straight)
            came = after(came, output)
        stays = next_sum(stays, came)
        bit *= 2
    came = swap(stays, "gx", 1)
    grad_features = add_halos(mask, cotangent, zp, *own_pre, 1, after(halos, stays))
    came = after(came, grad_features)
    factor = 1.0 / math.sqrt(count_x * count_y * shape[0] * shape[1] * shape[2])
    grad_second, grad_first = final_grads(stays, came, w_first.shape[0], factor)
    return output, grad_features, grad_first, grad_second


def solution(mesh):
    in_specs = (P("gx", "gy", None, None), P(), P(), P("gx", "gy", None), P("gx", "gy", None, None))
    out_specs = (
        P("gx", "gy", None, None),
        P("gx", "gy", None, None),
        P(None, "gy", None),
        P(None, "gy", None),
    )
    return jax.shard_map(body, mesh=mesh, in_specs=in_specs, out_specs=out_specs, check_vma=False)
```

```python
import math

import jax
import jax.numpy as jnp
from jax import lax
from jax.experimental import pallas as pl
from jax.experimental.pallas import tpu as pltpu
from jax.sharding import PartitionSpec as P

BF16 = jnp.bfloat16
F32 = jnp.float32
VMEM = pl.BlockSpec(memory_space=pltpu.VMEM)
HBM = pl.BlockSpec(memory_space=pltpu.HBM)
MIB = 1024 * 1024
BLOCK = 8


def call(kernel, out_shapes, args, spaces, scratch=(), flops=0, nbytes=0, vmem=16 * MIB, aliases=None):
    return pl.pallas_call(
        kernel,
        out_shape=out_shapes,
        in_specs=list(spaces) + [VMEM] * (len(args) - len(spaces)),
        out_specs=jax.tree.map(lambda _: VMEM, out_shapes),
        scratch_shapes=list(scratch),
        input_output_aliases=aliases or {},
        compiler_params=pltpu.CompilerParams(vmem_limit_bytes=vmem),
        cost_estimate=pl.CostEstimate(flops=flops, bytes_accessed=nbytes, transcendentals=0),
    )(*args)


def swap_pairs(axis, odd):
    count_x, count_y = lax.axis_size("gx"), lax.axis_size("gy")
    pairs = []
    for x in range(count_x):
        for y in range(count_y):
            at, count = (x, count_x) if axis == "gx" else (y, count_y)
            to = at - 1 if (at % 2 == 0) == odd else at + 1
            if not 0 <= to < count:
                other = (x, y ^ 1) if axis == "gx" else (x ^ 1, y)
            else:
                other = (to, y) if axis == "gx" else (x, to)
            pairs.append((x * count_y + y, other[0] * count_y + other[1]))
    return pairs


def plane_mask(occ, block_x, size_y, size_z):
    row = lax.broadcasted_iota(jnp.int32, (size_y * size_z, 128), 0)
    block_y = row // (BLOCK * size_z)
    block_z = (row % size_z) // BLOCK
    mask = jnp.zeros((size_y * size_z, 128), F32)
    for i in range(size_y // BLOCK):
        for j in range(size_z // BLOCK):
            here = (block_y == i) & (block_z == j)
            mask = jnp.where(here, occ[block_x, i, j].astype(F32), mask)
    return mask


def pick(odd, if_even, if_odd):
    return jnp.where(odd == 0, if_even, if_odd)


def one_if(condition):
    return jnp.where(condition, 1.0, 0.0).astype(BF16)


def side_of(axis):
    index = lax.axis_index(axis)
    return index % 2, one_if(index > 0), one_if(index < lax.axis_size(axis) - 1)


def pack_sides(features, cotangent, occ):
    size_x, size_y, size_z, channels = features.shape
    rows = size_y * size_z

    def kernel(occ_hbm, first, second, mask, xa, xb, ya, yb, own, occ_ref, sem, occ_sem, own_sem):
        odd_x, odd_y = lax.axis_index("gx") % 2, lax.axis_index("gy") % 2
        first_x = pick(odd_x, size_x - 1, 0)
        first_y = pick(odd_y, size_y - 1, 0)
        sides = ((xa, first_x), (xb, size_x - 1 - first_x))
        columns = ((ya, first_y), (yb, size_y - 1 - first_y))
        occ_copy = pltpu.make_async_copy(occ_hbm, occ_ref, occ_sem)
        own_copy = pltpu.make_async_copy(first, own, own_sem)
        copies = []
        for n, (out, x) in enumerate(sides):
            copies.append(pltpu.make_async_copy(second.at[x], out.at[1], sem.at[n]))
        for n, (out, y) in enumerate(columns):
            copies.append(pltpu.make_async_copy(second.at[:, y], out.at[1], sem.at[2 + n]))
        for copy in [occ_copy, own_copy, *copies]:
            copy.start()
        occ_copy.wait()
        for n in range(size_x // BLOCK):
            mask[n] = plane_mask(occ_ref, n, size_y, size_z)
        own_copy.wait()
        for out, x in sides:
            out[0] = own[x] * mask[x // BLOCK].astype(BF16).reshape(size_y, size_z, channels)
        for out, y in columns:
            at = pl.ds(pl.multiple_of(y * size_z, size_z), size_z)
            for x in range(size_x):
                out[0, x] = own[x, y] * mask[x // BLOCK, at, :].astype(BF16)
        for copy in copies:
            copy.wait()
        for out, x in sides:
            out[1] = out[1] * mask[x // BLOCK].astype(BF16).reshape(size_y, size_z, channels)
        for out, y in columns:
            at = pl.ds(pl.multiple_of(y * size_z, size_z), size_z)
            for x in range(size_x):
                out[1, x] = out[1, x] * mask[x // BLOCK, at, :].astype(BF16)

    side = pltpu.VMEM((2, size_y, size_z, channels), BF16)
    column = pltpu.VMEM((2, size_x, size_z, channels), BF16)
    return call(
        kernel,
        (
            pltpu.VMEM((size_x // BLOCK, rows, channels), F32),
            side,
            side,
            column,
            column,
            pltpu.VMEM(features.shape, BF16),
        ),
        [pltpu.with_memory_space_constraint(value, pltpu.HBM) for value in (occ, features, cotangent)],
        [HBM] * 3,
        scratch=[
            pltpu.SMEM(occ.shape, jnp.int32),
            pltpu.SemaphoreType.DMA((4,)),
            pltpu.SemaphoreType.DMA(()),
            pltpu.SemaphoreType.DMA(()),
        ],
        flops=8 << 30,
        nbytes=MIB,
        vmem=4 * MIB,
    )


def finish_columns(got_xa, got_xb, ya, yb):
    _, size_y, size_z, channels = got_xa.shape
    size_x = ya.shape[1]

    def kernel(xa, xb, ya, yb, out_a, out_b):
        odd, low_ok, high_ok = side_of("gx")
        first_y = pick(lax.axis_index("gy") % 2, size_y - 1, 0)
        for out, own, y in ((out_a, ya, first_y), (out_b, yb, size_y - 1 - first_y)):
            for f in range(2):
                out[f, 0] = pick(odd, xb[f, y], xa[f, y]) * low_ok
                out[f, size_x + 1] = pick(odd, xa[f, y], xb[f, y]) * high_ok
                out[f, 1 : size_x + 1] = own[f]

    shape = jax.ShapeDtypeStruct((2, size_x + 2, size_z, channels), BF16)
    return call(kernel, (shape, shape), (got_xa, got_xb, ya, yb), [], nbytes=MIB, vmem=4 * MIB)


def swap_neighbours(axis, first, second):
    second = lax.ppermute(second, ("gx", "gy"), swap_pairs(axis, True))
    first = lax.ppermute(first, ("gx", "gy"), swap_pairs(axis, False))
    return first, second


def store_shifts(zc, x, ys, rows):
    size_z = zc.shape[2]
    count, lanes = rows.shape
    wide = rows.astype(F32)
    z = lax.broadcasted_iota(jnp.int32, (count, lanes), 0) % size_z
    below = jnp.where(z == 0, 0.0, pltpu.roll(wide, 1, 0)).astype(BF16)
    above = jnp.where(z == size_z - 1, 0.0, pltpu.roll(wide, count - 1, 0)).astype(BF16)
    shape = (count // size_z, size_z, lanes)
    for k, part in enumerate((below, rows, above)):
        zc[x, ys[0] : ys[1], :, k * lanes : (k + 1) * lanes] = part.reshape(shape)


def fill_own(zc, plane):
    size_x, size_y = zc.shape[0] - 2, zc.shape[1] - 2
    zc[0] = jnp.zeros(zc.shape[1:], BF16)
    zc[size_x + 1] = jnp.zeros(zc.shape[1:], BF16)
    for x in range(size_x):
        for y in (0, size_y + 1):
            zc[x + 1, y] = jnp.zeros(zc.shape[2:], BF16)
        store_shifts(zc, x + 1, (1, size_y + 1), plane(x))


def fill_sides(zc, f, xa, xb):
    size_x, size_y, size_z = zc.shape[0] - 2, zc.shape[1] - 2, zc.shape[2]
    rows = size_y * size_z
    odd, low_ok, high_ok = side_of("gx")
    channels = xa.shape[3]
    store_shifts(zc, 0, (1, size_y + 1), (pick(odd, xb[f], xa[f]) * low_ok).reshape(rows, channels))
    store_shifts(zc, size_x + 1, (1, size_y + 1), (pick(odd, xa[f], xb[f]) * high_ok).reshape(rows, channels))


def fill_columns(zc, f, ya, yb):
    size_x, size_y = zc.shape[0] - 2, zc.shape[1] - 2
    odd, low_ok, high_ok = side_of("gy")
    for x in range(size_x + 2):
        store_shifts(zc, x, (0, 1), pick(odd, yb[f, x], ya[f, x]) * low_ok)
        store_shifts(zc, x, (size_y + 1, size_y + 2), pick(odd, ya[f, x], yb[f, x]) * high_ok)


def straight(w):
    return lambda tap: w[tap]


def turned(w):
    return lambda tap: w[26 - tap].T


def lay_weights(taps, weight):
    channels = taps.shape[2] // 2
    zero = jnp.zeros((channels, channels), BF16)
    for j in range(3):
        for k in range(3):
            rows = slice(k * channels, (k + 1) * channels)
            for tap in range(3):
                value = weight(9 * tap + 3 * j + k)
                taps[3 * tap + j, rows, :channels] = value
                taps[3 * (tap + 1) + j, rows, channels:] = value
            taps[j, rows, channels:] = zero
            taps[9 + j, rows, :channels] = zero


def convolve(zc, taps, emit):
    size_x, size_y, size_z = zc.shape[0] - 2, zc.shape[1] - 2, zc.shape[2]
    depth = zc.shape[3]
    channels = depth // 3
    rows = size_y * size_z
    for x in range(0, size_x, 4):
        pieces = []
        for i in range(4):
            for j in range(3):
                halves = [zc[x + 2 * h + i, j : j + size_y].reshape(rows, depth) for h in range(2)]
                pieces.append(jnp.concatenate(halves, axis=0))
        both = jnp.dot(
            jnp.concatenate(pieces, axis=1),
            taps[...].reshape(12 * depth, 2 * channels),
            preferred_element_type=F32,
        )
        for h in range(2):
            for side in range(2):
                emit(x + 2 * h + side, both[h * rows : (h + 1) * rows, side * channels : (side + 1) * channels])


def side_weights(taps, which):
    channels = taps.shape[2] // 2
    return jnp.concatenate([taps[n, :, :channels] for n in which], axis=0)


def add_side_terms(total, zc, taps):
    size_x, size_y, size_z = zc.shape[0] - 2, zc.shape[1] - 2, zc.shape[2]
    depth = zc.shape[3]
    rows = size_y * size_z
    for plane, x, first in ((0, 0, 0), (size_x + 1, size_x - 1, 6)):
        side = jnp.concatenate([zc[plane, j : j + size_y].reshape(rows, depth) for j in range(3)], axis=1)
        weights = side_weights(taps, (first, first + 1, first + 2))
        total[x] += jnp.dot(side, weights, preferred_element_type=F32)


def add_column_terms(total, zc, taps):
    size_x, size_y, size_z = zc.shape[0] - 2, zc.shape[1] - 2, zc.shape[2]
    depth = zc.shape[3]
    for column, y, j in ((0, 0, 0), (size_y + 1, size_y - 1, 2)):
        pieces = [zc[i : i + size_x, column].reshape(size_x * size_z, depth) for i in range(3)]
        weights = side_weights(taps, (j, 3 + j, 6 + j))
        term = jnp.dot(jnp.concatenate(pieces, axis=1), weights, preferred_element_type=F32)
        total[:, y * size_z : (y + 1) * size_z, :] += term.reshape(size_x, size_z, -1)


def field_shape(shape):
    size_x, size_y, size_z, channels = shape
    return (size_x + 2, size_y + 2, size_z, 3 * channels)


def taps_shape(channels):
    return (12, 3 * channels, 2 * channels)


def own_shapes(shape):
    size_x, size_y, size_z, channels = shape
    return (
        pltpu.VMEM(field_shape(shape), BF16),
        pltpu.VMEM(taps_shape(channels), BF16),
        pltpu.VMEM((size_x, size_y * size_z, channels), F32),
    )


def masked_plane(field, mask):
    def plane(x):
        value = field[x]
        return value.reshape(-1, value.shape[2]) * mask[x // BLOCK].astype(BF16)

    return plane


def store_in(total):
    def emit(x, value):
        total[x] = value

    return emit


def own_terms(mask, field, w, lay):
    size_x, size_y, size_z, channels = field.shape

    def kernel(mask, field, w, zc, taps, total):
        fill_own(zc, masked_plane(field, mask))
        lay_weights(taps, lay(w))
        convolve(zc, taps, store_in(total))

    return call(
        kernel,
        own_shapes(field.shape),
        (mask, field, w),
        [],
        flops=2 * 27 * field.size * channels,
        nbytes=4 * MIB,
        vmem=14 * MIB,
    )


def own_terms_and_sides(mask, field, w, zm, first_taps, pre, xa, xb):
    channels = field.shape[3]

    def kernel(mask, field, w, first_taps, xa, xb, zm_in, pre_in, zu, taps, total, zm, pre):
        fill_own(zu, masked_plane(field, mask))
        lay_weights(taps, turned(w))
        convolve(zu, taps, store_in(total))
        for f, (zc, weights, out) in enumerate(((zm, first_taps, pre), (zu, taps, total))):
            fill_sides(zc, f, xa, xb)
            add_side_terms(out, zc, weights)

    return call(
        kernel,
        (*own_shapes(field.shape), pltpu.VMEM(zm.shape, BF16), pltpu.VMEM(pre.shape, F32)),
        (mask, field, w, first_taps, xa, xb, zm, pre),
        [],
        flops=2 * 27 * field.size * channels,
        nbytes=4 * MIB,
        vmem=14 * MIB,
        aliases={6: 3, 7: 4},
    )


def copy_sides(f, value, xa, xb, ya, yb):
    size_x, size_y = value.shape[:2]
    first_x = pick(lax.axis_index("gx") % 2, size_x - 1, 0)
    first_y = pick(lax.axis_index("gy") % 2, size_y - 1, 0)
    xa[f], xb[f] = value[first_x], value[size_x - 1 - first_x]
    for x in range(size_x):
        ya[f, x], yb[f, x] = value[x, first_y], value[x, size_y - 1 - first_y]


def side_shapes(shape):
    size_x, size_y, size_z, channels = shape
    side = jax.ShapeDtypeStruct((2, size_y, size_z, channels), BF16)
    column = jax.ShapeDtypeStruct((2, size_x, size_z, channels), BF16)
    return (side, side, column, column)


def grad_terms(left, zc, start, store):
    size_x, size_y, size_z = zc.shape[0] - 2, zc.shape[1] - 2, zc.shape[2]
    depth = zc.shape[3]
    channels = depth // 3
    shifts = [(i, j) for i in range(3) for j in range(3)]
    for group in [shifts[n : n + 2] for n in range(0, 9, 2)]:
        pieces = []
        for i, j in group:
            a, b = start(i, j)
            pieces.append(zc[a : a + size_x, b : b + size_y].reshape(size_x * size_y * size_z, depth))
        out = jnp.dot(left, jnp.concatenate(pieces, axis=1), preferred_element_type=F32)
        for n, (i, j) in enumerate(group):
            for k in range(3):
                store(9 * i + 3 * j, k, out[:, (3 * n + k) * channels : (3 * n + k + 1) * channels])


def scatter_block(keep, send, d, block):
    count = 2 * keep.shape[0]
    share = keep.shape[2]
    index = lax.axis_index("gy")
    half, place = index % 2, index // 2
    for j in range(count // 2):
        even = block[2 * j * share : (2 * j + 1) * share]
        odd = block[(2 * j + 1) * share : (2 * j + 2) * share]
        at = jnp.bitwise_xor(place, j)
        keep[at, d] = pick(half, even, odd)
        send[at, d] = pick(half, odd, even).astype(send.dtype)


def terms_shape(channels, travel):
    count_y = lax.axis_size("gy")
    shape = (count_y // 2, 27, channels // count_y, channels)
    return jax.ShapeDtypeStruct(shape, F32), jax.ShapeDtypeStruct(shape, travel)


def hidden_and_terms(mask, ya, yb, zm, zu, taps, pre, shape):
    size_x, size_y, size_z, channels = shape
    rows = size_y * size_z

    def kernel(mask, ya, yb, taps, pre, zm_in, zu_in, zm, zu, hidden, slope, keep, send):
        for f, zc in enumerate((zm, zu)):
            fill_columns(zc, f, ya, yb)
        slope[...] = pre[...]
        add_column_terms(slope, zm, taps)
        for x in range(size_x):
            here = mask[x // BLOCK]
            value = slope[x]
            s = jax.nn.sigmoid(value)
            hidden[x] = (here * (value * s)).astype(BF16).reshape(size_y, size_z, channels)
            slope[x] = here * (s * (1.0 + value * (1.0 - s)))
        left = hidden[...].reshape(size_x * rows, channels).T

        def store(d, k, block):
            scatter_block(keep, send, d + 2 - k, block)

        grad_terms(left, zu, lambda i, j: (2 - i, 2 - j), store)

    field = jax.ShapeDtypeStruct(shape, BF16)
    wide = jax.ShapeDtypeStruct(pre.shape, F32)
    shifted = jax.ShapeDtypeStruct(zm.shape, BF16)
    return call(
        kernel,
        (shifted, shifted, field, wide, *terms_shape(channels, F32)),
        (mask, ya, yb, taps, pre, zm, zu),
        [],
        flops=2 * 27 * size_x * rows * channels * channels,
        nbytes=8 * MIB,
        vmem=14 * MIB,
        aliases={5: 0, 6: 1},
    )


def pre_grad_and_terms(hidden, slope, zm, zu, taps, grad):
    size_x, rows, channels = grad.shape
    size_y, size_z = zu.shape[1] - 2, zu.shape[2]
    shape = (size_x, size_y, size_z, channels)

    def kernel(hidden, slope, zm, zu, taps, grad, pre_grad, keep, send, xa, xb, ya, yb, total):
        total[...] = grad[...]
        add_column_terms(total, zu, taps)
        for x in range(size_x):
            pre_grad[x] = (total[x] * slope[x]).astype(BF16).reshape(size_y, size_z, channels)
        for f, value in enumerate((hidden, pre_grad)):
            copy_sides(f, value, xa, xb, ya, yb)
        left = pre_grad[...].reshape(size_x * rows, channels).T

        def store(d, k, block):
            scatter_block(keep, send, d + k, block.T)

        grad_terms(left, zm, lambda i, j: (i, j), store)

    return call(
        kernel,
        (jax.ShapeDtypeStruct(shape, BF16), *terms_shape(channels, F32), *side_shapes(shape)),
        (hidden, slope, zm, zu, taps, grad),
        [],
        scratch=[pltpu.VMEM(grad.shape, F32)],
        flops=2 * 27 * size_x * rows * channels * channels,
        nbytes=8 * MIB,
        vmem=14 * MIB,
    )


def add_convolution(mask, own, field, f, halos, w, lay):
    size_x, size_y, size_z, channels = own.shape
    rows = size_y * size_z

    def kernel(mask, own, field, xa, xb, ya, yb, w, out, zc, taps):
        for x in range(size_x):
            store_shifts(zc, x + 1, (1, size_y + 1), field[x].reshape(rows, channels))
        fill_sides(zc, f, xa, xb)
        fill_columns(zc, f, ya, yb)
        lay_weights(taps, lay(w))

        def emit(x, term):
            near = own[x].reshape(rows, channels).astype(F32)
            out[x] = (mask[x // BLOCK] * (near + term)).astype(BF16).reshape(size_y, size_z, channels)

        convolve(zc, taps, emit)

    return call(
        kernel,
        jax.ShapeDtypeStruct(own.shape, BF16),
        (mask, own, field, *halos, w),
        [],
        scratch=[pltpu.VMEM(field_shape(own.shape), BF16), pltpu.VMEM(taps_shape(channels), BF16)],
        flops=2 * 27 * size_x * rows * channels * channels,
        nbytes=3 * MIB,
        vmem=14 * MIB,
    )


def add_halos(mask, own, zc, taps, total, f, halos):
    size_x, size_y, size_z, channels = own.shape
    rows = size_y * size_z

    def kernel(mask, own, taps, total_in, xa, xb, ya, yb, zc_in, zc, out, total):
        total[...] = total_in[...]
        fill_sides(zc, f, xa, xb)
        add_side_terms(total, zc, taps)
        fill_columns(zc, f, ya, yb)
        add_column_terms(total, zc, taps)
        for x in range(size_x):
            near = own[x].reshape(rows, channels).astype(F32)
            value = mask[x // BLOCK] * (near + total[x])
            out[x] = value.astype(BF16).reshape(size_y, size_z, channels)

    return call(
        kernel,
        (pltpu.VMEM(zc.shape, BF16), jax.ShapeDtypeStruct(own.shape, BF16)),
        (mask, own, taps, total, *halos, zc),
        [],
        scratch=[pltpu.VMEM(total.shape, F32)],
        nbytes=3 * MIB,
        vmem=14 * MIB,
        aliases={8: 0},
    )[1]


def after(values, *others):
    return lax.optimization_barrier((values, others))[0]


def swap(value, axis, bit):
    return lax.ppermute(value, axis, [(i, i ^ bit) for i in range(lax.axis_size(axis))])


def is_far(place):
    return place & (place - 1) != 0


def first_sum(g, keep, came, earlier):
    places, taps, share, channels = keep.shape
    rows = taps * share
    far = [p for p in range(places) if is_far(p)]
    near = [p for p in range(1, places) if not is_far(p)]

    def kernel(keep, came, *refs):
        outs = refs[-places:]
        for p in range(places):
            value = (keep[p] + came[p].astype(F32)).reshape(rows, channels)
            if p == 0:
                outs[0][g] = value
            elif p in near:
                outs[1 + near.index(p)][g] = value.astype(BF16)
            else:
                outs[1 + len(near) + far.index(p)][...] = value.astype(BF16)

    stay = pltpu.VMEM((2, rows, channels), F32)
    both = pltpu.VMEM((2, rows, channels), BF16)
    one = pltpu.VMEM((rows, channels), BF16)
    outs = call(
        kernel,
        (stay,) + (both,) * len(near) + (one,) * len(far),
        (keep, came, *earlier),
        [],
        nbytes=2 * MIB,
        vmem=4 * MIB,
        aliases={2 + n: n for n in range(len(earlier))},
    )
    count = 1 + len(near)
    return outs[:count], outs[count:]


CODE_ROWS = 16
CODE_TOP = 32000.0


def encode(value, out):
    most = jnp.max(jnp.max(jnp.abs(value), axis=0, keepdims=True), axis=1, keepdims=True)
    power = jnp.ceil(jnp.log2(jnp.clip(most, 2.0**-100, 2.0**100)))
    power = jnp.broadcast_to(power, (1, value.shape[1]))
    head = jnp.broadcast_to(power, (CODE_ROWS, value.shape[1]))
    out[:CODE_ROWS] = head.astype(jnp.int32).astype(jnp.int16)
    scaled = value * (CODE_TOP * jnp.exp2(-power))
    out[CODE_ROWS:] = jnp.round(scaled).astype(jnp.int32).astype(jnp.int16)


def decode(ref):
    power = ref[:CODE_ROWS].astype(jnp.int32).astype(F32)[:1]
    return ref[CODE_ROWS:].astype(jnp.int32).astype(F32) * (jnp.exp2(power) * (1.0 / CODE_TOP))


def coded_shape(rows, channels):
    return pltpu.VMEM((CODE_ROWS + rows, channels), jnp.int16)


def second_sums(stays, near, far):
    _, rows, channels = stays.shape
    count = len(near)

    def kernel(stays, *refs):
        near, (stay, leave) = refs[:count], refs[-2:]
        far = (refs[count : count + len(far_second)], refs[count + len(far_second) : -2])
        odd = lax.axis_index("gx") % 2
        totals = []
        for g in range(2):
            value = stays[g]
            for ref in near:
                value += ref[g].astype(F32)
            for ref in far[g]:
                value += ref[...].astype(F32)
            totals.append(value)
        stay[...] = pick(odd, totals[0], totals[1])
        encode(pick(odd, totals[1], totals[0]), leave)

    far_second, far_first = far
    outs = (pltpu.VMEM((rows, channels), F32), coded_shape(rows, channels))
    return call(kernel, outs, (stays, *near, *far_second, *far_first), [], nbytes=2 * MIB, vmem=4 * MIB)


def next_sum(own, came):
    rows, channels = came.shape[0] - CODE_ROWS, came.shape[1]
    coded = own.dtype != F32

    def kernel(own, came, out):
        encode((decode(own) if coded else own[...]) + decode(came), out)

    return call(kernel, coded_shape(rows, channels), (own, came), [], nbytes=MIB, vmem=4 * MIB)


def final_grads(own, came, taps, factor):
    rows, channels = came.shape[0] - CODE_ROWS, came.shape[1]
    shape = (taps, rows // taps, channels)

    def kernel(own, came, second, first, mine, other, sem):
        odd = lax.axis_index("gx") % 2
        mine[...] = (decode(own) * factor).reshape(shape)

        def copies(value, is_odd, n):
            return (
                (odd == is_odd, pltpu.make_async_copy(value, second, sem.at[n])),
                (odd != is_odd, pltpu.make_async_copy(value, first, sem.at[n])),
            )

        started = copies(mine, 0, 0)
        for where, copy in started:
            pl.when(where)(copy.start)
        other[...] = (decode(came) * factor).reshape(shape)
        later = copies(other, 1, 1)
        for where, copy in later:
            pl.when(where)(copy.start)
        for where, copy in started + later:
            pl.when(where)(copy.wait)

    out = jax.ShapeDtypeStruct(shape, F32)
    return pl.pallas_call(
        kernel,
        out_shape=(out, out),
        in_specs=[VMEM, VMEM],
        out_specs=(HBM, HBM),
        scratch_shapes=[pltpu.VMEM(shape, F32), pltpu.VMEM(shape, F32), pltpu.SemaphoreType.DMA((2,))],
        compiler_params=pltpu.CompilerParams(vmem_limit_bytes=4 * MIB),
        cost_estimate=pl.CostEstimate(flops=0, bytes_accessed=MIB, transcendentals=0),
    )(own, came)


def body(features, w_first, w_second, occ, cotangent):
    count_x, count_y = lax.axis_size("gx"), lax.axis_size("gy")
    shape = features.shape
    mask, xa, xb, ya, yb, own = pack_sides(features, cotangent, occ)
    xa, xb = swap_neighbours("gx", xa, xb)
    zm, first_taps, pre = own_terms(mask, own, w_first, straight)
    xa, xb = after((xa, xb), pre)
    ya, yb = finish_columns(xa, xb, ya, yb)
    behind = after(mask, ya)
    ya, yb = swap_neighbours("gy", ya, yb)
    zu, second_taps, grad, zm, pre = own_terms_and_sides(behind, cotangent, w_second, zm, first_taps, pre, xa, xb)
    ya, yb = after((ya, yb), grad)
    zm, zu, hidden, slope, keep_second, send = hidden_and_terms(mask, ya, yb, zm, zu, first_taps, pre, shape)
    came = swap(send, "gy", 1)
    pre_grad, keep_first, send, xa, xb, ya, yb = pre_grad_and_terms(hidden, slope, zm, zu, second_taps, grad)

    places = range(1, keep_first.shape[0])
    sums, leaves = first_sum(0, keep_second, after(came, pre_grad), ())
    far_second = [swap(value, "gy", 2 * p) for value, p in zip(leaves, filter(is_far, places))]
    came = swap(send, "gy", 1)
    (stays, *near), leaves = first_sum(1, keep_first, after(came, sums[0]), sums)
    near = [swap(value, "gy", 2 * p) for value, p in zip(near, (p for p in places if not is_far(p)))]
    far_first = [swap(value, "gy", 2 * p) for value, p in zip(leaves, filter(is_far, places))]
    xa, xb = swap_neighbours("gx", *after((xa, xb), far_second))
    behind = after(mask, far_second, stays)
    zp, *own_pre = own_terms(behind, pre_grad, w_first, turned)
    xa, xb = after((xa, xb), own_pre[1])
    stays, leaves = second_sums(stays, *after((near, (far_second, far_first)), own_pre[1]))
    xa, xb = after((xa, xb), leaves)
    came = swap(leaves, "gx", 1)
    ya, yb = finish_columns(xa, xb, ya, yb)
    came = after(came, ya)
    ya, yb = swap_neighbours("gy", ya, yb)
    stays = next_sum(stays, came)
    bit = 2
    while bit < count_x:
        came = swap(stays, "gx", bit)
        if bit == 2:
            halos = after((xa, xb, ya, yb), stays)
            output = add_convolution(mask, features, hidden, 0, halos, w_second, straight)
            came = after(came, output)
        stays = next_sum(stays, came)
        bit *= 2
    came = swap(stays, "gx", 1)
    grad_features = add_halos(mask, cotangent, zp, *own_pre, 1, after(halos, stays))
    came = after(came, grad_features)
    factor = 1.0 / math.sqrt(count_x * count_y * shape[0] * shape[1] * shape[2])
    grad_second, grad_first = final_grads(stays, came, w_first.shape[0], factor)
    return output, grad_features, grad_first, grad_second


def solution(mesh):
    in_specs = (P("gx", "gy", None, None), P(), P(), P("gx", "gy", None), P("gx", "gy", None, None))
    out_specs = (
        P("gx", "gy", None, None),
        P("gx", "gy", None, None),
        P(None, "gy", None),
        P(None, "gy", None),
    )
    return jax.shard_map(body, mesh=mesh, in_specs=in_specs, out_specs=out_specs, check_vma=False)
```
